32 devices in a mesh: ax: 8 (over z, y), az: 4 (over x, core).
Axes of the slice: x: 2, y: 2, z: 4, core: 2. Of those that a mesh axis runs over, the one named last changes fastest.
Arguments:
- lamb_vector: bfloat16 [8192, 3, 512], P(('ax', 'az')), may hold values from -6 to 6
- owner: int32 [8192, 1], P(('ax', 'az')), may hold values from 0 to 31; in each aligned block of 256 rows (0 to 255, 256 to 511, ...) at most 24 rows name the same one
- element: int32 [8192], P(('ax', 'az')), may hold values from 0 to 1023
- shape_class: int32 [8192], P(('ax', 'az')), may hold values from 0 to 1
- interp_tables: bfloat16 [2, 512, 125], replicated, may hold values from -0.25 to 0.25
- acoustic_state: float32 [5, 125, 16, 16, 128], P(None, None, 'ax', 'az'), may hold values from -6 to 6
Outputs:
- new_state: float32 [5, 125, 16, 16, 128], P(None, None, 'ax', 'az')
- source: float32 [3, 125, 16, 16, 128], P(None, None, 'ax', 'az')
The draws below stay inside these ranges and needn't reach their ends.
Inputs may be any that keep to these rules, and one draw needn't show every extreme that they name: `owner`: among one device's 256 flow elements no device is named by more than 24 of them, and some device is named by exactly 24.
All inputs are finite; a program needn't handle non-finite values.
Results may differ from the reference program's by a relative error of at most 0.0013.
Values may be sent and summed in bfloat16 or wider, within the bound.
No kernel may reach another device: no remote copies, remote signals or barrier semaphores. Data moves between devices by JAX's collectives and lax.ppermute only.
A program may use at most 128 MiB of HBM per device.

```python
import math
import jax
import jax.numpy as jnp
import numpy as np
from jax import lax

NF = 512
NA = 125
FIELDS = 5
NTAB = 2
FE_DEV = 256
EX = 2
EY = 4
ER = 128
CAP = 24
AE_DEV = 1024
FLOW = 8192
NXE = 16
NYE = 16
N_AX = 8
N_AZ = 4
DEVICES = 32


def touch_ends(entries, key, smallest, largest):
    longest = entries.shape.index(max(entries.shape))
    spots = []
    for shift in (0, 1):
        where = [jax.random.randint(jax.random.fold_in(key, axis), (), 0, length) for axis, length in enumerate(entries.shape)]
        where[longest] = (where[longest] + shift) % entries.shape[longest]
        spots.append(tuple(where))
    return entries.at[spots[0]].set(smallest).at[spots[1]].set(largest)


def shard_levels(stream_key, extent, split, low, largest):
    gain, own = 1.0, jax.random.fold_in(stream_key, 6)
    for axis_at, shards_of in split:
        steps = jnp.exp(jax.random.uniform(jax.random.fold_in(own, axis_at), (shards_of,), jnp.float32, low / len(split), largest / len(split)))
        gain = gain * jnp.repeat(steps, extent[axis_at] // shards_of).reshape([-1 if axis == axis_at else 1 for axis in range(len(extent))])
    return gain


def routed_block(rng, own, number, rows, count, top, bound, skew):
    order = jax.random.permutation(rng, count)
    packed, common = shares(count, rows * top, bound, skew, True), shares(count, rows * top, bound, skew, False)
    places = jnp.arange(count)

    def named(sizes, rotation):
        used = int((sizes > 0).sum())
        fixed = max(1, used // 4)
        shifted = fixed + (places - fixed + rotation * (used - fixed)) % max(1, count - fixed)
        return jnp.zeros((count,), jnp.int32).at[order[jnp.where(places < fixed, places, shifted)]].set(jnp.asarray(sizes, jnp.int32))

    sizes = jnp.where(number % 4 == 0, named(packed, number // 4), named(common, number - number // 4 - 1))
    mixed = jax.random.permutation(jax.random.fold_in(own, 3), count)
    donor, taker = mixed[0:count // 2 * 2:2], mixed[1:count // 2 * 2:2]
    slack = jnp.minimum(sizes[donor] - 1, bound - sizes[taker]) // 2
    slack = jnp.where((donor == order[0]) | (taker == order[0]) | (sizes[taker] == 0), 0, jnp.maximum(slack, 0))
    shifted = jax.random.randint(jax.random.fold_in(own, 4), (count // 2,), 0, 1 << 20) % (slack + 1)
    sizes = sizes.at[donor].add(-shifted).at[taker].add(shifted)
    labels = jnp.searchsorted(jnp.cumsum(sizes), jnp.arange(rows * top), side="right").astype(jnp.int32)
    grid = labels.reshape(top, rows).T
    grid = grid[jax.random.permutation(jax.random.fold_in(own, 1), rows)]
    rotation = jax.random.randint(jax.random.fold_in(own, 2), (rows, 1), 0, top)
    return jnp.take_along_axis(grid, (jnp.arange(top)[None, :] + rotation) % top, axis=1)


def shares(number_of, total, reach, skew, full):
    portions = [(1 << 20) // math.isqrt(rank ** skew) + 1 for rank in range(1, number_of + 1)]
    largest = reach if full else min(reach, max(-(-total // number_of), total * portions[0] // sum(portions)))
    least = 1 if total - largest >= number_of - 1 else 0
    holding, spare = [largest] + [least] * (number_of - 1), total - largest - least * (number_of - 1)
    while spare > 0:
        free = [i for i in range(1, number_of) if holding[i] < largest] or [i for i in range(1, number_of) if holding[i] < reach]
        mass, budget = sum([portions[i] for i in free]), spare
        for i in free:
            more = min(reach - holding[i], max(1, budget * portions[i] // mass), spare)
            holding[i] = holding[i] + more
            spare = spare - more
    return np.array(holding)


def bell_draw(own_key, extent, deviation, limit, cuts=(), kind=jnp.bfloat16):
    values = jax.random.normal(own_key, extent, jnp.float32) * deviation
    if len(cuts) > 0:
        values = shard_levels(own_key, extent, cuts, -0.22, 0.18) * values
    return jnp.clip(values, min=-limit, max=limit).astype(kind)


def setup_inputs(seed: int = 0) -> dict:
    splits = jax.random.split(jax.random.key(seed), 7)
    lamb_vector = bell_draw(splits[0], (FLOW, 3, NF), 1.0, 6.0, ((0, 32),))
    owner_keys = jax.random.split(jax.random.fold_in(splits[1], 1), FLOW // FE_DEV)
    owner_turns = jax.random.permutation(jax.random.fold_in(splits[1], 3), FLOW // FE_DEV)
    owner = jax.vmap(lambda own, number: routed_block(jax.random.fold_in(splits[1], 2), own, number, FE_DEV, DEVICES, 1, CAP, 2))(owner_keys, owner_turns).reshape((FLOW, 1))
    element = touch_ends(jax.random.randint(splits[2], (FLOW,), 0, AE_DEV), jax.random.fold_in(splits[2], 1), 0, AE_DEV - 1).astype(jnp.int32)
    shape_class = touch_ends(jax.random.randint(splits[3], (FLOW,), 0, NTAB), jax.random.fold_in(splits[3], 1), 0, NTAB - 1).astype(jnp.int32)
    interp_tables = bell_draw(splits[4], (NTAB, NF, NA), NF ** -0.5, 0.25)
    acoustic_state = bell_draw(splits[5], (FIELDS, NA, NXE, NYE, ER), 1.0, 6.0, ((2, 8), (3, 4)), jnp.float32)
    return {"lamb_vector": lamb_vector, "owner": owner, "element": element, "shape_class": shape_class, "interp_tables": interp_tables, "acoustic_state": acoustic_state}


MACH_NUMBER = 0.3
RUSANOV_SPEED = 1.3
TIME_STEP = 0.03
LIFT_FACTOR = 10.0
VOLUME_FACTOR = 2.0

def gll_tables():
    points = np.array([-1.0, -math.sqrt(3.0 / 7.0), 0.0, math.sqrt(3.0 / 7.0), 1.0])
    barycentric = np.array([1.0 / np.prod([points[col_index] - points[other_index] for other_index in range(5) if other_index != col_index]) for col_index in range(5)])
    derivative = np.zeros((5, 5))
    for row_index in range(5):
        for col_index in range(5):
            if row_index != col_index:
                derivative[row_index, col_index] = barycentric[col_index] / barycentric[row_index] / (points[row_index] - points[col_index])
        derivative[row_index, row_index] = -np.sum(derivative[row_index])
    identity = np.eye(5)
    return [np.kron(np.kron(derivative, identity), identity), np.kron(np.kron(identity, derivative), identity), np.kron(np.kron(identity, identity), derivative)]

def flux(field, direction):
    pressure = field[0]
    axial = field[1]
    azimuthal = field[2]
    radial = field[3]
    density = field[4]
    nothing = jnp.zeros_like(pressure)
    gradient = MACH_NUMBER * axial + pressure
    if direction == 0:
        return jnp.stack([MACH_NUMBER * pressure + axial, gradient, nothing, nothing, MACH_NUMBER * density + axial])
    if direction == 1:
        return jnp.stack([azimuthal, nothing, gradient, nothing, azimuthal])
    return jnp.stack([radial, nothing, nothing, gradient, radial])

def face_term(inner, outer, direction, normal):
    jump = inner - outer
    return LIFT_FACTOR * (normal * flux(jump, direction) - RUSANOV_SPEED * jump)

def node_faces(state):
    trailing = state.shape[2:]
    count = state.shape[0]
    shaped = state.reshape((count, 5, 5, 5) + trailing)
    result = []
    for picked in [shaped[:, 0], shaped[:, 4], shaped[:, :, 0], shaped[:, :, 4], shaped[:, :, :, 0], shaped[:, :, :, 4]]:
        result.append(picked.reshape((count, 25) + trailing))
    return result

def add_faces(total, terms):
    trailing = total.shape[2:]
    count = total.shape[0]
    shaped = total.reshape((count, 5, 5, 5) + trailing)
    pieces = [term.reshape((count, 5, 5) + trailing) for term in terms]
    shaped = shaped.at[:, 0].add(pieces[0])
    shaped = shaped.at[:, 4].add(pieces[1])
    shaped = shaped.at[:, :, 0].add(pieces[2])
    shaped = shaped.at[:, :, 4].add(pieces[3])
    shaped = shaped.at[:, :, :, 0].add(pieces[4])
    shaped = shaped.at[:, :, :, 4].add(pieces[5])
    return shaped.reshape(total.shape)

def volume(state):
    tables = gll_tables()
    total = jnp.zeros_like(state)
    for direction in range(3):
        matrix = jnp.asarray(tables[direction], jnp.float32)
        gradient = jnp.einsum('ij,fjxyz->fixyz', matrix, state, precision=lax.Precision.HIGHEST)
        total = total - VOLUME_FACTOR * flux(gradient, direction)
    return total

def radial_outer(minus_face, plus_face):
    widths_low = ((0, 0), (0, 0), (0, 0), (0, 0), (1, 0))
    widths_high = ((0, 0), (0, 0), (0, 0), (0, 0), (0, 1))
    return (jnp.pad(plus_face, widths_low)[..., :-1], jnp.pad(minus_face, widths_high)[..., 1:])

def operate(state, source):
    faces = node_faces(state)
    outer_xm = jnp.pad(faces[1], ((0, 0), (0, 0), (1, 0), (0, 0), (0, 0)))[:, :, :-1]
    outer_xp = jnp.pad(faces[0], ((0, 0), (0, 0), (0, 1), (0, 0), (0, 0)))[:, :, 1:]
    outer_ym = jnp.roll(faces[3], 1, axis=3)
    outer_yp = jnp.roll(faces[2], -1, axis=3)
    outer_zm, outer_zp = radial_outer(faces[4], faces[5])
    terms = [face_term(faces[0], outer_xm, 0, -1.0), face_term(faces[1], outer_xp, 0, 1.0), face_term(faces[2], outer_ym, 1, -1.0), face_term(faces[3], outer_yp, 1, 1.0), face_term(faces[4], outer_zm, 2, -1.0), face_term(faces[5], outer_zp, 2, 1.0)]
    total = add_faces(volume(state), terms)
    return total.at[1:4].add(source)

def reference(lamb_vector, owner, element, shape_class, interp_tables, acoustic_state):
    devices = N_AX * N_AZ
    global_elements = NXE * NYE * ER
    target = owner[:, 0]
    axial_index = target // N_AZ
    azimuth_index = target % N_AZ
    elem_axial = element // (EY * ER)
    elem_azimuth = element // ER % EY
    elem_radial = element % ER
    global_index = ((axial_index * EX + elem_axial) * NYE + azimuth_index * EY + elem_azimuth) * ER + elem_radial
    keys = (shape_class * global_elements + global_index).astype(jnp.int32)
    blocks = lamb_vector.reshape(devices, FE_DEV, 3 * NF)
    key_blocks = keys.reshape(devices, FE_DEV)

    def accumulate(carry, pair):
        block, block_keys = pair
        return (carry.at[block_keys].add(block.astype(jnp.float32)), None)
    gathered, _ = lax.scan(accumulate, jnp.zeros((NTAB * global_elements, 3 * NF), jnp.float32), (blocks, key_blocks))
    gathered = gathered.reshape(NTAB, global_elements, 3, NF)
    source = jnp.einsum('keci,kij->cje', gathered, interp_tables.astype(jnp.float32), precision=lax.Precision.HIGHEST)
    source = source.reshape(3, NA, NXE, NYE, ER)
    first = operate(acoustic_state, source)
    second = operate(acoustic_state + 0.5 * TIME_STEP * first, source)
    third = operate(acoustic_state + 0.5 * TIME_STEP * second, source)
    fourth = operate(acoustic_state + TIME_STEP * third, source)
    new_state = acoustic_state + TIME_STEP / 6.0 * (first + 2.0 * second + 2.0 * third + fourth)
    return (new_state, source)
```

```python
import functools
import math

import jax
import jax.numpy as jnp
import numpy as np
from jax import lax
from jax.experimental import pallas as pl
from jax.experimental.pallas import tpu as pltpu
from jax.sharding import PartitionSpec as P

MACH = 0.3
RUSANOV = 1.3
DT = 0.03
LIFT = 10.0
VOLUME = 2.0
STEP_SCALES = (DT, DT / 2.0, DT / 3.0, DT / 4.0)

FIELDS = 5
NODES = 125
ROWS = 8
LANES = 128
VMEM_BYTES = 24 * 1024 * 1024


def derivative_matrix():
    points = np.array([-1.0, -math.sqrt(3.0 / 7.0), 0.0, math.sqrt(3.0 / 7.0), 1.0])
    weights = [1.0 / np.prod([points[j] - points[k] for k in range(5) if k != j]) for j in range(5)]
    matrix = np.zeros((5, 5))
    for i in range(5):
        for j in range(5):
            if i != j:
                matrix[i, j] = weights[j] / weights[i] / (points[i] - points[j])
        matrix[i, i] = -np.sum(matrix[i])
    return matrix


DERIVATIVE = -VOLUME * derivative_matrix()


def differentiate(g, scale):
    d = [[float(scale * v) for v in row] for row in DERIVATIVE]
    even_out, odd_out = g[0] - g[4], g[1] - g[3]
    s_out, s_in = g[0] + g[4], g[1] + g[3]
    results = [None] * 5
    for i in (0, 1):
        same = (d[i][0] - d[i][4]) / 2 * even_out + (d[i][1] - d[i][3]) / 2 * odd_out
        flip = (d[i][0] + d[i][4]) / 2 * s_out + (d[i][1] + d[i][3]) / 2 * s_in + d[i][2] * g[2]
        results[i] = same + flip
        results[4 - i] = same - flip
    results[2] = d[2][0] * even_out + d[2][1] * odd_out
    return results


def flux(q, direction):
    p, u, v, w, rho = q
    pressure = p + MACH * u
    if direction == 0:
        return [MACH * p + u, pressure, None, None, MACH * rho + u]
    if direction == 1:
        return [v, None, pressure, None, v]
    return [w, None, None, pressure, w]


def lifted(q, direction, normal, rusanov_sign):
    result = []
    for value, flow in zip(q, flux(q, direction)):
        term = (LIFT * RUSANOV * rusanov_sign) * value
        if flow is not None:
            term = term + (LIFT * normal) * flow
        result.append(term)
    return result


def coupled(jump, direction, normal, scale):
    p, u, v, w, rho = jump
    rusanov, lift = scale * LIFT * RUSANOV, scale * LIFT * normal
    if direction == 0:
        own = lift * MACH - rusanov
        if abs(own + lift) < 1e-9:
            across = lift * (u - p)
            return [across, -across, -rusanov * v, -rusanov * w, lift * (u - rho)]
        across = lift * u
        return [
            own * p + across,
            lift * p + own * u,
            -rusanov * v,
            -rusanov * w,
            own * rho + across,
        ]
    normal_velocity = (v, w)[direction - 1]
    across = lift * normal_velocity
    along = lift * p + (lift * MACH) * u - rusanov * normal_velocity
    return [
        across - rusanov * p,
        -rusanov * u,
        along if direction == 1 else -rusanov * v,
        along if direction == 2 else -rusanov * w,
        across - rusanov * rho,
    ]


def shifted(q, amount, axis, keep):
    return [jnp.where(keep, pltpu.roll(value, amount, axis), 0.0) for value in q]


def volume_into(state_ref, scale, store):
    row = lax.broadcasted_iota(jnp.int32, (ROWS, LANES), 0)
    lane = lax.broadcasted_iota(jnp.int32, (ROWS, LANES), 1)
    cell = row % 4
    keep = {
        0: (row >= 4, row < 4),
        1: (cell != 0, cell != 3),
        2: (lane != 0, lane != LANES - 1),
    }
    rolls = {0: (4, 4, 0), 1: (1, ROWS - 1, 0), 2: (1, LANES - 1, 1)}

    def load(field, node):
        return state_ref[field * NODES + node]

    def face_terms(direction, low, high):
        up, down, axis = rolls[direction]
        keep_low, keep_high = keep[direction]
        if direction == 0:
            turned = [pltpu.roll(jnp.where(keep_high, b, a), up, axis) for a, b in zip(low, high)]
            below = [jnp.where(keep_low, value, 0.0) for value in turned]
            above = [jnp.where(keep_high, value, 0.0) for value in turned]
        else:
            below = shifted(high, up, axis, keep_low)
            above = shifted(low, down, axis, keep_high)
        jump_low = [a - b for a, b in zip(low, below)]
        jump_high = [a - b for a, b in zip(high, above)]
        return coupled(jump_low, direction, -1.0, scale), coupled(jump_high, direction, 1.0, scale)

    def line(direction, nodes):
        q = [[load(f, n) for n in nodes] for f in range(FIELDS)]
        ends = face_terms(direction, [x[0] for x in q], [x[4] for x in q])
        if direction == 0:
            parts = {
                0: differentiate([MACH * q[0][k] + q[1][k] for k in range(5)], scale),
                1: differentiate([MACH * q[1][k] + q[0][k] for k in range(5)], scale),
                4: differentiate([MACH * q[4][k] + q[1][k] for k in range(5)], scale),
            }
        else:
            along = differentiate(q[direction + 1], scale)
            parts = {
                0: along,
                direction + 1: differentiate([MACH * q[1][k] + q[0][k] for k in range(5)], scale),
                4: along,
            }
        for f in range(FIELDS):
            for k in range(5):
                value = parts[f][k] if f in parts else None
                if k in (0, 4):
                    end = ends[0 if k == 0 else 1][f]
                    value = end if value is None else value + end
                store(direction, f, nodes[k], value, q[f][k])

    @pl.loop(0, 5)
    def _(outer):
        for inner in range(5):
            line(0, [k * 25 + outer * 5 + inner for k in range(5)])

    @pl.loop(0, 5)
    def _(outer):
        for inner in range(5):
            line(1, [outer * 25 + k * 5 + inner for k in range(5)])

    @pl.loop(0, 5)
    def _(outer):
        for inner in range(5):
            line(2, [outer * 25 + inner * 5 + k for k in range(5)])


def volume_first_kernel(scale, state_ref, out_ref):
    volume_into(state_ref, scale, add_to(out_ref))


def add_to(out_ref):
    def store(direction, field, node, value, q):
        at = field * NODES + node
        if direction == 0:
            out_ref[at] = jnp.zeros_like(q) if value is None else value
        elif value is not None:
            out_ref[at] += value

    return store


def volume_kernel(scale, state_ref, sum_in, out_ref, sum_ref):
    add = add_to(out_ref)

    def store(direction, field, node, value, q):
        add(direction, field, node, value, q)
        if direction == 2:
            at = field * NODES + node
            sum_ref[at] = sum_in[at] + q

    volume_into(state_ref, scale, store)


def volume_and_source_kernel(
    scale, state_ref, sum_in, source_ref, out_ref, sum_ref, out_hbm, sem
):
    copy = pltpu.make_async_copy(source_ref, out_hbm, sem.at[0])
    copy.start()
    volume_kernel(scale, state_ref, sum_in, out_ref, sum_ref)
    copy.wait()


def volume_last_kernel(scale, state_ref, sum_in, sum_ref, out_ref):
    add = add_to(out_ref)

    def store(direction, field, node, value, q):
        if direction < 2:
            add(direction, field, node, value, q)
        else:
            at = field * NODES + node
            total = sum_in[at] + q + out_ref[at]
            sum_ref[at] = total if value is None else total + value

    volume_into(state_ref, scale, store)


def on_parity(axis, even, odd):
    parity = lax.axis_index(axis) % 2
    pl.when(parity == 0)(even)
    pl.when(parity == 1)(odd)


def piece(face, row):
    if not isinstance(face, (tuple, list)):
        return face, pl.ds(row, 5)
    first = face[0].shape[0]
    return (face[0], pl.ds(row, 5)) if row < first else (face[1], pl.ds(row - first, 5))


def received(face, start):
    parts = [piece(face, f * 25 + start) for f in range(FIELDS)]
    return [ref[rows].astype(jnp.float32) for ref, rows in parts]


def add_ax(out_ref, face, high, weight):
    sign = -weight if high else weight
    first, rows = (100, slice(4, 8)) if high else (0, slice(0, 4))
    for chunk in range(5):
        terms = lifted(received(face, chunk * 5), 0, sign, weight)
        for f, term in enumerate(terms):
            out_ref[pl.ds(f * NODES + first + chunk * 5, 5), rows, :] += term


def add_far(out_ref, face, weight):
    on_parity(
        "ax",
        lambda: add_ax(out_ref, face, False, weight),
        lambda: add_ax(out_ref, face, True, weight),
    )


def add_near(out_ref, face, weight):
    on_parity(
        "ax",
        lambda: add_ax(out_ref, face, True, weight),
        lambda: add_ax(out_ref, face, False, weight),
    )


def add_az(out_ref, far, near, weight):
    def add(low, high):
        for a in range(5):
            at = a * 25
            for f, term in enumerate(lifted(received(low, a * 5), 1, weight, weight)):
                out_ref[pl.ds(f * NODES + at, 5), 0:1, :] += term[:, 0:1]
                out_ref[pl.ds(f * NODES + at, 5), 4:5, :] += term[:, 1:2]
            for f, term in enumerate(lifted(received(high, a * 5), 1, -weight, weight)):
                out_ref[pl.ds(f * NODES + at + 20, 5), 3:4, :] += term[:, 0:1]
                out_ref[pl.ds(f * NODES + at + 20, 5), 7:8, :] += term[:, 1:2]

    on_parity("az", lambda: add(far, near), lambda: add(near, far))


def pack_ax(state_ref, face, high):
    first, rows = (100, slice(4, 8)) if high else (0, slice(0, 4))
    for f in range(FIELDS):
        for at in range(0, 25, 5):
            ref, to = piece(face, f * 25 + at)
            ref[to] = state_ref[pl.ds(f * NODES + first + at, 5), rows, :].astype(jnp.bfloat16)


def pack_far(state_ref, face):
    on_parity("ax", lambda: pack_ax(state_ref, face, False), lambda: pack_ax(state_ref, face, True))


def pack_near(state_ref, face):
    on_parity("ax", lambda: pack_ax(state_ref, face, True), lambda: pack_ax(state_ref, face, False))


def pack_az(state_ref, far, near):
    def pack(az_low, az_high):
        for f in range(FIELDS):
            for a in range(5):
                at, to = f * NODES + a * 25, pl.ds((f * 5 + a) * 5, 5)
                low = [state_ref[pl.ds(at, 5), k : k + 1, :] for k in (0, 4)]
                high = [state_ref[pl.ds(at + 20, 5), k : k + 1, :] for k in (3, 7)]
                az_low[to] = jnp.concatenate(low, axis=1).astype(jnp.bfloat16)
                az_high[to] = jnp.concatenate(high, axis=1).astype(jnp.bfloat16)

    on_parity("az", lambda: pack(far, near), lambda: pack(near, far))


def load_kernel(state_hbm, state_ref, far, near_a, near_b, az_far, az_near, sems):
    copies = []
    for f in range(FIELDS):
        nodes = pl.ds(f * NODES, NODES)
        copy = pltpu.make_async_copy(state_hbm.at[nodes], state_ref.at[nodes], sems.at[f])
        copy.start()
        copies.append(copy)
    for copy in copies:
        copy.wait()
    pack_faces(state_ref, far, near_a, near_b, az_far, az_near)


def pack_faces(state_ref, far, near_a, near_b, az_far, az_near):
    pack_far(state_ref, far)
    pack_near(state_ref, (near_a, near_b))
    pack_az(state_ref, az_far, az_near)


def finish_first_kernel(
    scale, state_in, source_ref, far, near_a, near_b, az_far, az_near, state_ref, *faces
):
    add_far(state_ref, far, scale)
    add_near(state_ref, (near_a, near_b), scale)
    add_az(state_ref, az_far, az_near, scale)

    for node in range(3 * NODES):
        state_ref[NODES + node] += scale * source_ref[pl.ds(node * ROWS, ROWS), :]

    pack_faces(state_ref, *faces)


def finish_far_kernel(scale, state_in, far, az_far, az_near, state_ref, far_out):
    add_az(state_ref, az_far, az_near, scale)
    add_far(state_ref, far, scale)
    pack_far(state_ref, far_out)


def finish_near_kernel(
    scale, state_in, near_a, near_b, state_ref, near_a_out, near_b_out, az_far_out, az_near_out
):
    add_near(state_ref, (near_a, near_b), scale)
    pack_near(state_ref, (near_a_out, near_b_out))
    pack_az(state_ref, az_far_out, az_near_out)


def last_far_kernel(weight, state_in, far, az_far, az_near, state_ref, out_hbm, sems):
    add_az(state_ref, az_far, az_near, weight)
    add_far(state_ref, far, weight)
    first = 25 * (lax.axis_index("ax") % 2)
    copies = []
    for f in range(FIELDS):
        nodes = pl.ds(f * NODES + first, NODES - 25)
        copy = pltpu.make_async_copy(state_ref.at[nodes], out_hbm.at[nodes], sems.at[f])
        copy.start()
        copies.append(copy)
    for copy in copies:
        copy.wait()


def last_near_kernel(weight, state_in, out_in, near_a, near_b, state_ref, out_hbm, sems):
    add_near(state_ref, (near_a, near_b), weight)
    first = 100 - 100 * (lax.axis_index("ax") % 2)
    copies = []
    for f in range(FIELDS):
        nodes = pl.ds(f * NODES + first, 25)
        copy = pltpu.make_async_copy(state_ref.at[nodes], out_hbm.at[nodes], sems.at[f])
        copy.start()
        copies.append(copy)
    for copy in copies:
        copy.wait()


def contribution_kernel(
    capacity,
    devices,
    lamb_hbm,
    owner_hbm,
    element_hbm,
    class_hbm,
    tables_hbm,
    out_hbm,
    lamb_ref,
    owner_ref,
    rows_ref,
    tables_ref,
    out_ref,
    row_sems,
    tables_sem,
    lamb_sem,
    out_sems,
):
    flow = lamb_ref.shape[1]
    slots = devices * capacity
    row_copies = [
        pltpu.make_async_copy(owner_hbm, owner_ref, row_sems.at[0]),
        pltpu.make_async_copy(element_hbm, rows_ref.at[0], row_sems.at[1]),
        pltpu.make_async_copy(class_hbm, rows_ref.at[1], row_sems.at[2]),
    ]
    lamb_copy = pltpu.make_async_copy(lamb_hbm, lamb_ref, lamb_sem.at[0])
    tables_copy = pltpu.make_async_copy(tables_hbm, tables_ref, tables_sem.at[0])
    for copy in row_copies + [tables_copy, lamb_copy]:
        copy.start()
    for copy in row_copies:
        copy.wait()

    owner_row = owner_ref[...]
    rows = jnp.concatenate(
        [rows_ref[0], rows_ref[1], jnp.zeros((ROWS - 2, flow), jnp.int32)], axis=0
    )
    columns = jnp.transpose(rows.astype(jnp.float32))
    element = columns[:, 0:1]
    second = columns[:, 1:2]

    owned = (lax.broadcasted_iota(jnp.int32, (devices, flow), 0) == owner_row).astype(jnp.float32)
    earlier = lax.broadcasted_iota(jnp.int32, (flow, flow), 0) < lax.broadcasted_iota(
        jnp.int32, (flow, flow), 1
    )
    running = jnp.dot(
        owned.astype(jnp.bfloat16),
        earlier.astype(jnp.bfloat16),
        preferred_element_type=jnp.float32,
    )
    position = jnp.sum(running * owned, axis=0, keepdims=True).astype(jnp.int32)
    slot_row = owner_row * capacity + position
    placing = (lax.broadcasted_iota(jnp.int32, (slots, flow), 0) == slot_row).astype(jnp.bfloat16)

    tables_copy.wait()
    spare = jnp.zeros((LANES - NODES, lamb_ref.shape[2]), jnp.bfloat16)
    tables = jnp.concatenate([tables_ref[:, 0, :], spare, tables_ref[:, 1, :], spare], axis=0)
    lamb_copy.wait()
    both = lax.dot_general(
        lamb_ref[...].reshape(3 * flow, lamb_ref.shape[2]),
        tables,
        (((1,), (1,)), ((), ())),
        preferred_element_type=jnp.float32,
    )
    use_second = jnp.broadcast_to(second, (flow, LANES)) > 0.5
    values = [
        jnp.where(
            use_second, both[c * flow : (c + 1) * flow, LANES:], both[c * flow : (c + 1) * flow, :LANES]
        )
        for c in range(3)
    ]
    largest = jnp.maximum(jnp.maximum(jnp.abs(values[0]), jnp.abs(values[1])), jnp.abs(values[2]))
    largest = jnp.max(largest, axis=1, keepdims=True)
    exponent = jnp.clip(jnp.ceil(jnp.log2(jnp.maximum(largest, 1e-36))), -100.0, 30.0)
    scale = jnp.broadcast_to(jnp.exp2(14.0 - exponent), (flow, LANES))
    column = lax.broadcasted_iota(jnp.int32, (flow, LANES), 1)
    out_copies = []
    for c in range(3):
        whole = jnp.round(values[c] * scale)
        if c == 0:
            whole = jnp.where(column == NODES, exponent, whole)
            whole = jnp.where(column == NODES + 1, element, whole)
        high = jnp.floor(whole * (1.0 / 256.0))
        low = whole - 256.0 * high
        pieces = jnp.concatenate([high, low], axis=1).astype(jnp.bfloat16)
        placed = jnp.dot(placing, pieces, preferred_element_type=jnp.float32)
        placed = placed[:, :LANES] * 256.0 + placed[:, LANES:]
        out_ref[c] = placed.astype(jnp.int32).astype(jnp.int16)
        copy = pltpu.make_async_copy(
            out_ref.at[c], out_hbm.at[:, pl.ds(c * LANES, LANES)], out_sems.at[c]
        )
        copy.start()
        out_copies.append(copy)
    for copy in out_copies:
        copy.wait()


def source_kernel(received_ref, source_ref):
    slots = received_ref.shape[0]
    wide = 2 * LANES
    highs, lows = [], []
    for c in range(3):
        values = received_ref[:, pl.ds(c * LANES, LANES)].astype(jnp.int32).astype(jnp.float32)
        if c == 0:
            element = values[:, NODES + 1 : NODES + 2].astype(jnp.int32)
        values = jnp.transpose(values)
        if c == 0:
            scale = jnp.exp2(values[NODES : NODES + 1, :] - 14.0)
        values = values * scale
        high = values.astype(jnp.bfloat16)
        highs.append(high)
        lows.append((values - high.astype(jnp.float32)).astype(jnp.bfloat16))
    parts = jnp.concatenate(highs + lows, axis=0)
    column = lax.broadcasted_iota(jnp.int32, (slots, wide), 1)
    for group in range(ROWS // 2):
        member = (element == column + group * wide).astype(jnp.bfloat16)
        total = jnp.dot(parts, member, preferred_element_type=jnp.float32)
        total = total[0 : 3 * LANES] + total[3 * LANES :]
        for c in range(3):
            for k in range(2):
                start = c * NODES * ROWS + group * 2 + k
                source_ref[pl.ds(start, NODES, stride=ROWS), :] = total[
                    c * LANES : c * LANES + NODES, k * LANES : (k + 1) * LANES
                ]

STATE = (FIELDS * NODES, ROWS, LANES)
AX_FACE = (FIELDS * 25, 4, LANES)
NEAR_PIECES = ((65, 4, LANES), (60, 4, LANES))
AZ_FACE = (132, 2, LANES)


IN_VMEM = pl.BlockSpec(memory_space=pltpu.VMEM)
IN_HBM = pl.BlockSpec(memory_space=pltpu.HBM)


def in_hbm(x):
    return pltpu.with_memory_space_constraint(x, pltpu.HBM)


def call(kernel, out_shape, in_specs, out_specs=IN_VMEM, aliases=None, scratch=()):
    if not isinstance(out_specs, list):
        out_specs = jax.tree.map(lambda _: out_specs, out_shape)
    return pl.pallas_call(
        kernel,
        out_shape=out_shape,
        in_specs=in_specs if isinstance(in_specs, list) else [IN_VMEM] * in_specs,
        out_specs=out_specs,
        scratch_shapes=scratch,
        input_output_aliases=aliases or {},
        compiler_params=pltpu.CompilerParams(vmem_limit_bytes=VMEM_BYTES),
    )


def swap(far, near):
    count = lax.axis_size("ax")
    pairs = ([], [])
    for i in range(count - 1):
        pairs[i % 2].extend([(i, i + 1), (i + 1, i)])
    return (
        None if far is None else lax.ppermute(far, "ax", pairs[1]),
        None if near is None else [lax.ppermute(part, "ax", pairs[0]) for part in near],
    )


def turn(far, near):
    count = lax.axis_size("az")
    pairs = ([], [])
    for i in range(count):
        pairs[i % 2].extend([(i, (i + 1) % count), ((i + 1) % count, i)])
    return lax.ppermute(far, "az", pairs[1]), lax.ppermute(near, "az", pairs[0])


def body(lamb_vector, owner, element, shape_class, interp_tables, acoustic_state):
    devices = lax.axis_size("ax") * lax.axis_size("az")
    flow, _, points = lamb_vector.shape
    capacity = max(2, 3 * flow // devices)
    slots = devices * capacity
    f32, bf16 = jnp.float32, jnp.bfloat16

    state = acoustic_state.reshape(STATE)
    face_shapes = [jax.ShapeDtypeStruct(s, bf16) for s in (AX_FACE, *NEAR_PIECES, AZ_FACE, AZ_FACE)]
    vmem_state = pltpu.VMEM(STATE, f32)
    source_shape = (3 * NODES * ROWS, LANES)

    buffer = call(
        functools.partial(contribution_kernel, capacity, devices),
        pltpu.HBM((slots, 3 * LANES), jnp.int16),
        [IN_HBM] * 5,
        IN_HBM,
        scratch=[
            pltpu.VMEM((3, flow, points), bf16),
            pltpu.VMEM((1, flow), jnp.int32),
            pltpu.VMEM((2, 1, flow), jnp.int32),
            pltpu.VMEM((NODES, 2, points), bf16),
            pltpu.VMEM((3, slots, LANES), jnp.int16),
            pltpu.SemaphoreType.DMA((3,)),
            pltpu.SemaphoreType.DMA((1,)),
            pltpu.SemaphoreType.DMA((1,)),
            pltpu.SemaphoreType.DMA((3,)),
        ],
    )(
        in_hbm(jnp.transpose(lamb_vector, (1, 0, 2))),
        in_hbm(owner.reshape(1, flow)),
        in_hbm(element.reshape(1, flow)),
        in_hbm(shape_class.reshape(1, flow)),
        in_hbm(jnp.transpose(interp_tables, (2, 0, 1))),
    )
    routed = lax.all_to_all(buffer, ("ax", "az"), split_axis=0, concat_axis=0, tiled=True)

    state, far, *near, az_far, az_near = call(
        load_kernel,
        [vmem_state] + face_shapes,
        [IN_HBM],
        scratch=[pltpu.SemaphoreType.DMA((FIELDS,))],
    )(in_hbm(state))
    far, near = swap(far, near)
    az_far, az_near = turn(az_far, az_near)
    moved = call(functools.partial(volume_first_kernel, STEP_SCALES[0]), vmem_state, 1)(state)
    source = call(source_kernel, pltpu.VMEM(source_shape, f32), 1)(routed)
    rate, far, *near, az_far, az_near = call(
        functools.partial(finish_first_kernel, STEP_SCALES[0]),
        [vmem_state] + face_shapes,
        7,
        aliases={0: 0},
    )(moved, source, far, *near, az_far, az_near)
    far, near = swap(far, near)
    az_far, az_near = turn(az_far, az_near)
    moved, total, source = call(
        functools.partial(volume_and_source_kernel, STEP_SCALES[1]),
        [vmem_state, vmem_state, pltpu.HBM(source_shape, f32)],
        3,
        [IN_VMEM, IN_VMEM, IN_HBM],
        scratch=[pltpu.SemaphoreType.DMA((1,))],
    )(rate, state, source)

    for scale in STEP_SCALES[1:3]:
        rate, far = call(
            functools.partial(finish_far_kernel, scale),
            [vmem_state, face_shapes[0]],
            4,
            aliases={0: 0},
        )(moved, far, az_far, az_near)
        far, _ = swap(far, None)
        rate, *near, az_far, az_near = call(
            functools.partial(finish_near_kernel, scale),
            [vmem_state] + face_shapes[1:],
            3,
            aliases={0: 0},
        )(rate, *near)
        _, near = swap(None, near)
        az_far, az_near = turn(az_far, az_near)
        if scale == STEP_SCALES[1]:
            moved, total = call(
                functools.partial(volume_kernel, STEP_SCALES[2]), [vmem_state, vmem_state], 2
            )(rate, total)

    total = call(
        functools.partial(volume_last_kernel, STEP_SCALES[3]),
        vmem_state,
        2,
        scratch=[pltpu.VMEM(STATE, f32)],
    )(rate, total)
    hbm_state = pltpu.HBM(STATE, f32)
    total, partial = call(
        functools.partial(last_far_kernel, STEP_SCALES[3]),
        [vmem_state, hbm_state],
        4,
        [IN_VMEM, IN_HBM],
        aliases={0: 0},
        scratch=[pltpu.SemaphoreType.DMA((FIELDS,))],
    )(total, far, az_far, az_near)
    _, new_state = call(
        functools.partial(last_near_kernel, STEP_SCALES[3]),
        [vmem_state, hbm_state],
        [IN_VMEM, IN_HBM, IN_VMEM, IN_VMEM],
        [IN_VMEM, IN_HBM],
        aliases={0: 0, 1: 1},
        scratch=[pltpu.SemaphoreType.DMA((FIELDS,))],
    )(total, partial, *near)
    shape = acoustic_state.shape
    return new_state.reshape(shape), source.reshape((3,) + shape[1:])


def solution(mesh):
    in_specs = (
        P(("ax", "az"), None, None),
        P(("ax", "az"), None),
        P(("ax", "az")),
        P(("ax", "az")),
        P(),
        P(None, None, "ax", "az", None),
    )
    out_specs = (P(None, None, "ax", "az", None), P(None, None, "ax", "az", None))
    return jax.shard_map(body, mesh=mesh, in_specs=in_specs, out_specs=out_specs, check_vma=False)
```

```python
import functools
import math

import jax
import jax.numpy as jnp
import numpy as np
from jax import lax
from jax.experimental import pallas as pl
from jax.experimental.pallas import tpu as pltpu
from jax.sharding import PartitionSpec as P

MACH = 0.3
RUSANOV = 1.3
DT = 0.03
LIFT = 10.0
VOLUME = 2.0
STEP_SCALES = (DT, DT / 2.0, DT / 3.0, DT / 4.0)

FIELDS = 5
NODES = 125
ROWS = 8
LANES = 128
VMEM_BYTES = 24 * 1024 * 1024


def derivative_matrix():
    points = np.array([-1.0, -math.sqrt(3.0 / 7.0), 0.0, math.sqrt(3.0 / 7.0), 1.0])
    weights = [1.0 / np.prod([points[j] - points[k] for k in range(5) if k != j]) for j in range(5)]
    matrix = np.zeros((5, 5))
    for i in range(5):
        for j in range(5):
            if i != j:
                matrix[i, j] = weights[j] / weights[i] / (points[i] - points[j])
        matrix[i, i] = -np.sum(matrix[i])
    return matrix


DERIVATIVE = -VOLUME * derivative_matrix()


def differentiate(g, scale):
    d = [[float(scale * v) for v in row] for row in DERIVATIVE]
    even_out, odd_out = g[0] - g[4], g[1] - g[3]
    s_out, s_in = g[0] + g[4], g[1] + g[3]
    results = [None] * 5
    for i in (0, 1):
        same = (d[i][0] - d[i][4]) / 2 * even_out + (d[i][1] - d[i][3]) / 2 * odd_out
        flip = (d[i][0] + d[i][4]) / 2 * s_out + (d[i][1] + d[i][3]) / 2 * s_in + d[i][2] * g[2]
        results[i] = same + flip
        results[4 - i] = same - flip
    results[2] = d[2][0] * even_out + d[2][1] * odd_out
    return results


def flux(q, direction):
    g, u, v, w, e = q
    if direction == 0:
        return [(2.0 * MACH) * g + (1.0 - MACH**2) * u, g, None, None, MACH * e]
    if direction == 1:
        return [v, None, g, None, None]
    return [w, None, None, g, None]


def original(q):
    g, u, v, w, e = q
    p = g - MACH * u
    return [p, u, v, w, e + p]


def lifted(q, direction, normal, rusanov_sign):
    result = []
    for value, flow in zip(q, flux(q, direction)):
        term = (LIFT * RUSANOV * rusanov_sign) * value
        if flow is not None:
            term = term + (LIFT * normal) * flow
        result.append(term)
    return result


def coupled(jump, direction, normal, scale):
    g, u, v, w, e = jump
    rusanov, lift = scale * LIFT * RUSANOV, scale * LIFT * normal
    if direction == 0:
        return [
            (2.0 * MACH * lift - rusanov) * g + ((1.0 - MACH**2) * lift) * u,
            lift * g - rusanov * u,
            -rusanov * v,
            -rusanov * w,
            (MACH * lift - rusanov) * e,
        ]
    normal_velocity = (v, w)[direction - 1]
    along = lift * g - rusanov * normal_velocity
    return [
        lift * normal_velocity - rusanov * g,
        -rusanov * u,
        along if direction == 1 else -rusanov * v,
        along if direction == 2 else -rusanov * w,
        -rusanov * e,
    ]


def shifted(q, amount, axis, keep):
    return [jnp.where(keep, pltpu.roll(value, amount, axis), 0.0) for value in q]


def volume_into(state_ref, scale, store):
    row = lax.broadcasted_iota(jnp.int32, (ROWS, LANES), 0)
    lane = lax.broadcasted_iota(jnp.int32, (ROWS, LANES), 1)
    cell = row % 4
    keep = {
        0: (row >= 4, row < 4),
        1: (cell != 0, cell != 3),
        2: (lane != 0, lane != LANES - 1),
    }
    rolls = {0: (4, 4, 0), 1: (1, ROWS - 1, 0), 2: (1, LANES - 1, 1)}

    def load(field, node):
        return state_ref[field * NODES + node]

    def face_terms(direction, low, high):
        up, down, axis = rolls[direction]
        keep_low, keep_high = keep[direction]
        if direction == 0:
            turned = [pltpu.roll(jnp.where(keep_high, b, a), up, axis) for a, b in zip(low, high)]
            below = [jnp.where(keep_low, value, 0.0) for value in turned]
            above = [jnp.where(keep_high, value, 0.0) for value in turned]
        else:
            below = shifted(high, up, axis, keep_low)
            above = shifted(low, down, axis, keep_high)
        jump_low = [a - b for a, b in zip(low, below)]
        jump_high = [a - b for a, b in zip(high, above)]
        return coupled(jump_low, direction, -1.0, scale), coupled(jump_high, direction, 1.0, scale)

    def line(direction, nodes):
        q = [[load(f, n) for n in nodes] for f in range(FIELDS)]
        ends = face_terms(direction, [x[0] for x in q], [x[4] for x in q])
        g, u, e = q[0], q[1], q[4]
        if direction == 0:
            mixed = [(2.0 * MACH) * g[k] + (1.0 - MACH**2) * u[k] for k in range(5)]
            parts = {
                0: differentiate(mixed, scale),
                1: differentiate(g, scale),
                4: differentiate(e, scale * MACH),
            }
        else:
            parts = {
                0: differentiate(q[direction + 1], scale),
                direction + 1: differentiate(g, scale),
            }
        values = []
        for f in range(FIELDS):
            row = list(parts[f]) if f in parts else [None] * 5
            for k, end in ((0, ends[0][f]), (4, ends[1][f])):
                row[k] = end if row[k] is None else row[k] + end
            values.append(row)
        store(direction, nodes, values, q)

    @pl.loop(0, 5)
    def _(outer):
        for inner in range(5):
            line(0, [k * 25 + outer * 5 + inner for k in range(5)])

    @pl.loop(0, 5)
    def _(outer):
        for inner in range(5):
            line(1, [outer * 25 + k * 5 + inner for k in range(5)])

    @pl.loop(0, 5)
    def _(outer):
        for inner in range(5):
            line(2, [outer * 25 + inner * 5 + k for k in range(5)])


def volume_first_kernel(scale, state_ref, out_ref):
    volume_into(state_ref, scale, add_to(out_ref))


def add_to(out_ref):
    def store(direction, nodes, values, q):
        for f in range(FIELDS):
            for node, value in zip(nodes, values[f]):
                at = f * NODES + node
                if direction == 0:
                    out_ref[at] = jnp.zeros_like(q[0][0]) if value is None else value
                elif value is not None:
                    out_ref[at] += value

    return store


def volume_kernel(scale, state_ref, sum_in, out_ref, sum_ref):
    add = add_to(out_ref)

    def store(direction, nodes, values, q):
        add(direction, nodes, values, q)
        if direction == 2:
            for f in range(FIELDS):
                for node, value in zip(nodes, q[f]):
                    at = f * NODES + node
                    sum_ref[at] = sum_in[at] + value

    volume_into(state_ref, scale, store)


def volume_and_source_kernel(
    scale, state_ref, sum_in, source_ref, out_ref, sum_ref, out_hbm, sem
):
    copy = pltpu.make_async_copy(source_ref, out_hbm, sem.at[0])
    copy.start()
    volume_kernel(scale, state_ref, sum_in, out_ref, sum_ref)
    copy.wait()


def volume_last_kernel(scale, state_ref, sum_in, sum_ref, out_ref):
    add = add_to(out_ref)

    def store(direction, nodes, values, q):
        if direction < 2:
            add(direction, nodes, values, q)
            return
        for k, node in enumerate(nodes):
            totals = []
            for f in range(FIELDS):
                at = f * NODES + node
                total = sum_in[at] + q[f][k] + out_ref[at]
                totals.append(total if values[f][k] is None else total + values[f][k])
            for f, total in enumerate(original(totals)):
                sum_ref[f * NODES + node] = total

    volume_into(state_ref, scale, store)


def on_parity(axis, even, odd):
    parity = lax.axis_index(axis) % 2
    pl.when(parity == 0)(even)
    pl.when(parity == 1)(odd)


def received(ref, start):
    return [ref[pl.ds(f * 25 + start, 5)].astype(jnp.float32) for f in range(FIELDS)]


def add_ax(out_ref, face, high, weight, final):
    sign = -weight if high else weight
    first, rows = (100, slice(4, 8)) if high else (0, slice(0, 4))
    for chunk in range(5):
        terms = lifted(received(face, chunk * 5), 0, sign, weight)
        terms = original(terms) if final else terms
        for f, term in enumerate(terms):
            out_ref[pl.ds(f * NODES + first + chunk * 5, 5), rows, :] += term


def add_far(out_ref, face, weight, final=False):
    on_parity(
        "ax",
        lambda: add_ax(out_ref, face, False, weight, final),
        lambda: add_ax(out_ref, face, True, weight, final),
    )


def add_near(out_ref, face, weight, final=False):
    on_parity(
        "ax",
        lambda: add_ax(out_ref, face, True, weight, final),
        lambda: add_ax(out_ref, face, False, weight, final),
    )


def add_az(out_ref, far, near, weight, final=False):
    def add_side(face, at, rows, chunk, sign):
        terms = lifted(received(face, chunk), 1, sign, weight)
        for f, term in enumerate(original(terms) if final else terms):
            for k, row in enumerate(rows):
                out_ref[pl.ds(f * NODES + at, 5), row : row + 1, :] += term[:, k : k + 1]

    def add(low, high):
        for a in range(5):
            add_side(low, a * 25, (0, 4), a * 5, weight)
            add_side(high, a * 25 + 20, (3, 7), a * 5, -weight)

    on_parity("az", lambda: add(far, near), lambda: add(near, far))


def pack_ax(state_ref, face, high):
    first, rows = (100, slice(4, 8)) if high else (0, slice(0, 4))
    for f in range(FIELDS):
        face[pl.ds(f * 25, 25)] = state_ref[pl.ds(f * NODES + first, 25), rows, :].astype(
            jnp.bfloat16
        )


def pack_far(state_ref, face):
    on_parity("ax", lambda: pack_ax(state_ref, face, False), lambda: pack_ax(state_ref, face, True))


def pack_near(state_ref, face):
    on_parity("ax", lambda: pack_ax(state_ref, face, True), lambda: pack_ax(state_ref, face, False))


def pack_az(state_ref, far, near):
    def pack(az_low, az_high):
        for f in range(FIELDS):
            for a in range(5):
                at, to = f * NODES + a * 25, pl.ds((f * 5 + a) * 5, 5)
                low = [state_ref[pl.ds(at, 5), k : k + 1, :] for k in (0, 4)]
                high = [state_ref[pl.ds(at + 20, 5), k : k + 1, :] for k in (3, 7)]
                az_low[to] = jnp.concatenate(low, axis=1).astype(jnp.bfloat16)
                az_high[to] = jnp.concatenate(high, axis=1).astype(jnp.bfloat16)

    on_parity("az", lambda: pack(far, near), lambda: pack(near, far))


def load_kernel(state_hbm, state_ref, far, near, az_far, az_near, sems):
    copies = []
    for f in range(FIELDS):
        nodes = pl.ds(f * NODES, NODES)
        copy = pltpu.make_async_copy(state_hbm.at[nodes], state_ref.at[nodes], sems.at[f])
        copy.start()
        copies.append(copy)
    for copy in copies:
        copy.wait()

    @pl.loop(0, NODES // 5)
    def _(chunk):
        for k in range(5):
            node = chunk * 5 + k
            p = state_ref[node]
            state_ref[node] = p + MACH * state_ref[NODES + node]
            state_ref[4 * NODES + node] -= p

    pack_faces(state_ref, far, near, az_far, az_near)


def pack_faces(state_ref, far, near, az_far, az_near):
    pack_far(state_ref, far)
    pack_near(state_ref, near)
    pack_az(state_ref, az_far, az_near)


def finish_first_kernel(
    scale, state_in, source_ref, far, near, az_far, az_near, state_ref, *faces
):
    add_far(state_ref, far, scale)
    add_near(state_ref, near, scale)
    add_az(state_ref, az_far, az_near, scale)

    for node in range(3 * NODES):
        value = scale * source_ref[pl.ds(node * ROWS, ROWS), :]
        state_ref[NODES + node] += value
        if node < NODES:
            state_ref[node] += MACH * value

    pack_faces(state_ref, *faces)


def finish_far_kernel(scale, state_in, far, az_far, az_near, state_ref, far_out):
    add_az(state_ref, az_far, az_near, scale)
    add_far(state_ref, far, scale)
    pack_far(state_ref, far_out)


def finish_near_kernel(scale, state_in, near, state_ref, near_out, az_far_out, az_near_out):
    add_near(state_ref, near, scale)
    pack_near(state_ref, near_out)
    pack_az(state_ref, az_far_out, az_near_out)


def last_far_kernel(weight, state_in, far, az_far, az_near, state_ref, out_hbm, sems):
    add_az(state_ref, az_far, az_near, weight, final=True)
    add_far(state_ref, far, weight, final=True)
    first = 25 * (lax.axis_index("ax") % 2)
    copies = []
    for f in range(FIELDS):
        nodes = pl.ds(f * NODES + first, NODES - 25)
        copy = pltpu.make_async_copy(state_ref.at[nodes], out_hbm.at[nodes], sems.at[f])
        copy.start()
        copies.append(copy)
    for copy in copies:
        copy.wait()


def last_near_kernel(weight, state_in, out_in, near, state_ref, out_hbm, sems):
    add_near(state_ref, near, weight, final=True)
    first = 100 - 100 * (lax.axis_index("ax") % 2)
    copies = []
    for f in range(FIELDS):
        nodes = pl.ds(f * NODES + first, 25)
        copy = pltpu.make_async_copy(state_ref.at[nodes], out_hbm.at[nodes], sems.at[f])
        copy.start()
        copies.append(copy)
    for copy in copies:
        copy.wait()


def contribution_kernel(
    capacity,
    devices,
    lamb_hbm,
    owner_hbm,
    element_hbm,
    class_hbm,
    tables_hbm,
    out_hbm,
    lamb_ref,
    owner_ref,
    rows_ref,
    tables_ref,
    out_ref,
    row_sems,
    tables_sem,
    lamb_sem,
    out_sems,
):
    flow = lamb_ref.shape[1]
    slots = devices * capacity
    row_copies = [
        pltpu.make_async_copy(owner_hbm, owner_ref, row_sems.at[0]),
        pltpu.make_async_copy(element_hbm, rows_ref.at[0], row_sems.at[1]),
        pltpu.make_async_copy(class_hbm, rows_ref.at[1], row_sems.at[2]),
    ]
    lamb_copy = pltpu.make_async_copy(lamb_hbm, lamb_ref, lamb_sem.at[0])
    tables_copy = pltpu.make_async_copy(tables_hbm, tables_ref, tables_sem.at[0])
    for copy in row_copies + [tables_copy, lamb_copy]:
        copy.start()
    for copy in row_copies:
        copy.wait()

    owner_row = owner_ref[...]
    rows = jnp.concatenate(
        [rows_ref[0], rows_ref[1], jnp.zeros((ROWS - 2, flow), jnp.int32)], axis=0
    )
    columns = jnp.transpose(rows.astype(jnp.float32))
    element = columns[:, 0:1]
    second = columns[:, 1:2]

    owned = (lax.broadcasted_iota(jnp.int32, (devices, flow), 0) == owner_row).astype(jnp.float32)
    earlier = lax.broadcasted_iota(jnp.int32, (flow, flow), 0) < lax.broadcasted_iota(
        jnp.int32, (flow, flow), 1
    )
    running = jnp.dot(
        owned.astype(jnp.bfloat16),
        earlier.astype(jnp.bfloat16),
        preferred_element_type=jnp.float32,
    )
    position = jnp.sum(running * owned, axis=0, keepdims=True).astype(jnp.int32)
    slot_row = owner_row * capacity + position
    placing = (lax.broadcasted_iota(jnp.int32, (slots, flow), 0) == slot_row).astype(jnp.bfloat16)

    tables_copy.wait()
    spare = jnp.zeros((LANES - NODES, lamb_ref.shape[2]), jnp.bfloat16)
    tables = jnp.concatenate([tables_ref[:, 0, :], spare, tables_ref[:, 1, :], spare], axis=0)
    lamb_copy.wait()
    both = lax.dot_general(
        lamb_ref[...].reshape(3 * flow, lamb_ref.shape[2]),
        tables,
        (((1,), (1,)), ((), ())),
        preferred_element_type=jnp.float32,
    )
    use_second = jnp.broadcast_to(second, (flow, LANES)) > 0.5
    values = [
        jnp.where(
            use_second, both[c * flow : (c + 1) * flow, LANES:], both[c * flow : (c + 1) * flow, :LANES]
        )
        for c in range(3)
    ]
    largest = jnp.maximum(jnp.maximum(jnp.abs(values[0]), jnp.abs(values[1])), jnp.abs(values[2]))
    largest = jnp.max(largest, axis=1, keepdims=True)
    exponent = jnp.clip(jnp.ceil(jnp.log2(jnp.maximum(largest, 1e-36))), -100.0, 30.0)
    scale = jnp.broadcast_to(jnp.exp2(14.0 - exponent), (flow, LANES))
    column = lax.broadcasted_iota(jnp.int32, (flow, LANES), 1)
    out_copies = []
    for c in range(3):
        whole = jnp.round(values[c] * scale)
        if c == 0:
            whole = jnp.where(column == NODES, exponent, whole)
            whole = jnp.where(column == NODES + 1, element, whole)
        high = jnp.floor(whole * (1.0 / 256.0))
        low = whole - 256.0 * high
        pieces = jnp.concatenate([high, low], axis=1).astype(jnp.bfloat16)
        placed = jnp.dot(placing, pieces, preferred_element_type=jnp.float32)
        placed = placed[:, :LANES] * 256.0 + placed[:, LANES:]
        out_ref[c] = placed.astype(jnp.int32).astype(jnp.int16)
        copy = pltpu.make_async_copy(
            out_ref.at[c], out_hbm.at[:, pl.ds(c * LANES, LANES)], out_sems.at[c]
        )
        copy.start()
        out_copies.append(copy)
    for copy in out_copies:
        copy.wait()


def source_kernel(received_ref, source_ref):
    slots = received_ref.shape[0]
    wide = 2 * LANES
    highs, lows = [], []
    for c in range(3):
        values = received_ref[:, pl.ds(c * LANES, LANES)].astype(jnp.int32).astype(jnp.float32)
        if c == 0:
            element = values[:, NODES + 1 : NODES + 2].astype(jnp.int32)
        values = jnp.transpose(values)
        if c == 0:
            scale = jnp.exp2(values[NODES : NODES + 1, :] - 14.0)
        values = values * scale
        high = values.astype(jnp.bfloat16)
        highs.append(high)
        lows.append((values - high.astype(jnp.float32)).astype(jnp.bfloat16))
    parts = jnp.concatenate(highs + lows, axis=0)
    column = lax.broadcasted_iota(jnp.int32, (slots, wide), 1)
    for group in range(ROWS // 2):
        member = (element == column + group * wide).astype(jnp.bfloat16)
        total = jnp.dot(parts, member, preferred_element_type=jnp.float32)
        total = total[0 : 3 * LANES] + total[3 * LANES :]
        for c in range(3):
            for k in range(2):
                start = c * NODES * ROWS + group * 2 + k
                source_ref[pl.ds(start, NODES, stride=ROWS), :] = total[
                    c * LANES : c * LANES + NODES, k * LANES : (k + 1) * LANES
                ]

STATE = (FIELDS * NODES, ROWS, LANES)
AX_FACE = (FIELDS * 25, 4, LANES)
AZ_FACE = (FIELDS * 25, 2, LANES)


LONG = pl.CostEstimate(flops=10**11, bytes_accessed=10**9, transcendentals=0)
IN_VMEM = pl.BlockSpec(memory_space=pltpu.VMEM)
IN_HBM = pl.BlockSpec(memory_space=pltpu.HBM)


def in_hbm(x):
    return pltpu.with_memory_space_constraint(x, pltpu.HBM)


def call(kernel, out_shape, in_specs, out_specs=IN_VMEM, aliases=None, scratch=(), cost=None):
    if not isinstance(out_specs, list):
        out_specs = jax.tree.map(lambda _: out_specs, out_shape)
    return pl.pallas_call(
        kernel,
        out_shape=out_shape,
        in_specs=in_specs if isinstance(in_specs, list) else [IN_VMEM] * in_specs,
        out_specs=out_specs,
        scratch_shapes=scratch,
        input_output_aliases=aliases or {},
        cost_estimate=cost,
        compiler_params=pltpu.CompilerParams(vmem_limit_bytes=VMEM_BYTES),
    )


def swap(far, near):
    count = lax.axis_size("ax")
    pairs = ([], [])
    for i in range(count - 1):
        pairs[i % 2].extend([(i, i + 1), (i + 1, i)])
    return (
        None if far is None else lax.ppermute(far, "ax", pairs[1]),
        None if near is None else lax.ppermute(near, "ax", pairs[0]),
    )


def turn(far, near):
    count = lax.axis_size("az")
    pairs = ([], [])
    for i in range(count):
        pairs[i % 2].extend([(i, (i + 1) % count), ((i + 1) % count, i)])
    return lax.ppermute(far, "az", pairs[1]), lax.ppermute(near, "az", pairs[0])


def body(lamb_vector, owner, element, shape_class, interp_tables, acoustic_state):
    devices = lax.axis_size("ax") * lax.axis_size("az")
    flow, _, points = lamb_vector.shape
    capacity = max(2, 3 * flow // devices)
    slots = devices * capacity
    f32, bf16 = jnp.float32, jnp.bfloat16

    state = acoustic_state.reshape(STATE)
    face_shapes = [jax.ShapeDtypeStruct(s, bf16) for s in (AX_FACE, AX_FACE, AZ_FACE, AZ_FACE)]
    vmem_state = pltpu.VMEM(STATE, f32)
    source_shape = (3 * NODES * ROWS, LANES)

    buffer = call(
        functools.partial(contribution_kernel, capacity, devices),
        pltpu.HBM((slots, 3 * LANES), jnp.int16),
        [IN_HBM] * 5,
        IN_HBM,
        scratch=[
            pltpu.VMEM((3, flow, points), bf16),
            pltpu.VMEM((1, flow), jnp.int32),
            pltpu.VMEM((2, 1, flow), jnp.int32),
            pltpu.VMEM((NODES, 2, points), bf16),
            pltpu.VMEM((3, slots, LANES), jnp.int16),
            pltpu.SemaphoreType.DMA((3,)),
            pltpu.SemaphoreType.DMA((1,)),
            pltpu.SemaphoreType.DMA((1,)),
            pltpu.SemaphoreType.DMA((3,)),
        ],
    )(
        in_hbm(jnp.transpose(lamb_vector, (1, 0, 2))),
        in_hbm(owner.reshape(1, flow)),
        in_hbm(element.reshape(1, flow)),
        in_hbm(shape_class.reshape(1, flow)),
        in_hbm(jnp.transpose(interp_tables, (2, 0, 1))),
    )
    routed = lax.all_to_all(buffer, ("ax", "az"), split_axis=0, concat_axis=0, tiled=True)

    state, far, near, az_far, az_near = call(
        load_kernel,
        [vmem_state] + face_shapes,
        [IN_HBM],
        scratch=[pltpu.SemaphoreType.DMA((FIELDS,))],
    )(in_hbm(state))
    far, near = swap(far, near)
    az_far, az_near = turn(az_far, az_near)
    moved = call(functools.partial(volume_first_kernel, STEP_SCALES[0]), vmem_state, 1)(state)
    source = call(source_kernel, pltpu.VMEM(source_shape, f32), 1)(routed)
    rate, far, near, az_far, az_near = call(
        functools.partial(finish_first_kernel, STEP_SCALES[0]),
        [vmem_state] + face_shapes,
        6,
        aliases={0: 0},
    )(moved, source, far, near, az_far, az_near)
    far, near = swap(far, near)
    az_far, az_near = turn(az_far, az_near)
    moved, total, source = call(
        functools.partial(volume_and_source_kernel, STEP_SCALES[1]),
        [vmem_state, vmem_state, pltpu.HBM(source_shape, f32)],
        3,
        [IN_VMEM, IN_VMEM, IN_HBM],
        scratch=[pltpu.SemaphoreType.DMA((1,))],
    )(rate, state, source)

    for scale in STEP_SCALES[1:3]:
        rate, far = call(
            functools.partial(finish_far_kernel, scale),
            [vmem_state, face_shapes[0]],
            4,
            aliases={0: 0},
            cost=LONG,
        )(moved, far, az_far, az_near)
        far, _ = swap(far, None)
        rate, near, az_far, az_near = call(
            functools.partial(finish_near_kernel, scale),
            [vmem_state] + face_shapes[1:],
            2,
            aliases={0: 0},
        )(rate, near)
        _, near = swap(None, near)
        az_far, az_near = turn(az_far, az_near)
        if scale == STEP_SCALES[1]:
            moved, total = call(
                functools.partial(volume_kernel, STEP_SCALES[2]), [vmem_state, vmem_state], 2
            )(rate, total)

    total = call(
        functools.partial(volume_last_kernel, STEP_SCALES[3]),
        vmem_state,
        2,
        scratch=[pltpu.VMEM(STATE, f32)],
    )(rate, total)
    hbm_state = pltpu.HBM(STATE, f32)
    total, partial = call(
        functools.partial(last_far_kernel, STEP_SCALES[3]),
        [vmem_state, hbm_state],
        4,
        [IN_VMEM, IN_HBM],
        aliases={0: 0},
        cost=LONG,
        scratch=[pltpu.SemaphoreType.DMA((FIELDS,))],
    )(total, far, az_far, az_near)
    _, new_state = call(
        functools.partial(last_near_kernel, STEP_SCALES[3]),
        [vmem_state, hbm_state],
        [IN_VMEM, IN_HBM, IN_VMEM],
        [IN_VMEM, IN_HBM],
        aliases={0: 0, 1: 1},
        scratch=[pltpu.SemaphoreType.DMA((FIELDS,))],
    )(total, partial, near)
    shape = acoustic_state.shape
    return new_state.reshape(shape), source.reshape((3,) + shape[1:])


def solution(mesh):
    in_specs = (
        P(("ax", "az"), None, None),
        P(("ax", "az"), None),
        P(("ax", "az")),
        P(("ax", "az")),
        P(),
        P(None, None, "ax", "az", None),
    )
    out_specs = (P(None, None, "ax", "az", None), P(None, None, "ax", "az", None))
    return jax.shard_map(body, mesh=mesh, in_specs=in_specs, out_specs=out_specs, check_vma=False)
```

```python
import functools
import math

import jax
import jax.numpy as jnp
import numpy as np
from jax import lax
from jax.experimental import pallas as pl
from jax.experimental.pallas import tpu as pltpu
from jax.sharding import PartitionSpec as P

MACH = 0.3
RUSANOV = 1.3
DT = 0.03
LIFT = 10.0
VOLUME = 2.0
STEP_SCALES = (DT, DT / 2.0, DT / 3.0, DT / 4.0)

FIELDS = 5
NODES = 125
ROWS = 8
LANES = 128
VMEM_BYTES = 24 * 1024 * 1024


def derivative_matrix():
    points = np.array([-1.0, -math.sqrt(3.0 / 7.0), 0.0, math.sqrt(3.0 / 7.0), 1.0])
    weights = [1.0 / np.prod([points[j] - points[k] for k in range(5) if k != j]) for j in range(5)]
    matrix = np.zeros((5, 5))
    for i in range(5):
        for j in range(5):
            if i != j:
                matrix[i, j] = weights[j] / weights[i] / (points[i] - points[j])
        matrix[i, i] = -np.sum(matrix[i])
    return matrix


DERIVATIVE = -VOLUME * derivative_matrix()


def differentiate(g, scale):
    d = [[float(scale * v) for v in row] for row in DERIVATIVE]
    even_out, odd_out = g[0] - g[4], g[1] - g[3]
    s_out, s_in = g[0] + g[4], g[1] + g[3]
    results = [None] * 5
    for i in (0, 1):
        same = (d[i][0] - d[i][4]) / 2 * even_out + (d[i][1] - d[i][3]) / 2 * odd_out
        flip = (d[i][0] + d[i][4]) / 2 * s_out + (d[i][1] + d[i][3]) / 2 * s_in + d[i][2] * g[2]
        results[i] = same + flip
        results[4 - i] = same - flip
    results[2] = d[2][0] * even_out + d[2][1] * odd_out
    return results


def flux(q, direction):
    g, u, v, w, e = q
    if direction == 0:
        return [(2.0 * MACH) * g + (1.0 - MACH**2) * u, g, None, None, MACH * e]
    if direction == 1:
        return [v, None, g, None, None]
    return [w, None, None, g, None]


def original(q):
    g, u, v, w, e = q
    p = g - MACH * u
    return [p, u, v, w, e + p]


def lifted(q, direction, normal, rusanov_sign):
    result = []
    for value, flow in zip(q, flux(q, direction)):
        term = (LIFT * RUSANOV * rusanov_sign) * value
        if flow is not None:
            term = term + (LIFT * normal) * flow
        result.append(term)
    return result


def coupled(jump, direction, normal, scale):
    g, u, v, w, e = jump
    rusanov, lift = scale * LIFT * RUSANOV, scale * LIFT * normal
    if direction == 0:
        return [
            (2.0 * MACH * lift - rusanov) * g + ((1.0 - MACH**2) * lift) * u,
            lift * g - rusanov * u,
            -rusanov * v,
            -rusanov * w,
            (MACH * lift - rusanov) * e,
        ]
    normal_velocity = (v, w)[direction - 1]
    along = lift * g - rusanov * normal_velocity
    return [
        lift * normal_velocity - rusanov * g,
        -rusanov * u,
        along if direction == 1 else -rusanov * v,
        along if direction == 2 else -rusanov * w,
        -rusanov * e,
    ]


def shifted(q, amount, axis, keep):
    return [jnp.where(keep, pltpu.roll(value, amount, axis), 0.0) for value in q]


def volume_into(state_ref, scale, store):
    row = lax.broadcasted_iota(jnp.int32, (ROWS, LANES), 0)
    lane = lax.broadcasted_iota(jnp.int32, (ROWS, LANES), 1)
    cell = row % 4
    keep = {
        0: (row >= 4, row < 4),
        1: (cell != 0, cell != 3),
        2: (lane != 0, lane != LANES - 1),
    }
    rolls = {0: (4, 4, 0), 1: (1, ROWS - 1, 0), 2: (1, LANES - 1, 1)}

    def load(field, node):
        return state_ref[field * NODES + node]

    def face_terms(direction, low, high):
        up, down, axis = rolls[direction]
        keep_low, keep_high = keep[direction]
        if direction == 0:
            turned = [pltpu.roll(jnp.where(keep_high, b, a), up, axis) for a, b in zip(low, high)]
            below = [jnp.where(keep_low, value, 0.0) for value in turned]
            above = [jnp.where(keep_high, value, 0.0) for value in turned]
        else:
            below = shifted(high, up, axis, keep_low)
            above = shifted(low, down, axis, keep_high)
        jump_low = [a - b for a, b in zip(low, below)]
        jump_high = [a - b for a, b in zip(high, above)]
        return coupled(jump_low, direction, -1.0, scale), coupled(jump_high, direction, 1.0, scale)

    def line(direction, nodes):
        q = [[load(f, n) for n in nodes] for f in range(FIELDS)]
        ends = face_terms(direction, [x[0] for x in q], [x[4] for x in q])
        g, u, e = q[0], q[1], q[4]
        if direction == 0:
            mixed = [(2.0 * MACH) * g[k] + (1.0 - MACH**2) * u[k] for k in range(5)]
            parts = {
                0: differentiate(mixed, scale),
                1: differentiate(g, scale),
                4: differentiate(e, scale * MACH),
            }
        else:
            parts = {
                0: differentiate(q[direction + 1], scale),
                direction + 1: differentiate(g, scale),
            }
        values = []
        for f in range(FIELDS):
            row = list(parts[f]) if f in parts else [None] * 5
            for k, end in ((0, ends[0][f]), (4, ends[1][f])):
                row[k] = end if row[k] is None else row[k] + end
            values.append(row)
        store(direction, nodes, values, q)

    @pl.loop(0, 5)
    def _(outer):
        for inner in range(5):
            line(0, [k * 25 + outer * 5 + inner for k in range(5)])

    @pl.loop(0, 5)
    def _(outer):
        for inner in range(5):
            line(1, [outer * 25 + k * 5 + inner for k in range(5)])

    @pl.loop(0, 5)
    def _(outer):
        for inner in range(5):
            line(2, [outer * 25 + inner * 5 + k for k in range(5)])


def volume_first_kernel(scale, state_ref, out_ref):
    volume_into(state_ref, scale, add_to(out_ref))


def add_to(out_ref):
    def store(direction, nodes, values, q):
        for f in range(FIELDS):
            for node, value in zip(nodes, values[f]):
                at = f * NODES + node
                if direction == 0:
                    out_ref[at] = jnp.zeros_like(q[0][0]) if value is None else value
                elif value is not None:
                    out_ref[at] += value

    return store


def volume_kernel(scale, state_ref, sum_in, out_ref, sum_ref):
    add = add_to(out_ref)

    def store(direction, nodes, values, q):
        add(direction, nodes, values, q)
        if direction == 2:
            for f in range(FIELDS):
                for node, value in zip(nodes, q[f]):
                    at = f * NODES + node
                    sum_ref[at] = sum_in[at] + value

    volume_into(state_ref, scale, store)


def volume_and_source_kernel(
    scale, state_ref, sum_in, source_ref, out_ref, sum_ref, out_hbm, sem
):
    copy = pltpu.make_async_copy(source_ref, out_hbm, sem.at[0])
    copy.start()
    volume_kernel(scale, state_ref, sum_in, out_ref, sum_ref)
    copy.wait()


def volume_last_kernel(scale, state_ref, sum_in, sum_ref, out_ref):
    add = add_to(out_ref)

    def store(direction, nodes, values, q):
        if direction < 2:
            add(direction, nodes, values, q)
            return
        for k, node in enumerate(nodes):
            totals = []
            for f in range(FIELDS):
                at = f * NODES + node
                total = sum_in[at] + q[f][k] + out_ref[at]
                totals.append(total if values[f][k] is None else total + values[f][k])
            for f, total in enumerate(original(totals)):
                sum_ref[f * NODES + node] = total

    volume_into(state_ref, scale, store)


def on_parity(axis, even, odd):
    parity = lax.axis_index(axis) % 2
    pl.when(parity == 0)(even)
    pl.when(parity == 1)(odd)


def received(ref, start):
    return [ref[pl.ds(f * 25 + start, 5)].astype(jnp.float32) for f in range(FIELDS)]


def add_ax(out_ref, face, high, weight, final):
    sign = -weight if high else weight
    first, rows = (100, slice(4, 8)) if high else (0, slice(0, 4))
    for chunk in range(5):
        terms = lifted(received(face, chunk * 5), 0, sign, weight)
        terms = original(terms) if final else terms
        for f, term in enumerate(terms):
            out_ref[pl.ds(f * NODES + first + chunk * 5, 5), rows, :] += term


def add_far(out_ref, face, weight, final=False):
    on_parity(
        "ax",
        lambda: add_ax(out_ref, face, False, weight, final),
        lambda: add_ax(out_ref, face, True, weight, final),
    )


def add_near(out_ref, face, weight, final=False):
    on_parity(
        "ax",
        lambda: add_ax(out_ref, face, True, weight, final),
        lambda: add_ax(out_ref, face, False, weight, final),
    )


def add_az(out_ref, far, near, weight, final=False):
    row = lax.broadcasted_iota(jnp.int32, (5, ROWS, LANES), 1)

    def add_side(face, at, rows, chunk, sign):
        terms = lifted(received(face, chunk), 1, sign, weight)
        for f, term in enumerate(original(terms) if final else terms):
            spread = jnp.where(row == rows[1], term[:, 1:2], 0.0)
            out_ref[pl.ds(f * NODES + at, 5)] += jnp.where(row == rows[0], term[:, 0:1], spread)

    def add(low, high):
        for a in range(5):
            add_side(low, a * 25, (0, 4), a * 5, weight)
            add_side(high, a * 25 + 20, (3, 7), a * 5, -weight)

    on_parity("az", lambda: add(far, near), lambda: add(near, far))


def pack_ax(state_ref, face, high):
    first, rows = (100, slice(4, 8)) if high else (0, slice(0, 4))
    for f in range(FIELDS):
        face[pl.ds(f * 25, 25)] = state_ref[pl.ds(f * NODES + first, 25), rows, :].astype(
            jnp.bfloat16
        )


def pack_far(state_ref, face):
    on_parity("ax", lambda: pack_ax(state_ref, face, False), lambda: pack_ax(state_ref, face, True))


def pack_near(state_ref, face):
    on_parity("ax", lambda: pack_ax(state_ref, face, True), lambda: pack_ax(state_ref, face, False))


def pack_az(state_ref, far, near):
    def pack(az_low, az_high):
        for f in range(FIELDS):
            for a in range(5):
                at, to = f * NODES + a * 25, pl.ds((f * 5 + a) * 5, 5)
                low = [state_ref[pl.ds(at, 5), k : k + 1, :] for k in (0, 4)]
                high = [state_ref[pl.ds(at + 20, 5), k : k + 1, :] for k in (3, 7)]
                az_low[to] = jnp.concatenate(low, axis=1).astype(jnp.bfloat16)
                az_high[to] = jnp.concatenate(high, axis=1).astype(jnp.bfloat16)

    on_parity("az", lambda: pack(far, near), lambda: pack(near, far))


def load_kernel(state_hbm, state_ref, far, near, az_far, az_near, sems):
    copies = []
    for f in range(FIELDS):
        nodes = pl.ds(f * NODES, NODES)
        copy = pltpu.make_async_copy(state_hbm.at[nodes], state_ref.at[nodes], sems.at[f])
        copy.start()
        copies.append(copy)
    for copy in copies:
        copy.wait()

    @pl.loop(0, NODES // 5)
    def _(chunk):
        for k in range(5):
            node = chunk * 5 + k
            p = state_ref[node]
            state_ref[node] = p + MACH * state_ref[NODES + node]
            state_ref[4 * NODES + node] -= p

    pack_faces(state_ref, far, near, az_far, az_near)


def pack_faces(state_ref, far, near, az_far, az_near):
    pack_far(state_ref, far)
    pack_near(state_ref, near)
    pack_az(state_ref, az_far, az_near)


def add_source(state_ref, source_ref, scale, nodes):
    for node in nodes:
        for c in range(3):
            value = scale * source_ref[pl.ds((c * NODES + node) * ROWS, ROWS), :]
            state_ref[(c + 1) * NODES + node] += value
            if c == 0:
                state_ref[node] += MACH * value


def first_far_kernel(scale, state_in, source_ref, far, az_far, az_near, state_ref, far_out):
    add_az(state_ref, az_far, az_near, scale)
    add_far(state_ref, far, scale)
    add_source(state_ref, source_ref, scale, [*range(25), *range(100, NODES)])
    pack_far(state_ref, far_out)


def first_near_kernel(scale, state_in, source_ref, near, state_ref, near_out, *az_out):
    add_near(state_ref, near, scale)
    add_source(state_ref, source_ref, scale, range(25, 100))
    pack_near(state_ref, near_out)
    pack_az(state_ref, *az_out)


def finish_far_kernel(scale, state_in, far, az_far, az_near, state_ref, far_out):
    add_az(state_ref, az_far, az_near, scale)
    add_far(state_ref, far, scale)
    pack_far(state_ref, far_out)


def finish_near_kernel(scale, state_in, near, state_ref, near_out, az_far_out, az_near_out):
    add_near(state_ref, near, scale)
    pack_near(state_ref, near_out)
    pack_az(state_ref, az_far_out, az_near_out)


def last_far_kernel(weight, state_in, far, az_far, az_near, state_ref, out_hbm, sems):
    add_az(state_ref, az_far, az_near, weight, final=True)
    add_far(state_ref, far, weight, final=True)
    first = 25 * (lax.axis_index("ax") % 2)
    copies = []
    for f in range(FIELDS):
        nodes = pl.ds(f * NODES + first, NODES - 25)
        copy = pltpu.make_async_copy(state_ref.at[nodes], out_hbm.at[nodes], sems.at[f])
        copy.start()
        copies.append(copy)
    for copy in copies:
        copy.wait()


def last_near_kernel(weight, state_in, out_in, near, state_ref, out_hbm, sems):
    add_near(state_ref, near, weight, final=True)
    first = 100 - 100 * (lax.axis_index("ax") % 2)
    copies = []
    for f in range(FIELDS):
        nodes = pl.ds(f * NODES + first, 25)
        copy = pltpu.make_async_copy(state_ref.at[nodes], out_hbm.at[nodes], sems.at[f])
        copy.start()
        copies.append(copy)
    for copy in copies:
        copy.wait()


def contribution_kernel(
    capacity,
    devices,
    lamb_hbm,
    owner_hbm,
    element_hbm,
    class_hbm,
    tables_hbm,
    out_hbm,
    lamb_ref,
    owner_ref,
    rows_ref,
    tables_ref,
    out_ref,
    row_sems,
    tables_sem,
    lamb_sem,
    out_sems,
):
    flow = lamb_ref.shape[1]
    slots = devices * capacity
    row_copies = [
        pltpu.make_async_copy(owner_hbm, owner_ref, row_sems.at[0]),
        pltpu.make_async_copy(element_hbm, rows_ref.at[0], row_sems.at[1]),
        pltpu.make_async_copy(class_hbm, rows_ref.at[1], row_sems.at[2]),
    ]
    lamb_copy = pltpu.make_async_copy(lamb_hbm, lamb_ref, lamb_sem.at[0])
    tables_copy = pltpu.make_async_copy(tables_hbm, tables_ref, tables_sem.at[0])
    for copy in row_copies + [tables_copy, lamb_copy]:
        copy.start()
    for copy in row_copies + [tables_copy, lamb_copy]:
        copy.wait()

    owner_row = owner_ref[...]
    rows = jnp.concatenate(
        [rows_ref[0], rows_ref[1], jnp.zeros((ROWS - 2, flow), jnp.int32)], axis=0
    )
    columns = jnp.transpose(rows.astype(jnp.float32))
    element = columns[:, 0:1]
    second = columns[:, 1:2]

    owned = (lax.broadcasted_iota(jnp.int32, (devices, flow), 0) == owner_row).astype(jnp.float32)
    earlier = lax.broadcasted_iota(jnp.int32, (flow, flow), 0) < lax.broadcasted_iota(
        jnp.int32, (flow, flow), 1
    )
    running = jnp.dot(
        owned.astype(jnp.bfloat16),
        earlier.astype(jnp.bfloat16),
        preferred_element_type=jnp.float32,
    )
    position = jnp.sum(running * owned, axis=0, keepdims=True).astype(jnp.int32)
    slot_row = owner_row * capacity + position
    placing = (lax.broadcasted_iota(jnp.int32, (slots, flow), 0) == slot_row).astype(jnp.bfloat16)

    spare = jnp.zeros((LANES - NODES, lamb_ref.shape[2]), jnp.bfloat16)
    tables = jnp.concatenate([tables_ref[:, 0, :], spare, tables_ref[:, 1, :], spare], axis=0)
    both = lax.dot_general(
        lamb_ref[...].reshape(3 * flow, lamb_ref.shape[2]),
        tables,
        (((1,), (1,)), ((), ())),
        preferred_element_type=jnp.float32,
    )
    use_second = jnp.broadcast_to(second, (flow, LANES)) > 0.5
    values = [
        jnp.where(
            use_second, both[c * flow : (c + 1) * flow, LANES:], both[c * flow : (c + 1) * flow, :LANES]
        )
        for c in range(3)
    ]
    largest = jnp.maximum(jnp.maximum(jnp.abs(values[0]), jnp.abs(values[1])), jnp.abs(values[2]))
    largest = jnp.max(largest, axis=1, keepdims=True)
    exponent = jnp.clip(jnp.ceil(jnp.log2(jnp.maximum(largest, 1e-36))), -100.0, 30.0)
    scale = jnp.broadcast_to(jnp.exp2(14.0 - exponent), (flow, LANES))
    column = lax.broadcasted_iota(jnp.int32, (flow, LANES), 1)
    out_copies = []
    for c in range(3):
        whole = jnp.round(values[c] * scale)
        if c == 0:
            whole = jnp.where(column == NODES, exponent, whole)
            whole = jnp.where(column == NODES + 1, element, whole)
        high = jnp.floor(whole * (1.0 / 256.0))
        low = whole - 256.0 * high
        pieces = jnp.concatenate([high, low], axis=1).astype(jnp.bfloat16)
        placed = jnp.dot(placing, pieces, preferred_element_type=jnp.float32)
        placed = placed[:, :LANES] * 256.0 + placed[:, LANES:]
        out_ref[c] = placed.astype(jnp.int32).astype(jnp.int16)
        copy = pltpu.make_async_copy(
            out_ref.at[c], out_hbm.at[:, pl.ds(c * LANES, LANES)], out_sems.at[c]
        )
        copy.start()
        out_copies.append(copy)
    for copy in out_copies:
        copy.wait()


def source_kernel(received_ref, source_ref):
    slots = received_ref.shape[0]
    wide = 2 * LANES
    highs, lows = [], []
    for c in range(3):
        values = received_ref[:, pl.ds(c * LANES, LANES)].astype(jnp.int32).astype(jnp.float32)
        if c == 0:
            element = values[:, NODES + 1 : NODES + 2].astype(jnp.int32)
        values = jnp.transpose(values)
        if c == 0:
            scale = jnp.exp2(values[NODES : NODES + 1, :] - 14.0)
        values = values * scale
        high = values.astype(jnp.bfloat16)
        highs.append(high)
        lows.append((values - high.astype(jnp.float32)).astype(jnp.bfloat16))
    parts = jnp.concatenate(highs + lows, axis=0)
    column = lax.broadcasted_iota(jnp.int32, (slots, wide), 1)
    for group in range(ROWS // 2):
        member = (element == column + group * wide).astype(jnp.bfloat16)
        total = jnp.dot(parts, member, preferred_element_type=jnp.float32)
        total = total[0 : 3 * LANES] + total[3 * LANES :]
        for c in range(3):
            for k in range(2):
                start = c * NODES * ROWS + group * 2 + k
                source_ref[pl.ds(start, NODES, stride=ROWS), :] = total[
                    c * LANES : c * LANES + NODES, k * LANES : (k + 1) * LANES
                ]

STATE = (FIELDS * NODES, ROWS, LANES)
AX_FACE = (FIELDS * 25, 4, LANES)
AZ_FACE = (FIELDS * 25, 2, LANES)


LONG = pl.CostEstimate(flops=10**11, bytes_accessed=10**9, transcendentals=0)
IN_VMEM = pl.BlockSpec(memory_space=pltpu.VMEM)
IN_HBM = pl.BlockSpec(memory_space=pltpu.HBM)


def in_hbm(x):
    return pltpu.with_memory_space_constraint(x, pltpu.HBM)


def call(kernel, out_shape, in_specs, out_specs=IN_VMEM, aliases=None, scratch=(), cost=None):
    if not isinstance(out_specs, list):
        out_specs = jax.tree.map(lambda _: out_specs, out_shape)
    return pl.pallas_call(
        kernel,
        out_shape=out_shape,
        in_specs=in_specs if isinstance(in_specs, list) else [IN_VMEM] * in_specs,
        out_specs=out_specs,
        scratch_shapes=scratch,
        input_output_aliases=aliases or {},
        cost_estimate=cost,
        compiler_params=pltpu.CompilerParams(vmem_limit_bytes=VMEM_BYTES),
    )


def swap(far, near):
    count = lax.axis_size("ax")
    pairs = ([], [])
    for i in range(count - 1):
        pairs[i % 2].extend([(i, i + 1), (i + 1, i)])
    return (
        None if far is None else lax.ppermute(far, "ax", pairs[1]),
        None if near is None else lax.ppermute(near, "ax", pairs[0]),
    )


def turn(far, near):
    count = lax.axis_size("az")
    pairs = ([], [])
    for i in range(count):
        pairs[i % 2].extend([(i, (i + 1) % count), ((i + 1) % count, i)])
    return lax.ppermute(far, "az", pairs[1]), lax.ppermute(near, "az", pairs[0])


def body(lamb_vector, owner, element, shape_class, interp_tables, acoustic_state):
    devices = lax.axis_size("ax") * lax.axis_size("az")
    flow, _, points = lamb_vector.shape
    capacity = max(2, 3 * flow // devices)
    slots = devices * capacity
    f32, bf16 = jnp.float32, jnp.bfloat16

    state = acoustic_state.reshape(STATE)
    face_shapes = [jax.ShapeDtypeStruct(s, bf16) for s in (AX_FACE, AX_FACE, AZ_FACE, AZ_FACE)]
    vmem_state = pltpu.VMEM(STATE, f32)
    source_shape = (3 * NODES * ROWS, LANES)

    buffer = call(
        functools.partial(contribution_kernel, capacity, devices),
        pltpu.HBM((slots, 3 * LANES), jnp.int16),
        [IN_HBM] * 5,
        IN_HBM,
        scratch=[
            pltpu.VMEM((3, flow, points), bf16),
            pltpu.VMEM((1, flow), jnp.int32),
            pltpu.VMEM((2, 1, flow), jnp.int32),
            pltpu.VMEM((NODES, 2, points), bf16),
            pltpu.VMEM((3, slots, LANES), jnp.int16),
            pltpu.SemaphoreType.DMA((3,)),
            pltpu.SemaphoreType.DMA((1,)),
            pltpu.SemaphoreType.DMA((1,)),
            pltpu.SemaphoreType.DMA((3,)),
        ],
    )(
        in_hbm(jnp.transpose(lamb_vector, (1, 0, 2))),
        in_hbm(owner.reshape(1, flow)),
        in_hbm(element.reshape(1, flow)),
        in_hbm(shape_class.reshape(1, flow)),
        in_hbm(jnp.transpose(interp_tables, (2, 0, 1))),
    )
    routed = lax.all_to_all(buffer, ("ax", "az"), split_axis=0, concat_axis=0, tiled=True)

    state, far, near, az_far, az_near = call(
        load_kernel,
        [vmem_state] + face_shapes,
        [IN_HBM],
        scratch=[pltpu.SemaphoreType.DMA((FIELDS,))],
    )(in_hbm(state))
    far, near = swap(far, near)
    az_far, az_near = turn(az_far, az_near)
    moved = call(functools.partial(volume_first_kernel, STEP_SCALES[0]), vmem_state, 1)(state)
    source = call(source_kernel, pltpu.VMEM(source_shape, f32), 1)(routed)
    rate, far = call(
        functools.partial(first_far_kernel, STEP_SCALES[0]),
        [vmem_state, face_shapes[0]],
        5,
        aliases={0: 0},
    )(moved, source, far, az_far, az_near)
    far, _ = swap(far, None)
    rate, near, az_far, az_near = call(
        functools.partial(first_near_kernel, STEP_SCALES[0]),
        [vmem_state] + face_shapes[1:],
        3,
        aliases={0: 0},
    )(rate, source, near)
    _, near = swap(None, near)
    az_far, az_near = turn(az_far, az_near)
    moved, total, source = call(
        functools.partial(volume_and_source_kernel, STEP_SCALES[1]),
        [vmem_state, vmem_state, pltpu.HBM(source_shape, f32)],
        3,
        [IN_VMEM, IN_VMEM, IN_HBM],
        scratch=[pltpu.SemaphoreType.DMA((1,))],
    )(rate, state, source)

    for scale in STEP_SCALES[1:3]:
        rate, far = call(
            functools.partial(finish_far_kernel, scale),
            [vmem_state, face_shapes[0]],
            4,
            aliases={0: 0},
            cost=LONG,
        )(moved, far, az_far, az_near)
        far, _ = swap(far, None)
        rate, near, az_far, az_near = call(
            functools.partial(finish_near_kernel, scale),
            [vmem_state] + face_shapes[1:],
            2,
            aliases={0: 0},
        )(rate, near)
        _, near = swap(None, near)
        az_far, az_near = turn(az_far, az_near)
        if scale == STEP_SCALES[1]:
            moved, total = call(
                functools.partial(volume_kernel, STEP_SCALES[2]), [vmem_state, vmem_state], 2
            )(rate, total)

    total = call(
        functools.partial(volume_last_kernel, STEP_SCALES[3]),
        vmem_state,
        2,
        scratch=[pltpu.VMEM(STATE, f32)],
    )(rate, total)
    hbm_state = pltpu.HBM(STATE, f32)
    total, partial = call(
        functools.partial(last_far_kernel, STEP_SCALES[3]),
        [vmem_state, hbm_state],
        4,
        [IN_VMEM, IN_HBM],
        aliases={0: 0},
        cost=LONG,
        scratch=[pltpu.SemaphoreType.DMA((FIELDS,))],
    )(total, far, az_far, az_near)
    _, new_state = call(
        functools.partial(last_near_kernel, STEP_SCALES[3]),
        [vmem_state, hbm_state],
        [IN_VMEM, IN_HBM, IN_VMEM],
        [IN_VMEM, IN_HBM],
        aliases={0: 0, 1: 1},
        scratch=[pltpu.SemaphoreType.DMA((FIELDS,))],
    )(total, partial, near)
    shape = acoustic_state.shape
    return new_state.reshape(shape), source.reshape((3,) + shape[1:])


def solution(mesh):
    in_specs = (
        P(("ax", "az"), None, None),
        P(("ax", "az"), None),
        P(("ax", "az")),
        P(("ax", "az")),
        P(),
        P(None, None, "ax", "az", None),
    )
    out_specs = (P(None, None, "ax", "az", None), P(None, None, "ax", "az", None))
    return jax.shard_map(body, mesh=mesh, in_specs=in_specs, out_specs=out_specs, check_vma=False)
```

```python
import functools
import math

import jax
import jax.numpy as jnp
import numpy as np
from jax import lax
from jax.experimental import pallas as pl
from jax.experimental.pallas import tpu as pltpu
from jax.sharding import PartitionSpec as P

MACH = 0.3
RUSANOV = 1.3
DT = 0.03
LIFT = 10.0
VOLUME = 2.0
STEP_SCALES = (DT, DT / 2.0, DT / 3.0, DT / 4.0)

FIELDS = 5
NODES = 125
ROWS = 8
LANES = 128
VMEM_BYTES = 24 * 1024 * 1024


def derivative_matrix():
    points = np.array([-1.0, -math.sqrt(3.0 / 7.0), 0.0, math.sqrt(3.0 / 7.0), 1.0])
    weights = [1.0 / np.prod([points[j] - points[k] for k in range(5) if k != j]) for j in range(5)]
    matrix = np.zeros((5, 5))
    for i in range(5):
        for j in range(5):
            if i != j:
                matrix[i, j] = weights[j] / weights[i] / (points[i] - points[j])
        matrix[i, i] = -np.sum(matrix[i])
    return matrix


DERIVATIVE = -VOLUME * derivative_matrix()


def differentiate(g, scale):
    d = [[float(scale * v) for v in row] for row in DERIVATIVE]
    even_out, odd_out = g[0] - g[4], g[1] - g[3]
    s_out, s_in = g[0] + g[4], g[1] + g[3]
    results = [None] * 5
    for i in (0, 1):
        same = (d[i][0] - d[i][4]) / 2 * even_out + (d[i][1] - d[i][3]) / 2 * odd_out
        flip = (d[i][0] + d[i][4]) / 2 * s_out + (d[i][1] + d[i][3]) / 2 * s_in + d[i][2] * g[2]
        results[i] = same + flip
        results[4 - i] = same - flip
    results[2] = d[2][0] * even_out + d[2][1] * odd_out
    return results


def flux(q, direction):
    g, u, v, w, e = q
    if direction == 0:
        return [(2.0 * MACH) * g + (1.0 - MACH**2) * u, g, None, None, MACH * e]
    if direction == 1:
        return [v, None, g, None, None]
    return [w, None, None, g, None]


def original(q):
    g, u, v, w, e = q
    p = g - MACH * u
    return [p, u, v, w, e + p]


def lifted(q, direction, normal, rusanov_sign):
    result = []
    for value, flow in zip(q, flux(q, direction)):
        term = (LIFT * RUSANOV * rusanov_sign) * value
        if flow is not None:
            term = term + (LIFT * normal) * flow
        result.append(term)
    return result


def coupled(jump, direction, normal, scale):
    g, u, v, w, e = jump
    rusanov, lift = scale * LIFT * RUSANOV, scale * LIFT * normal
    if direction == 0:
        return [
            (2.0 * MACH * lift - rusanov) * g + ((1.0 - MACH**2) * lift) * u,
            lift * g - rusanov * u,
            -rusanov * v,
            -rusanov * w,
            (MACH * lift - rusanov) * e,
        ]
    normal_velocity = (v, w)[direction - 1]
    along = lift * g - rusanov * normal_velocity
    return [
        lift * normal_velocity - rusanov * g,
        -rusanov * u,
        along if direction == 1 else -rusanov * v,
        along if direction == 2 else -rusanov * w,
        -rusanov * e,
    ]


def shifted(q, amount, axis, keep):
    return [jnp.where(keep, pltpu.roll(value, amount, axis), 0.0) for value in q]


def volume_into(state_ref, scale, store):
    row = lax.broadcasted_iota(jnp.int32, (ROWS, LANES), 0)
    lane = lax.broadcasted_iota(jnp.int32, (ROWS, LANES), 1)
    cell = row % 4
    keep = {
        0: (row >= 4, row < 4),
        1: (cell != 0, cell != 3),
        2: (lane != 0, lane != LANES - 1),
    }
    rolls = {0: (4, 4, 0), 1: (1, ROWS - 1, 0), 2: (1, LANES - 1, 1)}

    def load(field, node):
        return state_ref[field * NODES + node]

    def face_terms(direction, low, high):
        up, down, axis = rolls[direction]
        keep_low, keep_high = keep[direction]
        if direction == 0:
            turned = [pltpu.roll(jnp.where(keep_high, b, a), up, axis) for a, b in zip(low, high)]
            below = [jnp.where(keep_low, value, 0.0) for value in turned]
            above = [jnp.where(keep_high, value, 0.0) for value in turned]
        else:
            below = shifted(high, up, axis, keep_low)
            above = shifted(low, down, axis, keep_high)
        jump_low = [a - b for a, b in zip(low, below)]
        jump_high = [a - b for a, b in zip(high, above)]
        return coupled(jump_low, direction, -1.0, scale), coupled(jump_high, direction, 1.0, scale)

    def line(direction, nodes):
        q = [[load(f, n) for n in nodes] for f in range(FIELDS)]
        ends = face_terms(direction, [x[0] for x in q], [x[4] for x in q])
        g, u, e = q[0], q[1], q[4]
        if direction == 0:
            mixed = [(2.0 * MACH) * g[k] + (1.0 - MACH**2) * u[k] for k in range(5)]
            parts = {
                0: differentiate(mixed, scale),
                1: differentiate(g, scale),
                4: differentiate(e, scale * MACH),
            }
        else:
            parts = {
                0: differentiate(q[direction + 1], scale),
                direction + 1: differentiate(g, scale),
            }
        values = []
        for f in range(FIELDS):
            row = list(parts[f]) if f in parts else [None] * 5
            for k, end in ((0, ends[0][f]), (4, ends[1][f])):
                row[k] = end if row[k] is None else row[k] + end
            values.append(row)
        store(direction, nodes, values, q)

    @pl.loop(0, 5)
    def _(outer):
        for inner in range(5):
            line(0, [k * 25 + outer * 5 + inner for k in range(5)])

    @pl.loop(0, 5)
    def _(outer):
        for inner in range(5):
            line(1, [outer * 25 + k * 5 + inner for k in range(5)])

    @pl.loop(0, 5)
    def _(outer):
        for inner in range(5):
            line(2, [outer * 25 + inner * 5 + k for k in range(5)])


def volume_first_kernel(scale, state_ref, out_ref):
    volume_into(state_ref, scale, add_to(out_ref))


def add_to(out_ref):
    def store(direction, nodes, values, q):
        for f in range(FIELDS):
            for node, value in zip(nodes, values[f]):
                at = f * NODES + node
                if direction == 0:
                    out_ref[at] = jnp.zeros_like(q[0][0]) if value is None else value
                elif value is not None:
                    out_ref[at] += value

    return store


def volume_kernel(scale, state_ref, sum_in, out_ref, sum_ref):
    add = add_to(out_ref)

    def store(direction, nodes, values, q):
        add(direction, nodes, values, q)
        if direction == 2:
            for f in range(FIELDS):
                for node, value in zip(nodes, q[f]):
                    at = f * NODES + node
                    sum_ref[at] = sum_in[at] + value

    volume_into(state_ref, scale, store)


def volume_and_source_kernel(
    scale, state_ref, sum_in, source_ref, out_ref, sum_ref, out_hbm, sem
):
    copy = pltpu.make_async_copy(source_ref, out_hbm, sem.at[0])
    copy.start()
    volume_kernel(scale, state_ref, sum_in, out_ref, sum_ref)
    copy.wait()


def volume_last_kernel(scale, state_ref, sum_in, sum_ref, out_ref):
    add = add_to(out_ref)

    def store(direction, nodes, values, q):
        if direction < 2:
            add(direction, nodes, values, q)
            return
        for k, node in enumerate(nodes):
            totals = []
            for f in range(FIELDS):
                at = f * NODES + node
                total = sum_in[at] + q[f][k] + out_ref[at]
                totals.append(total if values[f][k] is None else total + values[f][k])
            for f, total in enumerate(original(totals)):
                sum_ref[f * NODES + node] = total

    volume_into(state_ref, scale, store)


def on_parity(axis, even, odd):
    parity = lax.axis_index(axis) % 2
    pl.when(parity == 0)(even)
    pl.when(parity == 1)(odd)


def five(ref, f, at):
    return (pl.ds(f * NODES + at, 5),) if len(ref.shape) == 3 else (f, at // 25, pl.ds(at % 25, 5))


def received(ref, start):
    return [ref[pl.ds(f * 25 + start, 5)].astype(jnp.float32) for f in range(FIELDS)]


def add_ax(out_ref, face, high, weight, final):
    sign = -weight if high else weight
    first, rows = (100, slice(4, 8)) if high else (0, slice(0, 4))
    for chunk in range(5):
        terms = lifted(received(face, chunk * 5), 0, sign, weight)
        terms = original(terms) if final else terms
        for f, term in enumerate(terms):
            out_ref[*five(out_ref, f, first + chunk * 5), rows, :] += term


def add_far(out_ref, face, weight, final=False):
    on_parity(
        "ax",
        lambda: add_ax(out_ref, face, False, weight, final),
        lambda: add_ax(out_ref, face, True, weight, final),
    )


def add_near(out_ref, face, weight, final=False):
    on_parity(
        "ax",
        lambda: add_ax(out_ref, face, True, weight, final),
        lambda: add_ax(out_ref, face, False, weight, final),
    )


def add_az(out_ref, far, near, weight, final=False):
    row = lax.broadcasted_iota(jnp.int32, (5, ROWS, LANES), 1)

    def add_side(face, at, rows, chunk, sign):
        terms = lifted(received(face, chunk), 1, sign, weight)
        for f, term in enumerate(original(terms) if final else terms):
            spread = jnp.where(row == rows[1], term[:, 1:2], 0.0)
            out_ref[*five(out_ref, f, at)] += jnp.where(row == rows[0], term[:, 0:1], spread)

    def add(low, high):
        for a in range(5):
            add_side(low, a * 25, (0, 4), a * 5, weight)
            add_side(high, a * 25 + 20, (3, 7), a * 5, -weight)

    on_parity("az", lambda: add(far, near), lambda: add(near, far))


def pack_ax(state_ref, face, high):
    first, rows = (100, slice(4, 8)) if high else (0, slice(0, 4))
    for f in range(FIELDS):
        face[pl.ds(f * 25, 25)] = state_ref[pl.ds(f * NODES + first, 25), rows, :].astype(
            jnp.bfloat16
        )


def pack_far(state_ref, face):
    on_parity("ax", lambda: pack_ax(state_ref, face, False), lambda: pack_ax(state_ref, face, True))


def pack_near(state_ref, face):
    on_parity("ax", lambda: pack_ax(state_ref, face, True), lambda: pack_ax(state_ref, face, False))


def pack_az(state_ref, far, near):
    def pack(az_low, az_high):
        for f in range(FIELDS):
            for a in range(5):
                at, to = f * NODES + a * 25, pl.ds((f * 5 + a) * 5, 5)
                low = [state_ref[pl.ds(at, 5), k : k + 1, :] for k in (0, 4)]
                high = [state_ref[pl.ds(at + 20, 5), k : k + 1, :] for k in (3, 7)]
                az_low[to] = jnp.concatenate(low, axis=1).astype(jnp.bfloat16)
                az_high[to] = jnp.concatenate(high, axis=1).astype(jnp.bfloat16)

    on_parity("az", lambda: pack(far, near), lambda: pack(near, far))


def load_kernel(state_hbm, state_ref, far, near, az_far, az_near, sems):
    copies = []
    for f in range(FIELDS):
        nodes = pl.ds(f * NODES, NODES)
        copy = pltpu.make_async_copy(state_hbm.at[nodes], state_ref.at[nodes], sems.at[f])
        copy.start()
        copies.append(copy)
    for copy in copies:
        copy.wait()

    @pl.loop(0, NODES // 5)
    def _(chunk):
        for k in range(5):
            node = chunk * 5 + k
            p = state_ref[node]
            state_ref[node] = p + MACH * state_ref[NODES + node]
            state_ref[4 * NODES + node] -= p

    pack_faces(state_ref, far, near, az_far, az_near)


def pack_faces(state_ref, far, near, az_far, az_near):
    pack_far(state_ref, far)
    pack_near(state_ref, near)
    pack_az(state_ref, az_far, az_near)


def add_source(state_ref, source_ref, scale, nodes):
    for node in nodes:
        for c in range(3):
            value = scale * source_ref[pl.ds((c * NODES + node) * ROWS, ROWS), :]
            state_ref[(c + 1) * NODES + node] += value
            if c == 0:
                state_ref[node] += MACH * value


def first_far_kernel(scale, state_in, source_ref, far, az_far, az_near, state_ref, far_out):
    add_az(state_ref, az_far, az_near, scale)
    add_far(state_ref, far, scale)
    add_source(state_ref, source_ref, scale, [*range(25), *range(100, NODES)])
    pack_far(state_ref, far_out)


def first_near_kernel(scale, state_in, source_ref, near, state_ref, near_out, *az_out):
    add_near(state_ref, near, scale)
    add_source(state_ref, source_ref, scale, range(25, 100))
    pack_near(state_ref, near_out)
    pack_az(state_ref, *az_out)


def finish_far_kernel(scale, state_in, far, az_far, az_near, state_ref, far_out):
    add_az(state_ref, az_far, az_near, scale)
    add_far(state_ref, far, scale)
    pack_far(state_ref, far_out)


def finish_near_kernel(scale, state_in, near, state_ref, near_out, az_far_out, az_near_out):
    add_near(state_ref, near, scale)
    pack_near(state_ref, near_out)
    pack_az(state_ref, az_far_out, az_near_out)


def last_far_kernel(weight, state_in, far, az_far, az_near, state_ref, out_hbm, sems):
    far_plane = 4 * (lax.axis_index("ax") % 2)

    def copy(k, plane, nodes):
        part = (slice(None), plane, nodes)
        return pltpu.make_async_copy(state_ref.at[*part], out_hbm.at[*part], sems.at[k])

    inside = [copy(k, plane, pl.ds(5, 15)) for k, plane in enumerate((1, 2, 3))]
    for part in inside:
        part.start()
    add_az(state_ref, az_far, az_near, weight, final=True)
    add_far(state_ref, far, weight, final=True)
    outside = [copy(3, far_plane, pl.ds(0, 25))]
    outside += [copy(4 + k, k + 1, pl.ds(0, 5)) for k in range(3)]
    outside += [copy(7 + k, k + 1, pl.ds(20, 5)) for k in range(3)]
    for part in outside:
        part.start()
    for part in inside + outside:
        part.wait()


def last_near_kernel(weight, state_in, out_in, near, state_ref, out_hbm, sem):
    add_near(state_ref, near, weight, final=True)
    part = (slice(None), 4 - 4 * (lax.axis_index("ax") % 2))
    copy = pltpu.make_async_copy(state_ref.at[*part], out_hbm.at[*part], sem.at[0])
    copy.start()
    copy.wait()


def contribution_kernel(
    capacity,
    devices,
    lamb_hbm,
    owner_hbm,
    element_hbm,
    class_hbm,
    tables_hbm,
    out_hbm,
    lamb_ref,
    owner_ref,
    rows_ref,
    tables_ref,
    out_ref,
    row_sems,
    tables_sem,
    lamb_sem,
    out_sems,
):
    flow = lamb_ref.shape[1]
    slots = devices * capacity
    row_copies = [
        pltpu.make_async_copy(owner_hbm, owner_ref, row_sems.at[0]),
        pltpu.make_async_copy(element_hbm, rows_ref.at[0], row_sems.at[1]),
        pltpu.make_async_copy(class_hbm, rows_ref.at[1], row_sems.at[2]),
    ]
    lamb_copy = pltpu.make_async_copy(lamb_hbm, lamb_ref, lamb_sem.at[0])
    tables_copy = pltpu.make_async_copy(tables_hbm, tables_ref, tables_sem.at[0])
    for copy in row_copies + [tables_copy, lamb_copy]:
        copy.start()
    for copy in row_copies:
        copy.wait()

    owner_row = owner_ref[...]
    rows = jnp.concatenate(
        [rows_ref[0], rows_ref[1], jnp.zeros((ROWS - 2, flow), jnp.int32)], axis=0
    )
    columns = jnp.transpose(rows.astype(jnp.float32))
    element = columns[:, 0:1]
    second = columns[:, 1:2]

    owned = (lax.broadcasted_iota(jnp.int32, (devices, flow), 0) == owner_row).astype(jnp.float32)
    earlier = lax.broadcasted_iota(jnp.int32, (flow, flow), 0) < lax.broadcasted_iota(
        jnp.int32, (flow, flow), 1
    )
    running = jnp.dot(
        owned.astype(jnp.bfloat16),
        earlier.astype(jnp.bfloat16),
        preferred_element_type=jnp.float32,
    )
    position = jnp.sum(running * owned, axis=0, keepdims=True).astype(jnp.int32)
    slot_row = owner_row * capacity + position
    placing = (lax.broadcasted_iota(jnp.int32, (slots, flow), 0) == slot_row).astype(jnp.bfloat16)

    tables_copy.wait()
    spare = jnp.zeros((LANES - NODES, lamb_ref.shape[2]), jnp.bfloat16)
    tables = jnp.concatenate([tables_ref[:, 0, :], spare, tables_ref[:, 1, :], spare], axis=0)
    lamb_copy.wait()
    both = lax.dot_general(
        lamb_ref[...].reshape(3 * flow, lamb_ref.shape[2]),
        tables,
        (((1,), (1,)), ((), ())),
        preferred_element_type=jnp.float32,
    )
    use_second = jnp.broadcast_to(second, (flow, LANES)) > 0.5
    values = [
        jnp.where(
            use_second, both[c * flow : (c + 1) * flow, LANES:], both[c * flow : (c + 1) * flow, :LANES]
        )
        for c in range(3)
    ]
    largest = jnp.maximum(jnp.maximum(jnp.abs(values[0]), jnp.abs(values[1])), jnp.abs(values[2]))
    largest = jnp.max(largest, axis=1, keepdims=True)
    exponent = jnp.clip(jnp.ceil(jnp.log2(jnp.maximum(largest, 1e-36))), -100.0, 30.0)
    scale = jnp.broadcast_to(jnp.exp2(14.0 - exponent), (flow, LANES))
    column = lax.broadcasted_iota(jnp.int32, (flow, LANES), 1)
    out_copies = []
    for c in range(3):
        whole = jnp.round(values[c] * scale)
        if c == 0:
            whole = jnp.where(column == NODES, exponent, whole)
            whole = jnp.where(column == NODES + 1, element, whole)
        high = jnp.floor(whole * (1.0 / 256.0))
        low = whole - 256.0 * high
        pieces = jnp.concatenate([high, low], axis=1).astype(jnp.bfloat16)
        placed = jnp.dot(placing, pieces, preferred_element_type=jnp.float32)
        placed = placed[:, :LANES] * 256.0 + placed[:, LANES:]
        out_ref[c] = placed.astype(jnp.int32).astype(jnp.int16)
        copy = pltpu.make_async_copy(
            out_ref.at[c], out_hbm.at[:, pl.ds(c * LANES, LANES)], out_sems.at[c]
        )
        copy.start()
        out_copies.append(copy)
    for copy in out_copies:
        copy.wait()


def source_kernel(received_ref, source_ref):
    slots = received_ref.shape[0]
    wide = 2 * LANES
    highs, lows = [], []
    for c in range(3):
        values = received_ref[:, pl.ds(c * LANES, LANES)].astype(jnp.int32).astype(jnp.float32)
        if c == 0:
            element = values[:, NODES + 1 : NODES + 2].astype(jnp.int32)
        values = jnp.transpose(values)
        if c == 0:
            scale = jnp.exp2(values[NODES : NODES + 1, :] - 14.0)
        values = values * scale
        high = values.astype(jnp.bfloat16)
        highs.append(high)
        lows.append((values - high.astype(jnp.float32)).astype(jnp.bfloat16))
    parts = jnp.concatenate(highs + lows, axis=0)
    column = lax.broadcasted_iota(jnp.int32, (slots, wide), 1)
    for group in range(ROWS // 2):
        member = (element == column + group * wide).astype(jnp.bfloat16)
        total = jnp.dot(parts, member, preferred_element_type=jnp.float32)
        total = total[0 : 3 * LANES] + total[3 * LANES :]
        for c in range(3):
            for k in range(2):
                start = c * NODES * ROWS + group * 2 + k
                source_ref[pl.ds(start, NODES, stride=ROWS), :] = total[
                    c * LANES : c * LANES + NODES, k * LANES : (k + 1) * LANES
                ]

STATE = (FIELDS * NODES, ROWS, LANES)
AX_FACE = (FIELDS * 25, 4, LANES)
AZ_FACE = (FIELDS * 25, 2, LANES)


LONG = pl.CostEstimate(flops=10**11, bytes_accessed=10**9, transcendentals=0)
IN_VMEM = pl.BlockSpec(memory_space=pltpu.VMEM)
IN_HBM = pl.BlockSpec(memory_space=pltpu.HBM)


def in_hbm(x):
    return pltpu.with_memory_space_constraint(x, pltpu.HBM)


def call(kernel, out_shape, in_specs, out_specs=IN_VMEM, aliases=None, scratch=(), cost=None):
    if not isinstance(out_specs, list):
        out_specs = jax.tree.map(lambda _: out_specs, out_shape)
    return pl.pallas_call(
        kernel,
        out_shape=out_shape,
        in_specs=in_specs if isinstance(in_specs, list) else [IN_VMEM] * in_specs,
        out_specs=out_specs,
        scratch_shapes=scratch,
        input_output_aliases=aliases or {},
        cost_estimate=cost,
        compiler_params=pltpu.CompilerParams(vmem_limit_bytes=VMEM_BYTES),
    )


def swap(far, near):
    count = lax.axis_size("ax")
    pairs = ([], [])
    for i in range(count - 1):
        pairs[i % 2].extend([(i, i + 1), (i + 1, i)])
    return (
        None if far is None else lax.ppermute(far, "ax", pairs[1]),
        None if near is None else lax.ppermute(near, "ax", pairs[0]),
    )


def turn(far, near):
    count = lax.axis_size("az")
    pairs = ([], [])
    for i in range(count):
        pairs[i % 2].extend([(i, (i + 1) % count), ((i + 1) % count, i)])
    return lax.ppermute(far, "az", pairs[1]), lax.ppermute(near, "az", pairs[0])


def body(lamb_vector, owner, element, shape_class, interp_tables, acoustic_state):
    devices = lax.axis_size("ax") * lax.axis_size("az")
    flow, _, points = lamb_vector.shape
    capacity = max(2, 3 * flow // devices)
    slots = devices * capacity
    f32, bf16 = jnp.float32, jnp.bfloat16

    state = acoustic_state.reshape(STATE)
    face_shapes = [jax.ShapeDtypeStruct(s, bf16) for s in (AX_FACE, AX_FACE, AZ_FACE, AZ_FACE)]
    vmem_state = pltpu.VMEM(STATE, f32)
    source_shape = (3 * NODES * ROWS, LANES)

    buffer = call(
        functools.partial(contribution_kernel, capacity, devices),
        pltpu.HBM((slots, 3 * LANES), jnp.int16),
        [IN_HBM] * 5,
        IN_HBM,
        scratch=[
            pltpu.VMEM((3, flow, points), bf16),
            pltpu.VMEM((1, flow), jnp.int32),
            pltpu.VMEM((2, 1, flow), jnp.int32),
            pltpu.VMEM((NODES, 2, points), bf16),
            pltpu.VMEM((3, slots, LANES), jnp.int16),
            pltpu.SemaphoreType.DMA((3,)),
            pltpu.SemaphoreType.DMA((1,)),
            pltpu.SemaphoreType.DMA((1,)),
            pltpu.SemaphoreType.DMA((3,)),
        ],
    )(
        in_hbm(jnp.transpose(lamb_vector, (1, 0, 2))),
        in_hbm(owner.reshape(1, flow)),
        in_hbm(element.reshape(1, flow)),
        in_hbm(shape_class.reshape(1, flow)),
        in_hbm(jnp.transpose(interp_tables, (2, 0, 1))),
    )
    routed = lax.all_to_all(buffer, ("ax", "az"), split_axis=0, concat_axis=0, tiled=True)

    state, far, near, az_far, az_near = call(
        load_kernel,
        [vmem_state] + face_shapes,
        [IN_HBM],
        scratch=[pltpu.SemaphoreType.DMA((FIELDS,))],
    )(in_hbm(state))
    far, near = swap(far, near)
    az_far, az_near = turn(az_far, az_near)
    moved = call(functools.partial(volume_first_kernel, STEP_SCALES[0]), vmem_state, 1)(state)
    source = call(source_kernel, pltpu.VMEM(source_shape, f32), 1)(routed)
    rate, far = call(
        functools.partial(first_far_kernel, STEP_SCALES[0]),
        [vmem_state, face_shapes[0]],
        5,
        aliases={0: 0},
    )(moved, source, far, az_far, az_near)
    far, _ = swap(far, None)
    rate, near, az_far, az_near = call(
        functools.partial(first_near_kernel, STEP_SCALES[0]),
        [vmem_state] + face_shapes[1:],
        3,
        aliases={0: 0},
    )(rate, source, near)
    _, near = swap(None, near)
    az_far, az_near = turn(az_far, az_near)
    moved, total, source = call(
        functools.partial(volume_and_source_kernel, STEP_SCALES[1]),
        [vmem_state, vmem_state, pltpu.HBM(source_shape, f32)],
        3,
        [IN_VMEM, IN_VMEM, IN_HBM],
        scratch=[pltpu.SemaphoreType.DMA((1,))],
    )(rate, state, source)

    for scale in STEP_SCALES[1:3]:
        rate, far = call(
            functools.partial(finish_far_kernel, scale),
            [vmem_state, face_shapes[0]],
            4,
            aliases={0: 0},
            cost=LONG,
        )(moved, far, az_far, az_near)
        far, _ = swap(far, None)
        rate, near, az_far, az_near = call(
            functools.partial(finish_near_kernel, scale),
            [vmem_state] + face_shapes[1:],
            2,
            aliases={0: 0},
        )(rate, near)
        _, near = swap(None, near)
        az_far, az_near = turn(az_far, az_near)
        if scale == STEP_SCALES[1]:
            moved, total = call(
                functools.partial(volume_kernel, STEP_SCALES[2]), [vmem_state, vmem_state], 2
            )(rate, total)

    total = call(
        functools.partial(volume_last_kernel, STEP_SCALES[3]),
        vmem_state,
        2,
        scratch=[pltpu.VMEM(STATE, f32)],
    )(rate, total)
    planes = (FIELDS, 5, 25, ROWS, LANES)
    vmem_planes, hbm_planes = pltpu.VMEM(planes, f32), pltpu.HBM(planes, f32)
    total, partial = call(
        functools.partial(last_far_kernel, STEP_SCALES[3]),
        [vmem_planes, hbm_planes],
        4,
        [IN_VMEM, IN_HBM],
        aliases={0: 0},
        cost=LONG,
        scratch=[pltpu.SemaphoreType.DMA((10,))],
    )(total.reshape(planes), far, az_far, az_near)
    _, new_state = call(
        functools.partial(last_near_kernel, STEP_SCALES[3]),
        [vmem_planes, hbm_planes],
        [IN_VMEM, IN_HBM, IN_VMEM],
        [IN_VMEM, IN_HBM],
        aliases={0: 0, 1: 1},
        scratch=[pltpu.SemaphoreType.DMA((1,))],
    )(total, partial, near)
    shape = acoustic_state.shape
    return new_state.reshape(shape), source.reshape((3,) + shape[1:])


def solution(mesh):
    in_specs = (
        P(("ax", "az"), None, None),
        P(("ax", "az"), None),
        P(("ax", "az")),
        P(("ax", "az")),
        P(),
        P(None, None, "ax", "az", None),
    )
    out_specs = (P(None, None, "ax", "az", None), P(None, None, "ax", "az", None))
    return jax.shard_map(body, mesh=mesh, in_specs=in_specs, out_specs=out_specs, check_vma=False)
```

```python
import functools
import math

import jax
import jax.numpy as jnp
import numpy as np
from jax import lax
from jax.experimental import pallas as pl
from jax.experimental.pallas import tpu as pltpu
from jax.sharding import PartitionSpec as P

MACH = 0.3
RUSANOV = 1.3
DT = 0.03
LIFT = 10.0
VOLUME = 2.0
STEP_SCALES = (DT, DT / 2.0, DT / 3.0, DT / 4.0)

FIELDS = 5
NODES = 125
ROWS = 8
LANES = 128
VMEM_BYTES = 24 * 1024 * 1024


def derivative_matrix():
    points = np.array([-1.0, -math.sqrt(3.0 / 7.0), 0.0, math.sqrt(3.0 / 7.0), 1.0])
    weights = [1.0 / np.prod([points[j] - points[k] for k in range(5) if k != j]) for j in range(5)]
    matrix = np.zeros((5, 5))
    for i in range(5):
        for j in range(5):
            if i != j:
                matrix[i, j] = weights[j] / weights[i] / (points[i] - points[j])
        matrix[i, i] = -np.sum(matrix[i])
    return matrix


DERIVATIVE = -VOLUME * derivative_matrix()


def differentiate(g, scale):
    d = [[float(scale * v) for v in row] for row in DERIVATIVE]
    even_out, odd_out = g[0] - g[4], g[1] - g[3]
    s_out, s_in = g[0] + g[4], g[1] + g[3]
    results = [None] * 5
    for i in (0, 1):
        same = (d[i][0] - d[i][4]) / 2 * even_out + (d[i][1] - d[i][3]) / 2 * odd_out
        flip = (d[i][0] + d[i][4]) / 2 * s_out + (d[i][1] + d[i][3]) / 2 * s_in + d[i][2] * g[2]
        results[i] = same + flip
        results[4 - i] = same - flip
    results[2] = d[2][0] * even_out + d[2][1] * odd_out
    return results


def flux(q, direction):
    g, u, v, w, e = q
    if direction == 0:
        return [(2.0 * MACH) * g + (1.0 - MACH**2) * u, g, None, None, MACH * e]
    if direction == 1:
        return [v, None, g, None, None]
    return [w, None, None, g, None]


def original(q):
    g, u, v, w, e = q
    p = g - MACH * u
    return [p, u, v, w, e + p]


def lifted(q, direction, normal, rusanov_sign):
    result = []
    for value, flow in zip(q, flux(q, direction)):
        term = (LIFT * RUSANOV * rusanov_sign) * value
        if flow is not None:
            term = term + (LIFT * normal) * flow
        result.append(term)
    return result


def coupled(jump, direction, normal, scale):
    g, u, v, w, e = jump
    rusanov, lift = scale * LIFT * RUSANOV, scale * LIFT * normal
    if direction == 0:
        return [
            (2.0 * MACH * lift - rusanov) * g + ((1.0 - MACH**2) * lift) * u,
            lift * g - rusanov * u,
            -rusanov * v,
            -rusanov * w,
            (MACH * lift - rusanov) * e,
        ]
    normal_velocity = (v, w)[direction - 1]
    along = lift * g - rusanov * normal_velocity
    return [
        lift * normal_velocity - rusanov * g,
        -rusanov * u,
        along if direction == 1 else -rusanov * v,
        along if direction == 2 else -rusanov * w,
        -rusanov * e,
    ]


def shifted(q, amount, axis, keep):
    return [jnp.where(keep, pltpu.roll(value, amount, axis), 0.0) for value in q]


def volume_into(state_ref, scale, store):
    row = lax.broadcasted_iota(jnp.int32, (ROWS, LANES), 0)
    lane = lax.broadcasted_iota(jnp.int32, (ROWS, LANES), 1)
    cell = row % 4
    keep = {
        0: (row >= 4, row < 4),
        1: (cell != 0, cell != 3),
        2: (lane != 0, lane != LANES - 1),
    }
    rolls = {0: (4, 4, 0), 1: (1, ROWS - 1, 0), 2: (1, LANES - 1, 1)}

    def load(field, node):
        return state_ref[field * NODES + node]

    def face_terms(direction, low, high):
        up, down, axis = rolls[direction]
        keep_low, keep_high = keep[direction]
        if direction == 0:
            turned = [pltpu.roll(jnp.where(keep_high, b, a), up, axis) for a, b in zip(low, high)]
            below = [jnp.where(keep_low, value, 0.0) for value in turned]
            above = [jnp.where(keep_high, value, 0.0) for value in turned]
        else:
            below = shifted(high, up, axis, keep_low)
            above = shifted(low, down, axis, keep_high)
        jump_low = [a - b for a, b in zip(low, below)]
        jump_high = [a - b for a, b in zip(high, above)]
        return coupled(jump_low, direction, -1.0, scale), coupled(jump_high, direction, 1.0, scale)

    def line(direction, nodes):
        q = [[load(f, n) for n in nodes] for f in range(FIELDS)]
        ends = face_terms(direction, [x[0] for x in q], [x[4] for x in q])
        g, u, e = q[0], q[1], q[4]
        if direction == 0:
            mixed = [(2.0 * MACH) * g[k] + (1.0 - MACH**2) * u[k] for k in range(5)]
            parts = {
                0: differentiate(mixed, scale),
                1: differentiate(g, scale),
                4: differentiate(e, scale * MACH),
            }
        else:
            parts = {
                0: differentiate(q[direction + 1], scale),
                direction + 1: differentiate(g, scale),
            }
        values = []
        for f in range(FIELDS):
            row = list(parts[f]) if f in parts else [None] * 5
            for k, end in ((0, ends[0][f]), (4, ends[1][f])):
                row[k] = end if row[k] is None else row[k] + end
            values.append(row)
        store(direction, nodes, values, q)

    @pl.loop(0, 5)
    def _(outer):
        for inner in range(5):
            line(0, [k * 25 + outer * 5 + inner for k in range(5)])

    @pl.loop(0, 5)
    def _(outer):
        for inner in range(5):
            line(1, [outer * 25 + k * 5 + inner for k in range(5)])

    @pl.loop(0, 5)
    def _(outer):
        for inner in range(5):
            line(2, [outer * 25 + inner * 5 + k for k in range(5)])


def volume_first_kernel(scale, state_ref, out_ref):
    volume_into(state_ref, scale, add_to(out_ref))


def add_to(out_ref):
    def store(direction, nodes, values, q):
        for f in range(FIELDS):
            for node, value in zip(nodes, values[f]):
                at = f * NODES + node
                if direction == 0:
                    out_ref[at] = jnp.zeros_like(q[0][0]) if value is None else value
                elif value is not None:
                    out_ref[at] += value

    return store


def volume_kernel(scale, state_ref, sum_in, out_ref, sum_ref):
    add = add_to(out_ref)

    def store(direction, nodes, values, q):
        add(direction, nodes, values, q)
        if direction == 2:
            for f in range(FIELDS):
                for node, value in zip(nodes, q[f]):
                    at = f * NODES + node
                    sum_ref[at] = sum_in[at] + value

    volume_into(state_ref, scale, store)


def volume_and_source_kernel(
    scale, state_ref, sum_in, source_ref, out_ref, sum_ref, out_hbm, sem
):
    rows = pl.ds(0, out_hbm.shape[0])
    copy = pltpu.make_async_copy(source_ref.at[rows], out_hbm, sem.at[0])
    copy.start()
    volume_kernel(scale, state_ref, sum_in, out_ref, sum_ref)
    copy.wait()


def volume_last_kernel(scale, state_ref, sum_in, sum_ref, out_ref):
    add = add_to(out_ref)

    def store(direction, nodes, values, q):
        if direction < 2:
            add(direction, nodes, values, q)
            return
        for k, node in enumerate(nodes):
            totals = []
            for f in range(FIELDS):
                at = f * NODES + node
                total = sum_in[at] + q[f][k] + out_ref[at]
                totals.append(total if values[f][k] is None else total + values[f][k])
            for f, total in enumerate(original(totals)):
                sum_ref[f * NODES + node] = total

    volume_into(state_ref, scale, store)


def on_parity(axis, even, odd):
    parity = lax.axis_index(axis) % 2
    pl.when(parity == 0)(even)
    pl.when(parity == 1)(odd)


def five(ref, f, at):
    return (pl.ds(f * NODES + at, 5),) if len(ref.shape) == 3 else (f, at // 25, pl.ds(at % 25, 5))


def received(ref, start):
    return [ref[pl.ds(f * 25 + start, 5)].astype(jnp.float32) for f in range(FIELDS)]


def add_ax(out_ref, face, high, weight, final):
    sign = -weight if high else weight
    first, rows = (100, slice(4, 8)) if high else (0, slice(0, 4))
    for chunk in range(5):
        terms = lifted(received(face, chunk * 5), 0, sign, weight)
        terms = original(terms) if final else terms
        for f, term in enumerate(terms):
            out_ref[*five(out_ref, f, first + chunk * 5), rows, :] += term


def add_far(out_ref, face, weight, final=False):
    on_parity(
        "ax",
        lambda: add_ax(out_ref, face, False, weight, final),
        lambda: add_ax(out_ref, face, True, weight, final),
    )


def add_near(out_ref, face, weight, final=False):
    on_parity(
        "ax",
        lambda: add_ax(out_ref, face, True, weight, final),
        lambda: add_ax(out_ref, face, False, weight, final),
    )


def add_az(out_ref, far, near, weight, final=False):
    row = lax.broadcasted_iota(jnp.int32, (5, ROWS, LANES), 1)

    def add_side(face, at, rows, chunk, sign):
        terms = lifted(received(face, chunk), 1, sign, weight)
        for f, term in enumerate(original(terms) if final else terms):
            spread = jnp.where(row == rows[1], term[:, 1:2], 0.0)
            out_ref[*five(out_ref, f, at)] += jnp.where(row == rows[0], term[:, 0:1], spread)

    def add(low, high):
        for a in range(5):
            add_side(low, a * 25, (0, 4), a * 5, weight)
            add_side(high, a * 25 + 20, (3, 7), a * 5, -weight)

    on_parity("az", lambda: add(far, near), lambda: add(near, far))


def pack_ax(state_ref, face, high):
    first, rows = (100, slice(4, 8)) if high else (0, slice(0, 4))
    for f in range(FIELDS):
        face[pl.ds(f * 25, 25)] = state_ref[pl.ds(f * NODES + first, 25), rows, :].astype(
            jnp.bfloat16
        )


def pack_far(state_ref, face):
    on_parity("ax", lambda: pack_ax(state_ref, face, False), lambda: pack_ax(state_ref, face, True))


def pack_near(state_ref, face):
    on_parity("ax", lambda: pack_ax(state_ref, face, True), lambda: pack_ax(state_ref, face, False))


def pack_az(state_ref, far, near):
    def pack(az_low, az_high):
        for f in range(FIELDS):
            for a in range(5):
                at, to = f * NODES + a * 25, pl.ds((f * 5 + a) * 5, 5)
                low = [state_ref[pl.ds(at, 5), k : k + 1, :] for k in (0, 4)]
                high = [state_ref[pl.ds(at + 20, 5), k : k + 1, :] for k in (3, 7)]
                az_low[to] = jnp.concatenate(low, axis=1).astype(jnp.bfloat16)
                az_high[to] = jnp.concatenate(high, axis=1).astype(jnp.bfloat16)

    on_parity("az", lambda: pack(far, near), lambda: pack(near, far))


def load_kernel(state_hbm, state_ref, far, near, az_far, az_near, sems):
    copies = []
    for f in range(FIELDS):
        nodes = pl.ds(f * NODES, NODES)
        copy = pltpu.make_async_copy(state_hbm.at[nodes], state_ref.at[nodes], sems.at[f])
        copy.start()
        copies.append(copy)
    for copy in copies:
        copy.wait()

    @pl.loop(0, NODES // 5)
    def _(chunk):
        for k in range(5):
            node = chunk * 5 + k
            p = state_ref[node]
            state_ref[node] = p + MACH * state_ref[NODES + node]
            state_ref[4 * NODES + node] -= p

    pack_faces(state_ref, far, near, az_far, az_near)


def pack_faces(state_ref, far, near, az_far, az_near):
    pack_far(state_ref, far)
    pack_near(state_ref, near)
    pack_az(state_ref, az_far, az_near)


def add_source(state_ref, source_ref, scale, nodes):
    for node in nodes:
        for c in range(3):
            value = scale * source_ref[pl.ds((c * NODES + node) * ROWS, ROWS), :]
            state_ref[(c + 1) * NODES + node] += value
            if c == 0:
                state_ref[node] += MACH * value


def first_far_kernel(scale, state_in, source_ref, far, az_far, az_near, state_ref, far_out):
    add_az(state_ref, az_far, az_near, scale)
    add_far(state_ref, far, scale)
    add_source(state_ref, source_ref, scale, [*range(25), *range(100, NODES)])
    pack_far(state_ref, far_out)


def first_near_kernel(scale, state_in, source_ref, near, state_ref, near_out, *az_out):
    add_near(state_ref, near, scale)
    add_source(state_ref, source_ref, scale, range(25, 100))
    pack_near(state_ref, near_out)
    pack_az(state_ref, *az_out)


def finish_far_kernel(scale, state_in, far, az_far, az_near, state_ref, far_out):
    add_az(state_ref, az_far, az_near, scale)
    add_far(state_ref, far, scale)
    pack_far(state_ref, far_out)


def finish_near_kernel(scale, state_in, near, state_ref, near_out, az_far_out, az_near_out):
    add_near(state_ref, near, scale)
    pack_near(state_ref, near_out)
    pack_az(state_ref, az_far_out, az_near_out)


def last_far_kernel(weight, state_in, far, az_far, az_near, state_ref, out_hbm, sems):
    far_plane = 4 * (lax.axis_index("ax") % 2)

    def copy(k, plane, nodes):
        part = (slice(None), plane, nodes)
        return pltpu.make_async_copy(state_ref.at[*part], out_hbm.at[*part], sems.at[k])

    inside = [copy(k, plane, pl.ds(5, 15)) for k, plane in enumerate((1, 2, 3))]
    for part in inside:
        part.start()
    add_az(state_ref, az_far, az_near, weight, final=True)
    add_far(state_ref, far, weight, final=True)
    outside = [copy(3, far_plane, pl.ds(0, 25))]
    outside += [copy(4 + k, k + 1, pl.ds(0, 5)) for k in range(3)]
    outside += [copy(7 + k, k + 1, pl.ds(20, 5)) for k in range(3)]
    for part in outside:
        part.start()
    for part in inside + outside:
        part.wait()


def last_near_kernel(weight, state_in, out_in, near, state_ref, out_hbm, sem):
    add_near(state_ref, near, weight, final=True)
    part = (slice(None), 4 - 4 * (lax.axis_index("ax") % 2))
    copy = pltpu.make_async_copy(state_ref.at[*part], out_hbm.at[*part], sem.at[0])
    copy.start()
    copy.wait()


def contribution_kernel(
    capacity,
    devices,
    lamb_hbm,
    owner_hbm,
    element_hbm,
    class_hbm,
    tables_hbm,
    out_hbm,
    lamb_ref,
    owner_ref,
    rows_ref,
    tables_ref,
    out_ref,
    row_sems,
    tables_sem,
    lamb_sem,
    out_sems,
):
    flow = lamb_ref.shape[1]
    slots = devices * capacity
    row_copies = [
        pltpu.make_async_copy(owner_hbm, owner_ref, row_sems.at[0]),
        pltpu.make_async_copy(element_hbm, rows_ref.at[0], row_sems.at[1]),
        pltpu.make_async_copy(class_hbm, rows_ref.at[1], row_sems.at[2]),
    ]
    lamb_copy = pltpu.make_async_copy(lamb_hbm, lamb_ref, lamb_sem.at[0])
    tables_copy = pltpu.make_async_copy(
        tables_hbm, tables_ref.at[pl.ds(0, NODES)], tables_sem.at[0]
    )
    for copy in row_copies + [tables_copy, lamb_copy]:
        copy.start()
    for copy in row_copies:
        copy.wait()

    tables_ref[pl.ds(NODES, LANES - NODES)] = jnp.zeros(
        (LANES - NODES,) + tables_ref.shape[1:], jnp.bfloat16
    )
    owner_row = owner_ref[...]
    rows = jnp.concatenate(
        [rows_ref[0], rows_ref[1], jnp.zeros((ROWS - 2, flow), jnp.int32)], axis=0
    )
    columns = jnp.transpose(rows.astype(jnp.float32))
    element = columns[:, 0:1]
    second = columns[:, 1:2]

    owned = (lax.broadcasted_iota(jnp.int32, (devices, flow), 0) == owner_row).astype(jnp.float32)
    earlier = lax.broadcasted_iota(jnp.int32, (flow, flow), 0) < lax.broadcasted_iota(
        jnp.int32, (flow, flow), 1
    )
    running = jnp.dot(
        owned.astype(jnp.bfloat16),
        earlier.astype(jnp.bfloat16),
        preferred_element_type=jnp.float32,
    )
    position = jnp.sum(running * owned, axis=0, keepdims=True).astype(jnp.int32)
    slot_row = owner_row * capacity + position
    placing = (lax.broadcasted_iota(jnp.int32, (slots, flow), 0) == slot_row).astype(jnp.bfloat16)

    tables_copy.wait()
    tables = jnp.concatenate([tables_ref[:, 0, :], tables_ref[:, 1, :]], axis=0)
    lamb_copy.wait()
    both = lax.dot_general(
        lamb_ref[...].reshape(3 * flow, lamb_ref.shape[2]),
        tables,
        (((1,), (1,)), ((), ())),
        preferred_element_type=jnp.float32,
    )
    use_second = jnp.broadcast_to(second, (flow, LANES)) > 0.5
    values = [
        jnp.where(
            use_second, both[c * flow : (c + 1) * flow, LANES:], both[c * flow : (c + 1) * flow, :LANES]
        )
        for c in range(3)
    ]
    largest = jnp.maximum(jnp.maximum(jnp.abs(values[0]), jnp.abs(values[1])), jnp.abs(values[2]))
    largest = jnp.max(largest, axis=1, keepdims=True)
    exponent = jnp.clip(jnp.ceil(jnp.log2(jnp.maximum(largest, 1e-36))), -100.0, 30.0)
    scale = jnp.broadcast_to(jnp.exp2(14.0 - exponent), (flow, LANES))
    column = lax.broadcasted_iota(jnp.int32, (flow, LANES), 1)
    out_copies = []
    for c in range(3):
        whole = jnp.round(values[c] * scale)
        if c == 0:
            whole = jnp.where(column == NODES, exponent, whole)
            whole = jnp.where(column == NODES + 1, element, whole)
        high = jnp.floor(whole * (1.0 / 256.0))
        low = whole - 256.0 * high
        pieces = jnp.concatenate([high, low], axis=1).astype(jnp.bfloat16)
        placed = jnp.dot(placing, pieces, preferred_element_type=jnp.float32)
        placed = placed[:, :LANES] * 256.0 + placed[:, LANES:]
        out_ref[c] = placed.astype(jnp.int32).astype(jnp.int16)
        copy = pltpu.make_async_copy(
            out_ref.at[c], out_hbm.at[:, pl.ds(c * LANES, LANES)], out_sems.at[c]
        )
        copy.start()
        out_copies.append(copy)
    for copy in out_copies:
        copy.wait()


def source_kernel(received_ref, source_ref):
    slots = received_ref.shape[0]
    wide = 2 * LANES
    highs, lows = [], []
    for c in range(3):
        values = received_ref[:, pl.ds(c * LANES, LANES)].astype(jnp.int32).astype(jnp.float32)
        if c == 0:
            element = values[:, NODES + 1 : NODES + 2].astype(jnp.int32)
        values = jnp.transpose(values)
        if c == 0:
            scale = jnp.exp2(values[NODES : NODES + 1, :] - 14.0)
        values = values * scale
        high = values.astype(jnp.bfloat16)
        highs.append(high)
        lows.append((values - high.astype(jnp.float32)).astype(jnp.bfloat16))
    parts = jnp.concatenate(highs + lows, axis=0)
    column = lax.broadcasted_iota(jnp.int32, (slots, wide), 1)
    for group in range(ROWS // 2):
        member = (element == column + group * wide).astype(jnp.bfloat16)
        total = jnp.dot(parts, member, preferred_element_type=jnp.float32)
        total = total[0 : 3 * LANES] + total[3 * LANES :]
        for c in range(3):
            for k in range(2):
                start = c * NODES * ROWS + group * 2 + k
                source_ref[pl.ds(start, LANES, stride=ROWS), :] = total[
                    c * LANES : (c + 1) * LANES, k * LANES : (k + 1) * LANES
                ]

STATE = (FIELDS * NODES, ROWS, LANES)
AX_FACE = (FIELDS * 25, 4, LANES)
AZ_FACE = (FIELDS * 25, 2, LANES)


LONG = pl.CostEstimate(flops=10**11, bytes_accessed=10**9, transcendentals=0)
IN_VMEM = pl.BlockSpec(memory_space=pltpu.VMEM)
IN_HBM = pl.BlockSpec(memory_space=pltpu.HBM)


def in_hbm(x):
    return pltpu.with_memory_space_constraint(x, pltpu.HBM)


def call(kernel, out_shape, in_specs, out_specs=IN_VMEM, aliases=None, scratch=(), cost=None):
    if not isinstance(out_specs, list):
        out_specs = jax.tree.map(lambda _: out_specs, out_shape)
    return pl.pallas_call(
        kernel,
        out_shape=out_shape,
        in_specs=in_specs if isinstance(in_specs, list) else [IN_VMEM] * in_specs,
        out_specs=out_specs,
        scratch_shapes=scratch,
        input_output_aliases=aliases or {},
        cost_estimate=cost,
        compiler_params=pltpu.CompilerParams(vmem_limit_bytes=VMEM_BYTES),
    )


def swap(far, near):
    count = lax.axis_size("ax")
    pairs = ([], [])
    for i in range(count - 1):
        pairs[i % 2].extend([(i, i + 1), (i + 1, i)])
    return (
        None if far is None else lax.ppermute(far, "ax", pairs[1]),
        None if near is None else lax.ppermute(near, "ax", pairs[0]),
    )


def turn(far, near):
    count = lax.axis_size("az")
    pairs = ([], [])
    for i in range(count):
        pairs[i % 2].extend([(i, (i + 1) % count), ((i + 1) % count, i)])
    return lax.ppermute(far, "az", pairs[1]), lax.ppermute(near, "az", pairs[0])


def body(lamb_vector, owner, element, shape_class, interp_tables, acoustic_state):
    devices = lax.axis_size("ax") * lax.axis_size("az")
    flow, _, points = lamb_vector.shape
    capacity = max(2, 3 * flow // devices)
    slots = devices * capacity
    f32, bf16 = jnp.float32, jnp.bfloat16

    state = acoustic_state.reshape(STATE)
    face_shapes = [jax.ShapeDtypeStruct(s, bf16) for s in (AX_FACE, AX_FACE, AZ_FACE, AZ_FACE)]
    vmem_state = pltpu.VMEM(STATE, f32)
    source_shape = (3 * NODES * ROWS, LANES)

    buffer = call(
        functools.partial(contribution_kernel, capacity, devices),
        pltpu.HBM((slots, 3 * LANES), jnp.int16),
        [IN_HBM] * 5,
        IN_HBM,
        scratch=[
            pltpu.VMEM((3, flow, points), bf16),
            pltpu.VMEM((1, flow), jnp.int32),
            pltpu.VMEM((2, 1, flow), jnp.int32),
            pltpu.VMEM((LANES, 2, points), bf16),
            pltpu.VMEM((3, slots, LANES), jnp.int16),
            pltpu.SemaphoreType.DMA((3,)),
            pltpu.SemaphoreType.DMA((1,)),
            pltpu.SemaphoreType.DMA((1,)),
            pltpu.SemaphoreType.DMA((3,)),
        ],
    )(
        in_hbm(jnp.transpose(lamb_vector, (1, 0, 2))),
        in_hbm(owner.reshape(1, flow)),
        in_hbm(element.reshape(1, flow)),
        in_hbm(shape_class.reshape(1, flow)),
        in_hbm(jnp.transpose(interp_tables, (2, 0, 1))),
    )
    routed = lax.all_to_all(buffer, ("ax", "az"), split_axis=0, concat_axis=0, tiled=True)

    state, far, near, az_far, az_near = call(
        load_kernel,
        [vmem_state] + face_shapes,
        [IN_HBM],
        scratch=[pltpu.SemaphoreType.DMA((FIELDS,))],
    )(in_hbm(state))
    far, near = swap(far, near)
    az_far, az_near = turn(az_far, az_near)
    moved = call(functools.partial(volume_first_kernel, STEP_SCALES[0]), vmem_state, 1)(state)
    source_rows = 3 * NODES * ROWS + 3 * ROWS
    source = call(source_kernel, pltpu.VMEM((source_rows, LANES), f32), 1)(routed)
    rate, far = call(
        functools.partial(first_far_kernel, STEP_SCALES[0]),
        [vmem_state, face_shapes[0]],
        5,
        aliases={0: 0},
    )(moved, source, far, az_far, az_near)
    far, _ = swap(far, None)
    rate, near, az_far, az_near = call(
        functools.partial(first_near_kernel, STEP_SCALES[0]),
        [vmem_state] + face_shapes[1:],
        3,
        aliases={0: 0},
    )(rate, source, near)
    _, near = swap(None, near)
    az_far, az_near = turn(az_far, az_near)
    moved, total, source = call(
        functools.partial(volume_and_source_kernel, STEP_SCALES[1]),
        [vmem_state, vmem_state, pltpu.HBM(source_shape, f32)],
        3,
        [IN_VMEM, IN_VMEM, IN_HBM],
        scratch=[pltpu.SemaphoreType.DMA((1,))],
    )(rate, state, source)

    for scale in STEP_SCALES[1:3]:
        rate, far = call(
            functools.partial(finish_far_kernel, scale),
            [vmem_state, face_shapes[0]],
            4,
            aliases={0: 0},
            cost=LONG,
        )(moved, far, az_far, az_near)
        far, _ = swap(far, None)
        rate, near, az_far, az_near = call(
            functools.partial(finish_near_kernel, scale),
            [vmem_state] + face_shapes[1:],
            2,
            aliases={0: 0},
        )(rate, near)
        _, near = swap(None, near)
        az_far, az_near = turn(az_far, az_near)
        if scale == STEP_SCALES[1]:
            moved, total = call(
                functools.partial(volume_kernel, STEP_SCALES[2]), [vmem_state, vmem_state], 2
            )(rate, total)

    total = call(
        functools.partial(volume_last_kernel, STEP_SCALES[3]),
        vmem_state,
        2,
        scratch=[pltpu.VMEM(STATE, f32)],
    )(rate, total)
    planes = (FIELDS, 5, 25, ROWS, LANES)
    vmem_planes, hbm_planes = pltpu.VMEM(planes, f32), pltpu.HBM(planes, f32)
    total, partial = call(
        functools.partial(last_far_kernel, STEP_SCALES[3]),
        [vmem_planes, hbm_planes],
        4,
        [IN_VMEM, IN_HBM],
        aliases={0: 0},
        cost=LONG,
        scratch=[pltpu.SemaphoreType.DMA((10,))],
    )(total.reshape(planes), far, az_far, az_near)
    _, new_state = call(
        functools.partial(last_near_kernel, STEP_SCALES[3]),
        [vmem_planes, hbm_planes],
        [IN_VMEM, IN_HBM, IN_VMEM],
        [IN_VMEM, IN_HBM],
        aliases={0: 0, 1: 1},
        scratch=[pltpu.SemaphoreType.DMA((1,))],
    )(total, partial, near)
    shape = acoustic_state.shape
    return new_state.reshape(shape), source.reshape((3,) + shape[1:])


def solution(mesh):
    in_specs = (
        P(("ax", "az"), None, None),
        P(("ax", "az"), None),
        P(("ax", "az")),
        P(("ax", "az")),
        P(),
        P(None, None, "ax", "az", None),
    )
    out_specs = (P(None, None, "ax", "az", None), P(None, None, "ax", "az", None))
    return jax.shard_map(body, mesh=mesh, in_specs=in_specs, out_specs=out_specs, check_vma=False)
```

```python
import functools
import math

import jax
import jax.numpy as jnp
import numpy as np
from jax import lax
from jax.experimental import pallas as pl
from jax.experimental.pallas import tpu as pltpu
from jax.sharding import PartitionSpec as P

MACH = 0.3
RUSANOV = 1.3
DT = 0.03
LIFT = 10.0
VOLUME = 2.0
STEP_SCALES = (DT, DT / 2.0, DT / 3.0, DT / 4.0)

FIELDS = 5
NODES = 125
ROWS = 8
LANES = 128
VMEM_BYTES = 24 * 1024 * 1024


def derivative_matrix():
    points = np.array([-1.0, -math.sqrt(3.0 / 7.0), 0.0, math.sqrt(3.0 / 7.0), 1.0])
    weights = [1.0 / np.prod([points[j] - points[k] for k in range(5) if k != j]) for j in range(5)]
    matrix = np.zeros((5, 5))
    for i in range(5):
        for j in range(5):
            if i != j:
                matrix[i, j] = weights[j] / weights[i] / (points[i] - points[j])
        matrix[i, i] = -np.sum(matrix[i])
    return matrix


DERIVATIVE = -VOLUME * derivative_matrix()


def differentiate(g, scale):
    d = [[float(scale * v) for v in row] for row in DERIVATIVE]
    even_out, odd_out = g[0] - g[4], g[1] - g[3]
    s_out, s_in = g[0] + g[4], g[1] + g[3]
    results = [None] * 5
    for i in (0, 1):
        same = (d[i][0] - d[i][4]) / 2 * even_out + (d[i][1] - d[i][3]) / 2 * odd_out
        flip = (d[i][0] + d[i][4]) / 2 * s_out + (d[i][1] + d[i][3]) / 2 * s_in + d[i][2] * g[2]
        results[i] = same + flip
        results[4 - i] = same - flip
    results[2] = d[2][0] * even_out + d[2][1] * odd_out
    return results


def original(q):
    g, u, v, w, e = q
    p = g - MACH * u
    return [p, u, v, w, e + p]


def coupled(jump, direction, normal, scale):
    g, u, v, w, e = jump
    rusanov, lift = scale * LIFT * RUSANOV, scale * LIFT * normal
    if direction == 0:
        return [
            (2.0 * MACH * lift - rusanov) * g + ((1.0 - MACH**2) * lift) * u,
            lift * g - rusanov * u,
            -rusanov * v,
            -rusanov * w,
            (MACH * lift - rusanov) * e,
        ]
    normal_velocity = (v, w)[direction - 1]
    along = lift * g - rusanov * normal_velocity
    return [
        lift * normal_velocity - rusanov * g,
        -rusanov * u,
        along if direction == 1 else -rusanov * v,
        along if direction == 2 else -rusanov * w,
        -rusanov * e,
    ]


def shifted(q, amount, axis, keep):
    return [jnp.where(keep, pltpu.roll(value, amount, axis), 0.0) for value in q]


def volume_into(state_ref, scale, store):
    row = lax.broadcasted_iota(jnp.int32, (ROWS, LANES), 0)
    lane = lax.broadcasted_iota(jnp.int32, (ROWS, LANES), 1)
    cell = row % 4
    keep = {
        0: (row >= 4, row < 4),
        1: (cell != 0, cell != 3),
        2: (lane != 0, lane != LANES - 1),
    }
    rolls = {0: (4, 4, 0), 1: (1, ROWS - 1, 0), 2: (1, LANES - 1, 1)}

    def load(field, node):
        return state_ref[field * NODES + node]

    def face_terms(direction, low, high):
        up, down, axis = rolls[direction]
        keep_low, keep_high = keep[direction]
        if direction == 0:
            turned = [pltpu.roll(jnp.where(keep_high, b, a), up, axis) for a, b in zip(low, high)]
            below = [jnp.where(keep_low, value, 0.0) for value in turned]
            above = [jnp.where(keep_high, value, 0.0) for value in turned]
        else:
            below = shifted(high, up, axis, keep_low)
            above = shifted(low, down, axis, keep_high)
        jump_low = [a - b for a, b in zip(low, below)]
        jump_high = [a - b for a, b in zip(high, above)]
        return coupled(jump_low, direction, -1.0, scale), coupled(jump_high, direction, 1.0, scale)

    def line(direction, nodes):
        q = [[load(f, n) for n in nodes] for f in range(FIELDS)]
        ends = face_terms(direction, [x[0] for x in q], [x[4] for x in q])
        g, u, e = q[0], q[1], q[4]
        if direction == 0:
            mixed = [(2.0 * MACH) * g[k] + (1.0 - MACH**2) * u[k] for k in range(5)]
            parts = {
                0: differentiate(mixed, scale),
                1: differentiate(g, scale),
                4: differentiate(e, scale * MACH),
            }
        else:
            parts = {
                0: differentiate(q[direction + 1], scale),
                direction + 1: differentiate(g, scale),
            }
        values = []
        for f in range(FIELDS):
            row = list(parts[f]) if f in parts else [None] * 5
            for k, end in ((0, ends[0][f]), (4, ends[1][f])):
                row[k] = end if row[k] is None else row[k] + end
            values.append(row)
        store(direction, nodes, values, q)

    @pl.loop(0, 5)
    def _(outer):
        for inner in range(5):
            line(0, [k * 25 + outer * 5 + inner for k in range(5)])

    @pl.loop(0, 5)
    def _(outer):
        for inner in range(5):
            line(1, [outer * 25 + k * 5 + inner for k in range(5)])

    @pl.loop(0, 5)
    def _(outer):
        for inner in range(5):
            line(2, [outer * 25 + inner * 5 + k for k in range(5)])


def volume_first_kernel(scale, state_ref, out_ref):
    volume_into(state_ref, scale, add_to(out_ref))


def add_to(out_ref):
    def store(direction, nodes, values, q):
        for f in range(FIELDS):
            for node, value in zip(nodes, values[f]):
                at = f * NODES + node
                if direction == 0:
                    out_ref[at] = jnp.zeros_like(q[0][0]) if value is None else value
                elif value is not None:
                    out_ref[at] += value

    return store


def volume_kernel(scale, state_ref, sum_in, out_ref, sum_ref):
    add = add_to(out_ref)

    def store(direction, nodes, values, q):
        add(direction, nodes, values, q)
        if direction == 2:
            for f in range(FIELDS):
                for node, value in zip(nodes, q[f]):
                    at = f * NODES + node
                    sum_ref[at] = sum_in[at] + value

    volume_into(state_ref, scale, store)


def volume_and_source_kernel(
    scale, state_ref, sum_in, source_ref, out_ref, sum_ref, out_hbm, sem
):
    rows = pl.ds(0, out_hbm.shape[0])
    copy = pltpu.make_async_copy(source_ref.at[rows], out_hbm, sem.at[0])
    copy.start()
    volume_kernel(scale, state_ref, sum_in, out_ref, sum_ref)
    copy.wait()


def volume_last_kernel(scale, state_ref, sum_in, sum_ref, out_ref):
    add = add_to(out_ref)

    def store(direction, nodes, values, q):
        if direction < 2:
            add(direction, nodes, values, q)
            return
        for k, node in enumerate(nodes):
            totals = []
            for f in range(FIELDS):
                at = f * NODES + node
                total = sum_in[at] + q[f][k] + out_ref[at]
                totals.append(total if values[f][k] is None else total + values[f][k])
            for f, total in enumerate(original(totals)):
                sum_ref[f * NODES + node] = total

    volume_into(state_ref, scale, store)


def on_parity(axis, even, odd):
    parity = lax.axis_index(axis) % 2
    pl.when(parity == 0)(even)
    pl.when(parity == 1)(odd)


def five(ref, f, at):
    return (pl.ds(f * NODES + at, 5),) if len(ref.shape) == 3 else (f, at // 25, pl.ds(at % 25, 5))


def received(ref, start):
    return [ref[pl.ds(f * 25 + start, 5)].astype(jnp.float32) for f in range(FIELDS)]


def add_ax(out_ref, face, high, weight, final):
    first, rows = (100, slice(4, 8)) if high else (0, slice(0, 4))
    for chunk in range(5):
        terms = coupled(received(face, chunk * 5), 0, 1.0 if high else -1.0, -weight)
        terms = original(terms) if final else terms
        for f, term in enumerate(terms):
            out_ref[*five(out_ref, f, first + chunk * 5), rows, :] += term


def add_far(out_ref, face, weight, final=False):
    on_parity(
        "ax",
        lambda: add_ax(out_ref, face, False, weight, final),
        lambda: add_ax(out_ref, face, True, weight, final),
    )


def add_near(out_ref, face, weight, final=False):
    on_parity(
        "ax",
        lambda: add_ax(out_ref, face, True, weight, final),
        lambda: add_ax(out_ref, face, False, weight, final),
    )


def add_az(out_ref, far, near, weight, final=False):
    row = lax.broadcasted_iota(jnp.int32, (5, ROWS, LANES), 1)

    def add_side(face, at, rows, chunk, normal):
        terms = coupled(received(face, chunk), 1, normal, -weight)
        for f, term in enumerate(original(terms) if final else terms):
            spread = jnp.where(row == rows[1], term[:, 1:2], 0.0)
            out_ref[*five(out_ref, f, at)] += jnp.where(row == rows[0], term[:, 0:1], spread)

    def add(low, high):
        for a in range(5):
            add_side(low, a * 25, (0, 4), a * 5, -1.0)
            add_side(high, a * 25 + 20, (3, 7), a * 5, 1.0)

    on_parity("az", lambda: add(far, near), lambda: add(near, far))


def pack_ax(state_ref, face, high):
    first, rows = (100, slice(4, 8)) if high else (0, slice(0, 4))
    for f in range(FIELDS):
        face[pl.ds(f * 25, 25)] = state_ref[pl.ds(f * NODES + first, 25), rows, :].astype(
            jnp.bfloat16
        )


def pack_far(state_ref, face):
    on_parity("ax", lambda: pack_ax(state_ref, face, False), lambda: pack_ax(state_ref, face, True))


def pack_near(state_ref, face):
    on_parity("ax", lambda: pack_ax(state_ref, face, True), lambda: pack_ax(state_ref, face, False))


def pack_az(state_ref, far, near):
    def pack(az_low, az_high):
        for f in range(FIELDS):
            for a in range(5):
                at, to = f * NODES + a * 25, pl.ds((f * 5 + a) * 5, 5)
                low = [state_ref[pl.ds(at, 5), k : k + 1, :] for k in (0, 4)]
                high = [state_ref[pl.ds(at + 20, 5), k : k + 1, :] for k in (3, 7)]
                az_low[to] = jnp.concatenate(low, axis=1).astype(jnp.bfloat16)
                az_high[to] = jnp.concatenate(high, axis=1).astype(jnp.bfloat16)

    on_parity("az", lambda: pack(far, near), lambda: pack(near, far))


def load_kernel(state_hbm, state_ref, far, near, az_far, az_near, sems):
    copies = []
    for f in range(FIELDS):
        nodes = pl.ds(f * NODES, NODES)
        copy = pltpu.make_async_copy(state_hbm.at[nodes], state_ref.at[nodes], sems.at[f])
        copy.start()
        copies.append(copy)
    for copy in copies:
        copy.wait()

    @pl.loop(0, NODES // 5)
    def _(chunk):
        for k in range(5):
            node = chunk * 5 + k
            p = state_ref[node]
            state_ref[node] = p + MACH * state_ref[NODES + node]
            state_ref[4 * NODES + node] -= p

    pack_faces(state_ref, far, near, az_far, az_near)


def pack_faces(state_ref, far, near, az_far, az_near):
    pack_far(state_ref, far)
    pack_near(state_ref, near)
    pack_az(state_ref, az_far, az_near)


def add_source(state_ref, source_ref, scale, nodes):
    for node in nodes:
        for c in range(3):
            value = scale * source_ref[pl.ds((c * NODES + node) * ROWS, ROWS), :]
            state_ref[(c + 1) * NODES + node] += value
            if c == 0:
                state_ref[node] += MACH * value


def first_az_kernel(scale, state_in, az_far, az_near, state_ref):
    add_az(state_ref, az_far, az_near, scale)


def first_far_kernel(scale, state_in, source_ref, far, state_ref, far_out):
    add_far(state_ref, far, scale)
    add_source(state_ref, source_ref, scale, [*range(25), *range(100, NODES)])
    pack_far(state_ref, far_out)


def first_near_kernel(scale, state_in, source_ref, near, state_ref, near_out, *az_out):
    add_near(state_ref, near, scale)
    add_source(state_ref, source_ref, scale, range(25, 100))
    pack_near(state_ref, near_out)
    pack_az(state_ref, *az_out)


def finish_far_kernel(scale, state_in, far, az_far, az_near, state_ref, far_out):
    add_az(state_ref, az_far, az_near, scale)
    add_far(state_ref, far, scale)
    pack_far(state_ref, far_out)


def finish_near_kernel(scale, state_in, near, state_ref, near_out, az_far_out, az_near_out):
    add_near(state_ref, near, scale)
    pack_near(state_ref, near_out)
    pack_az(state_ref, az_far_out, az_near_out)


def last_far_kernel(weight, state_in, far, az_far, az_near, state_ref, out_hbm, sems):
    far_plane = 4 * (lax.axis_index("ax") % 2)

    def copy(k, plane, nodes):
        part = (slice(None), plane, nodes)
        return pltpu.make_async_copy(state_ref.at[*part], out_hbm.at[*part], sems.at[k])

    inside = [copy(k, plane, pl.ds(5, 15)) for k, plane in enumerate((1, 2, 3))]
    for part in inside:
        part.start()
    add_az(state_ref, az_far, az_near, weight, final=True)
    add_far(state_ref, far, weight, final=True)
    outside = [copy(3, far_plane, pl.ds(0, 25))]
    outside += [copy(4 + k, k + 1, pl.ds(0, 5)) for k in range(3)]
    outside += [copy(7 + k, k + 1, pl.ds(20, 5)) for k in range(3)]
    for part in outside:
        part.start()
    for part in inside + outside:
        part.wait()


def last_near_kernel(weight, state_in, out_in, near, state_ref, out_hbm, sem):
    add_near(state_ref, near, weight, final=True)
    part = (slice(None), 4 - 4 * (lax.axis_index("ax") % 2))
    copy = pltpu.make_async_copy(state_ref.at[*part], out_hbm.at[*part], sem.at[0])
    copy.start()
    copy.wait()


def contribution_kernel(
    capacity,
    devices,
    lamb_hbm,
    owner_hbm,
    element_hbm,
    class_hbm,
    tables_hbm,
    out_hbm,
    lamb_ref,
    owner_ref,
    rows_ref,
    tables_ref,
    out_ref,
    row_sems,
    tables_sem,
    lamb_sem,
    out_sems,
):
    flow = lamb_ref.shape[1]
    slots = devices * capacity
    row_copies = [
        pltpu.make_async_copy(owner_hbm, owner_ref, row_sems.at[0]),
        pltpu.make_async_copy(element_hbm, rows_ref.at[0], row_sems.at[1]),
        pltpu.make_async_copy(class_hbm, rows_ref.at[1], row_sems.at[2]),
    ]
    lamb_copy = pltpu.make_async_copy(lamb_hbm, lamb_ref, lamb_sem.at[0])
    tables_copy = pltpu.make_async_copy(
        tables_hbm, tables_ref.at[pl.ds(0, NODES)], tables_sem.at[0]
    )
    for copy in row_copies + [tables_copy, lamb_copy]:
        copy.start()
    for copy in row_copies:
        copy.wait()

    tables_ref[pl.ds(NODES, LANES - NODES)] = jnp.zeros(
        (LANES - NODES,) + tables_ref.shape[1:], jnp.bfloat16
    )
    owner_row = owner_ref[...]
    rows = jnp.concatenate(
        [rows_ref[0], rows_ref[1], jnp.zeros((ROWS - 2, flow), jnp.int32)], axis=0
    )
    columns = jnp.transpose(rows.astype(jnp.float32))
    element = columns[:, 0:1]
    second = columns[:, 1:2]

    owned = (lax.broadcasted_iota(jnp.int32, (devices, flow), 0) == owner_row).astype(jnp.float32)
    earlier = lax.broadcasted_iota(jnp.int32, (flow, flow), 0) < lax.broadcasted_iota(
        jnp.int32, (flow, flow), 1
    )
    running = jnp.dot(
        owned.astype(jnp.bfloat16),
        earlier.astype(jnp.bfloat16),
        preferred_element_type=jnp.float32,
    )
    position = jnp.sum(running * owned, axis=0, keepdims=True).astype(jnp.int32)
    slot_row = owner_row * capacity + position
    placing = (lax.broadcasted_iota(jnp.int32, (slots, flow), 0) == slot_row).astype(jnp.bfloat16)

    tables_copy.wait()
    tables = jnp.concatenate([tables_ref[:, 0, :], tables_ref[:, 1, :]], axis=0)
    lamb_copy.wait()
    both = lax.dot_general(
        lamb_ref[...].reshape(3 * flow, lamb_ref.shape[2]),
        tables,
        (((1,), (1,)), ((), ())),
        preferred_element_type=jnp.float32,
    )
    use_second = jnp.broadcast_to(second, (flow, LANES)) > 0.5
    values = [
        jnp.where(
            use_second, both[c * flow : (c + 1) * flow, LANES:], both[c * flow : (c + 1) * flow, :LANES]
        )
        for c in range(3)
    ]
    largest = jnp.maximum(jnp.maximum(jnp.abs(values[0]), jnp.abs(values[1])), jnp.abs(values[2]))
    largest = jnp.max(largest, axis=1, keepdims=True)
    exponent = jnp.clip(jnp.ceil(jnp.log2(jnp.maximum(largest, 1e-36))), -100.0, 30.0)
    scale = jnp.broadcast_to(jnp.exp2(14.0 - exponent), (flow, LANES))
    column = lax.broadcasted_iota(jnp.int32, (flow, LANES), 1)
    out_copies = []
    for c in range(3):
        whole = jnp.round(values[c] * scale)
        if c == 0:
            whole = jnp.where(column == NODES, exponent, whole)
            whole = jnp.where(column == NODES + 1, element, whole)
        high = jnp.floor(whole * (1.0 / 256.0))
        low = whole - 256.0 * high
        pieces = jnp.concatenate([high, low], axis=1).astype(jnp.bfloat16)
        placed = jnp.dot(placing, pieces, preferred_element_type=jnp.float32)
        placed = placed[:, :LANES] * 256.0 + placed[:, LANES:]
        out_ref[c] = placed.astype(jnp.int32).astype(jnp.int16)
        copy = pltpu.make_async_copy(
            out_ref.at[c], out_hbm.at[:, pl.ds(c * LANES, LANES)], out_sems.at[c]
        )
        copy.start()
        out_copies.append(copy)
    for copy in out_copies:
        copy.wait()


def source_kernel(received_ref, source_ref):
    slots = received_ref.shape[0]
    wide = 2 * LANES
    highs, lows = [], []
    for c in range(3):
        values = received_ref[:, pl.ds(c * LANES, LANES)].astype(jnp.int32).astype(jnp.float32)
        if c == 0:
            element = values[:, NODES + 1 : NODES + 2].astype(jnp.int32)
        values = jnp.transpose(values)
        if c == 0:
            scale = jnp.exp2(values[NODES : NODES + 1, :] - 14.0)
        values = values * scale
        high = values.astype(jnp.bfloat16)
        highs.append(high)
        lows.append((values - high.astype(jnp.float32)).astype(jnp.bfloat16))
    parts = jnp.concatenate(highs + lows, axis=0)
    column = lax.broadcasted_iota(jnp.int32, (slots, wide), 1)
    for group in range(ROWS // 2):
        member = (element == column + group * wide).astype(jnp.bfloat16)
        total = jnp.dot(parts, member, preferred_element_type=jnp.float32)
        total = total[0 : 3 * LANES] + total[3 * LANES :]
        for c in range(3):
            for k in range(2):
                start = c * NODES * ROWS + group * 2 + k
                source_ref[pl.ds(start, LANES, stride=ROWS), :] = total[
                    c * LANES : (c + 1) * LANES, k * LANES : (k + 1) * LANES
                ]

STATE = (FIELDS * NODES, ROWS, LANES)
AX_FACE = (FIELDS * 25, 4, LANES)
AZ_FACE = (FIELDS * 25, 2, LANES)


LONG = pl.CostEstimate(flops=10**11, bytes_accessed=10**9, transcendentals=0)
IN_VMEM = pl.BlockSpec(memory_space=pltpu.VMEM)
IN_HBM = pl.BlockSpec(memory_space=pltpu.HBM)


def in_hbm(x):
    return pltpu.with_memory_space_constraint(x, pltpu.HBM)


def call(kernel, out_shape, in_specs, out_specs=IN_VMEM, aliases=None, scratch=(), cost=None):
    if not isinstance(out_specs, list):
        out_specs = jax.tree.map(lambda _: out_specs, out_shape)
    return pl.pallas_call(
        kernel,
        out_shape=out_shape,
        in_specs=in_specs if isinstance(in_specs, list) else [IN_VMEM] * in_specs,
        out_specs=out_specs,
        scratch_shapes=scratch,
        input_output_aliases=aliases or {},
        cost_estimate=cost,
        compiler_params=pltpu.CompilerParams(vmem_limit_bytes=VMEM_BYTES),
    )


def swap(far, near):
    count = lax.axis_size("ax")
    pairs = ([], [])
    for i in range(count - 1):
        pairs[i % 2].extend([(i, i + 1), (i + 1, i)])
    return (
        None if far is None else lax.ppermute(far, "ax", pairs[1]),
        None if near is None else lax.ppermute(near, "ax", pairs[0]),
    )


def turn(far, near):
    count = lax.axis_size("az")
    pairs = ([], [])
    for i in range(count):
        pairs[i % 2].extend([(i, (i + 1) % count), ((i + 1) % count, i)])
    return lax.ppermute(far, "az", pairs[1]), lax.ppermute(near, "az", pairs[0])


def body(lamb_vector, owner, element, shape_class, interp_tables, acoustic_state):
    devices = lax.axis_size("ax") * lax.axis_size("az")
    flow, _, points = lamb_vector.shape
    capacity = max(2, 3 * flow // devices)
    slots = devices * capacity
    f32, bf16 = jnp.float32, jnp.bfloat16

    state = acoustic_state.reshape(STATE)
    face_shapes = [jax.ShapeDtypeStruct(s, bf16) for s in (AX_FACE, AX_FACE, AZ_FACE, AZ_FACE)]
    vmem_state = pltpu.VMEM(STATE, f32)
    source_shape = (3 * NODES * ROWS, LANES)

    buffer = call(
        functools.partial(contribution_kernel, capacity, devices),
        pltpu.HBM((slots, 3 * LANES), jnp.int16),
        [IN_HBM] * 5,
        IN_HBM,
        scratch=[
            pltpu.VMEM((3, flow, points), bf16),
            pltpu.VMEM((1, flow), jnp.int32),
            pltpu.VMEM((2, 1, flow), jnp.int32),
            pltpu.VMEM((LANES, 2, points), bf16),
            pltpu.VMEM((3, slots, LANES), jnp.int16),
            pltpu.SemaphoreType.DMA((3,)),
            pltpu.SemaphoreType.DMA((1,)),
            pltpu.SemaphoreType.DMA((1,)),
            pltpu.SemaphoreType.DMA((3,)),
        ],
    )(
        in_hbm(jnp.transpose(lamb_vector, (1, 0, 2))),
        in_hbm(owner.reshape(1, flow)),
        in_hbm(element.reshape(1, flow)),
        in_hbm(shape_class.reshape(1, flow)),
        in_hbm(jnp.transpose(interp_tables, (2, 0, 1))),
    )
    routed = lax.all_to_all(buffer, ("ax", "az"), split_axis=0, concat_axis=0, tiled=True)

    state, far, near, az_far, az_near = call(
        load_kernel,
        [vmem_state] + face_shapes,
        [IN_HBM],
        scratch=[pltpu.SemaphoreType.DMA((FIELDS,))],
    )(in_hbm(state))
    far, near = swap(far, near)
    az_far, az_near = turn(az_far, az_near)
    moved = call(functools.partial(volume_first_kernel, STEP_SCALES[0]), vmem_state, 1)(state)
    moved = call(
        functools.partial(first_az_kernel, STEP_SCALES[0]), vmem_state, 3, aliases={0: 0}
    )(moved, az_far, az_near)
    source_rows = 3 * NODES * ROWS + 3 * ROWS
    source = call(source_kernel, pltpu.VMEM((source_rows, LANES), f32), 1)(routed)
    rate, far = call(
        functools.partial(first_far_kernel, STEP_SCALES[0]),
        [vmem_state, face_shapes[0]],
        3,
        aliases={0: 0},
    )(moved, source, far)
    far, _ = swap(far, None)
    rate, near, az_far, az_near = call(
        functools.partial(first_near_kernel, STEP_SCALES[0]),
        [vmem_state] + face_shapes[1:],
        3,
        aliases={0: 0},
    )(rate, source, near)
    _, near = swap(None, near)
    az_far, az_near = turn(az_far, az_near)
    moved, total, source = call(
        functools.partial(volume_and_source_kernel, STEP_SCALES[1]),
        [vmem_state, vmem_state, pltpu.HBM(source_shape, f32)],
        3,
        [IN_VMEM, IN_VMEM, IN_HBM],
        scratch=[pltpu.SemaphoreType.DMA((1,))],
    )(rate, state, source)

    for scale in STEP_SCALES[1:3]:
        rate, far = call(
            functools.partial(finish_far_kernel, scale),
            [vmem_state, face_shapes[0]],
            4,
            aliases={0: 0},
            cost=LONG,
        )(moved, far, az_far, az_near)
        far, _ = swap(far, None)
        rate, near, az_far, az_near = call(
            functools.partial(finish_near_kernel, scale),
            [vmem_state] + face_shapes[1:],
            2,
            aliases={0: 0},
        )(rate, near)
        _, near = swap(None, near)
        az_far, az_near = turn(az_far, az_near)
        if scale == STEP_SCALES[1]:
            moved, total = call(
                functools.partial(volume_kernel, STEP_SCALES[2]), [vmem_state, vmem_state], 2
            )(rate, total)

    total = call(
        functools.partial(volume_last_kernel, STEP_SCALES[3]),
        vmem_state,
        2,
        scratch=[pltpu.VMEM(STATE, f32)],
    )(rate, total)
    planes = (FIELDS, 5, 25, ROWS, LANES)
    vmem_planes, hbm_planes = pltpu.VMEM(planes, f32), pltpu.HBM(planes, f32)
    total, partial = call(
        functools.partial(last_far_kernel, STEP_SCALES[3]),
        [vmem_planes, hbm_planes],
        4,
        [IN_VMEM, IN_HBM],
        aliases={0: 0},
        cost=LONG,
        scratch=[pltpu.SemaphoreType.DMA((10,))],
    )(total.reshape(planes), far, az_far, az_near)
    _, new_state = call(
        functools.partial(last_near_kernel, STEP_SCALES[3]),
        [vmem_planes, hbm_planes],
        [IN_VMEM, IN_HBM, IN_VMEM],
        [IN_VMEM, IN_HBM],
        aliases={0: 0, 1: 1},
        scratch=[pltpu.SemaphoreType.DMA((1,))],
    )(total, partial, near)
    shape = acoustic_state.shape
    return new_state.reshape(shape), source.reshape((3,) + shape[1:])


def solution(mesh):
    in_specs = (
        P(("ax", "az"), None, None),
        P(("ax", "az"), None),
        P(("ax", "az")),
        P(("ax", "az")),
        P(),
        P(None, None, "ax", "az", None),
    )
    out_specs = (P(None, None, "ax", "az", None), P(None, None, "ax", "az", None))
    return jax.shard_map(body, mesh=mesh, in_specs=in_specs, out_specs=out_specs, check_vma=False)
```

```python
import functools
import math

import jax
import jax.numpy as jnp
import numpy as np
from jax import lax
from jax.experimental import pallas as pl
from jax.experimental.pallas import tpu as pltpu
from jax.sharding import PartitionSpec as P

MACH = 0.3
RUSANOV = 1.3
DT = 0.03
LIFT = 10.0
VOLUME = 2.0
STEP_SCALES = (DT, DT / 2.0, DT / 3.0, DT / 4.0)

FIELDS = 5
NODES = 125
ROWS = 8
LANES = 128
VMEM_BYTES = 24 * 1024 * 1024


def derivative_matrix():
    points = np.array([-1.0, -math.sqrt(3.0 / 7.0), 0.0, math.sqrt(3.0 / 7.0), 1.0])
    weights = [1.0 / np.prod([points[j] - points[k] for k in range(5) if k != j]) for j in range(5)]
    matrix = np.zeros((5, 5))
    for i in range(5):
        for j in range(5):
            if i != j:
                matrix[i, j] = weights[j] / weights[i] / (points[i] - points[j])
        matrix[i, i] = -np.sum(matrix[i])
    return matrix


DERIVATIVE = -VOLUME * derivative_matrix()


def differentiate(g, scale):
    d = [[float(scale * v) for v in row] for row in DERIVATIVE]
    even_out, odd_out = g[0] - g[4], g[1] - g[3]
    s_out, s_in = g[0] + g[4], g[1] + g[3]
    results = [None] * 5
    for i in (0, 1):
        same = (d[i][0] - d[i][4]) / 2 * even_out + (d[i][1] - d[i][3]) / 2 * odd_out
        flip = (d[i][0] + d[i][4]) / 2 * s_out + (d[i][1] + d[i][3]) / 2 * s_in + d[i][2] * g[2]
        results[i] = same + flip
        results[4 - i] = same - flip
    results[2] = d[2][0] * even_out + d[2][1] * odd_out
    return results


def original(q):
    g, u, v, w, e = q
    p = g - MACH * u
    return [p, u, v, w, e + p]


def coupled(jump, direction, normal, scale):
    g, u, v, w, e = jump
    rusanov, lift = scale * LIFT * RUSANOV, scale * LIFT * normal
    if direction == 0:
        return [
            (2.0 * MACH * lift - rusanov) * g + ((1.0 - MACH**2) * lift) * u,
            lift * g - rusanov * u,
            -rusanov * v,
            -rusanov * w,
            (MACH * lift - rusanov) * e,
        ]
    normal_velocity = (v, w)[direction - 1]
    along = lift * g - rusanov * normal_velocity
    return [
        lift * normal_velocity - rusanov * g,
        -rusanov * u,
        along if direction == 1 else -rusanov * v,
        along if direction == 2 else -rusanov * w,
        -rusanov * e,
    ]


def shifted(q, amount, axis, keep):
    return [jnp.where(keep, pltpu.roll(value, amount, axis), 0.0) for value in q]


def volume_into(state_ref, scale, store, unroll=False):
    row = lax.broadcasted_iota(jnp.int32, (ROWS, LANES), 0)
    lane = lax.broadcasted_iota(jnp.int32, (ROWS, LANES), 1)
    cell = row % 4
    keep = {
        0: (row >= 4, row < 4),
        1: (cell != 0, cell != 3),
        2: (lane != 0, lane != LANES - 1),
    }
    rolls = {0: (4, 4, 0), 1: (1, ROWS - 1, 0), 2: (1, LANES - 1, 1)}

    def load(field, node):
        return state_ref[field * NODES + node]

    def face_terms(direction, low, high):
        up, down, axis = rolls[direction]
        keep_low, keep_high = keep[direction]
        if direction == 0:
            turned = [pltpu.roll(jnp.where(keep_high, b, a), up, axis) for a, b in zip(low, high)]
            below = [jnp.where(keep_low, value, 0.0) for value in turned]
            above = [jnp.where(keep_high, value, 0.0) for value in turned]
        else:
            below = shifted(high, up, axis, keep_low)
            above = shifted(low, down, axis, keep_high)
        jump_low = [a - b for a, b in zip(low, below)]
        jump_high = [a - b for a, b in zip(high, above)]
        return coupled(jump_low, direction, -1.0, scale), coupled(jump_high, direction, 1.0, scale)

    def line(direction, nodes):
        q = [[load(f, n) for n in nodes] for f in range(FIELDS)]
        ends = face_terms(direction, [x[0] for x in q], [x[4] for x in q])
        g, u, e = q[0], q[1], q[4]
        if direction == 0:
            mixed = [(2.0 * MACH) * g[k] + (1.0 - MACH**2) * u[k] for k in range(5)]
            parts = {
                0: differentiate(mixed, scale),
                1: differentiate(g, scale),
                4: differentiate(e, scale * MACH),
            }
        else:
            parts = {
                0: differentiate(q[direction + 1], scale),
                direction + 1: differentiate(g, scale),
            }
        values = []
        for f in range(FIELDS):
            row = list(parts[f]) if f in parts else [None] * 5
            for k, end in ((0, ends[0][f]), (4, ends[1][f])):
                row[k] = end if row[k] is None else row[k] + end
            values.append(row)
        store(direction, nodes, values, q)

    strides = ((25, 5, 1), (5, 25, 1), (1, 25, 5))
    for direction, (step, outer_step, inner_step) in enumerate(strides):

        def lines(outer):
            for inner in range(5):
                first = outer * outer_step + inner * inner_step
                line(direction, [first + k * step for k in range(5)])

        if unroll:
            for outer in range(5):
                lines(outer)
        else:
            pl.loop(0, 5)(lines)


def volume_first_kernel(scale, state_ref, out_ref):
    volume_into(state_ref, scale, add_to(out_ref))


def add_to(out_ref):
    def store(direction, nodes, values, q):
        for f in range(FIELDS):
            for node, value in zip(nodes, values[f]):
                at = f * NODES + node
                if direction == 0:
                    out_ref[at] = jnp.zeros_like(q[0][0]) if value is None else value
                elif value is not None:
                    out_ref[at] += value

    return store


def volume_kernel(scale, state_ref, sum_in, out_ref, sum_ref):
    add = add_to(out_ref)

    def store(direction, nodes, values, q):
        add(direction, nodes, values, q)
        if direction == 2:
            for f in range(FIELDS):
                for node, value in zip(nodes, q[f]):
                    at = f * NODES + node
                    sum_ref[at] = sum_in[at] + value

    volume_into(state_ref, scale, store)


def volume_and_source_kernel(
    scale, state_ref, sum_in, source_ref, out_ref, sum_ref, out_hbm, sem
):
    rows = pl.ds(0, out_hbm.shape[0])
    copy = pltpu.make_async_copy(source_ref.at[rows], out_hbm, sem.at[0])
    copy.start()
    volume_kernel(scale, state_ref, sum_in, out_ref, sum_ref)
    copy.wait()


def volume_last_kernel(scale, state_ref, sum_in, sum_ref, out_ref):
    add = add_to(out_ref)

    def store(direction, nodes, values, q):
        if direction < 2:
            add(direction, nodes, values, q)
            return
        for k, node in enumerate(nodes):
            totals = []
            for f in range(FIELDS):
                at = f * NODES + node
                total = sum_in[at] + q[f][k] + out_ref[at]
                totals.append(total if values[f][k] is None else total + values[f][k])
            for f, total in enumerate(original(totals)):
                sum_ref[f * NODES + node] = total

    volume_into(state_ref, scale, store, unroll=True)


def on_parity(axis, even, odd):
    parity = lax.axis_index(axis) % 2
    pl.when(parity == 0)(even)
    pl.when(parity == 1)(odd)


def five(ref, f, at):
    return (pl.ds(f * NODES + at, 5),) if len(ref.shape) == 3 else (f, at // 25, pl.ds(at % 25, 5))


def received(ref, start):
    return [ref[pl.ds(f * 25 + start, 5)].astype(jnp.float32) for f in range(FIELDS)]


def add_ax(out_ref, face, high, weight, final):
    first, rows = (100, slice(4, 8)) if high else (0, slice(0, 4))
    for chunk in range(5):
        terms = coupled(received(face, chunk * 5), 0, 1.0 if high else -1.0, -weight)
        terms = original(terms) if final else terms
        for f, term in enumerate(terms):
            out_ref[*five(out_ref, f, first + chunk * 5), rows, :] += term


def add_far(out_ref, face, weight, final=False):
    on_parity(
        "ax",
        lambda: add_ax(out_ref, face, False, weight, final),
        lambda: add_ax(out_ref, face, True, weight, final),
    )


def add_near(out_ref, face, weight, final=False):
    on_parity(
        "ax",
        lambda: add_ax(out_ref, face, True, weight, final),
        lambda: add_ax(out_ref, face, False, weight, final),
    )


def add_az(out_ref, far, near, weight, final=False):
    row = lax.broadcasted_iota(jnp.int32, (5, ROWS, LANES), 1)

    def add_side(face, at, rows, chunk, normal):
        terms = coupled(received(face, chunk), 1, normal, -weight)
        for f, term in enumerate(original(terms) if final else terms):
            spread = jnp.where(row == rows[1], term[:, 1:2], 0.0)
            out_ref[*five(out_ref, f, at)] += jnp.where(row == rows[0], term[:, 0:1], spread)

    def add(low, high):
        for a in range(5):
            add_side(low, a * 25, (0, 4), a * 5, -1.0)
            add_side(high, a * 25 + 20, (3, 7), a * 5, 1.0)

    on_parity("az", lambda: add(far, near), lambda: add(near, far))


def pack_ax(state_ref, face, high):
    first, rows = (100, slice(4, 8)) if high else (0, slice(0, 4))
    for f in range(FIELDS):
        face[pl.ds(f * 25, 25)] = state_ref[pl.ds(f * NODES + first, 25), rows, :].astype(
            jnp.bfloat16
        )


def pack_far(state_ref, face):
    on_parity("ax", lambda: pack_ax(state_ref, face, False), lambda: pack_ax(state_ref, face, True))


def pack_near(state_ref, face):
    on_parity("ax", lambda: pack_ax(state_ref, face, True), lambda: pack_ax(state_ref, face, False))


def pack_az(state_ref, far, near):
    def pack(az_low, az_high):
        for f in range(FIELDS):
            for a in range(5):
                at, to = f * NODES + a * 25, pl.ds((f * 5 + a) * 5, 5)
                low = [state_ref[pl.ds(at, 5), k : k + 1, :] for k in (0, 4)]
                high = [state_ref[pl.ds(at + 20, 5), k : k + 1, :] for k in (3, 7)]
                az_low[to] = jnp.concatenate(low, axis=1).astype(jnp.bfloat16)
                az_high[to] = jnp.concatenate(high, axis=1).astype(jnp.bfloat16)

    on_parity("az", lambda: pack(far, near), lambda: pack(near, far))


def load_kernel(state_hbm, state_ref, far, near, az_far, az_near, sems):
    copies = []
    for f in range(FIELDS):
        nodes = pl.ds(f * NODES, NODES)
        copy = pltpu.make_async_copy(state_hbm.at[nodes], state_ref.at[nodes], sems.at[f])
        copy.start()
        copies.append(copy)
    for copy in copies:
        copy.wait()

    @pl.loop(0, NODES // 5)
    def _(chunk):
        for k in range(5):
            node = chunk * 5 + k
            p = state_ref[node]
            state_ref[node] = p + MACH * state_ref[NODES + node]
            state_ref[4 * NODES + node] -= p

    pack_faces(state_ref, far, near, az_far, az_near)


def pack_faces(state_ref, far, near, az_far, az_near):
    pack_far(state_ref, far)
    pack_near(state_ref, near)
    pack_az(state_ref, az_far, az_near)


def add_source(state_ref, source_ref, scale, nodes):
    for node in nodes:
        for c in range(3):
            value = scale * source_ref[pl.ds((c * NODES + node) * ROWS, ROWS), :]
            state_ref[(c + 1) * NODES + node] += value
            if c == 0:
                state_ref[node] += MACH * value


def first_az_kernel(scale, state_in, az_far, az_near, state_ref):
    add_az(state_ref, az_far, az_near, scale)


def first_far_kernel(scale, state_in, source_ref, far, state_ref, far_out):
    add_far(state_ref, far, scale)
    add_source(state_ref, source_ref, scale, [*range(25), *range(100, NODES)])
    pack_far(state_ref, far_out)


def first_near_kernel(scale, state_in, source_ref, near, state_ref, near_out, *az_out):
    add_near(state_ref, near, scale)
    add_source(state_ref, source_ref, scale, range(25, 100))
    pack_near(state_ref, near_out)
    pack_az(state_ref, *az_out)


def finish_far_kernel(scale, state_in, far, az_far, az_near, state_ref, far_out):
    add_az(state_ref, az_far, az_near, scale)
    add_far(state_ref, far, scale)
    pack_far(state_ref, far_out)


def finish_near_kernel(scale, state_in, near, state_ref, near_out, az_far_out, az_near_out):
    add_near(state_ref, near, scale)
    pack_near(state_ref, near_out)
    pack_az(state_ref, az_far_out, az_near_out)


def last_far_kernel(weight, state_in, far, az_far, az_near, state_ref, out_hbm, sems):
    far_plane = 4 * (lax.axis_index("ax") % 2)

    def copy(k, plane, nodes):
        part = (slice(None), plane, nodes)
        return pltpu.make_async_copy(state_ref.at[*part], out_hbm.at[*part], sems.at[k])

    inside = [copy(k, plane, pl.ds(5, 15)) for k, plane in enumerate((1, 2, 3))]
    for part in inside:
        part.start()
    add_az(state_ref, az_far, az_near, weight, final=True)
    outside = [copy(3 + k, k + 1, pl.ds(0, 5)) for k in range(3)]
    outside += [copy(6 + k, k + 1, pl.ds(20, 5)) for k in range(3)]
    for part in outside:
        part.start()
    add_far(state_ref, far, weight, final=True)
    face = copy(9, far_plane, pl.ds(0, 25))
    face.start()
    for part in inside + outside + [face]:
        part.wait()


def last_near_kernel(weight, state_in, out_in, near, state_ref, out_hbm, sem):
    add_near(state_ref, near, weight, final=True)
    part = (slice(None), 4 - 4 * (lax.axis_index("ax") % 2))
    copy = pltpu.make_async_copy(state_ref.at[*part], out_hbm.at[*part], sem.at[0])
    copy.start()
    copy.wait()


def contribution_kernel(
    capacity,
    devices,
    lamb_hbm,
    owner_hbm,
    element_hbm,
    class_hbm,
    tables_hbm,
    out_hbm,
    lamb_ref,
    owner_ref,
    rows_ref,
    tables_ref,
    out_ref,
    row_sems,
    tables_sem,
    lamb_sem,
    out_sems,
):
    flow = lamb_ref.shape[1]
    slots = devices * capacity
    row_copies = [
        pltpu.make_async_copy(owner_hbm, owner_ref, row_sems.at[0]),
        pltpu.make_async_copy(element_hbm, rows_ref.at[0], row_sems.at[1]),
        pltpu.make_async_copy(class_hbm, rows_ref.at[1], row_sems.at[2]),
    ]
    lamb_copy = pltpu.make_async_copy(lamb_hbm, lamb_ref, lamb_sem.at[0])
    tables_copy = pltpu.make_async_copy(
        tables_hbm, tables_ref.at[pl.ds(0, NODES)], tables_sem.at[0]
    )
    for copy in row_copies + [tables_copy, lamb_copy]:
        copy.start()
    for copy in row_copies:
        copy.wait()

    tables_ref[pl.ds(NODES, LANES - NODES)] = jnp.zeros(
        (LANES - NODES,) + tables_ref.shape[1:], jnp.bfloat16
    )
    owner_row = owner_ref[...]
    rows = jnp.concatenate(
        [rows_ref[0], rows_ref[1], jnp.zeros((ROWS - 2, flow), jnp.int32)], axis=0
    )
    columns = jnp.transpose(rows.astype(jnp.float32))
    element = columns[:, 0:1]
    second = columns[:, 1:2]

    owned = (lax.broadcasted_iota(jnp.int32, (devices, flow), 0) == owner_row).astype(jnp.float32)
    earlier = lax.broadcasted_iota(jnp.int32, (flow, flow), 0) < lax.broadcasted_iota(
        jnp.int32, (flow, flow), 1
    )
    running = jnp.dot(
        owned.astype(jnp.bfloat16),
        earlier.astype(jnp.bfloat16),
        preferred_element_type=jnp.float32,
    )
    position = jnp.sum(running * owned, axis=0, keepdims=True).astype(jnp.int32)
    slot_row = owner_row * capacity + position
    placing = (lax.broadcasted_iota(jnp.int32, (slots, flow), 0) == slot_row).astype(jnp.bfloat16)

    tables_copy.wait()
    tables = jnp.concatenate([tables_ref[:, 0, :], tables_ref[:, 1, :]], axis=0)
    lamb_copy.wait()
    both = lax.dot_general(
        lamb_ref[...].reshape(3 * flow, lamb_ref.shape[2]),
        tables,
        (((1,), (1,)), ((), ())),
        preferred_element_type=jnp.float32,
    )
    use_second = jnp.broadcast_to(second, (flow, LANES)) > 0.5
    values = [
        jnp.where(
            use_second, both[c * flow : (c + 1) * flow, LANES:], both[c * flow : (c + 1) * flow, :LANES]
        )
        for c in range(3)
    ]
    largest = jnp.maximum(jnp.maximum(jnp.abs(values[0]), jnp.abs(values[1])), jnp.abs(values[2]))
    largest = jnp.max(largest, axis=1, keepdims=True)
    exponent = jnp.clip(jnp.ceil(jnp.log2(jnp.maximum(largest, 1e-36))), -100.0, 30.0)
    scale = jnp.broadcast_to(jnp.exp2(14.0 - exponent), (flow, LANES))
    column = lax.broadcasted_iota(jnp.int32, (flow, LANES), 1)
    out_copies = []
    for c in range(3):
        whole = jnp.round(values[c] * scale)
        if c == 0:
            whole = jnp.where(column == NODES, exponent, whole)
            whole = jnp.where(column == NODES + 1, element, whole)
        high = jnp.floor(whole * (1.0 / 256.0))
        low = whole - 256.0 * high
        pieces = jnp.concatenate([high, low], axis=1).astype(jnp.bfloat16)
        placed = jnp.dot(placing, pieces, preferred_element_type=jnp.float32)
        placed = placed[:, :LANES] * 256.0 + placed[:, LANES:]
        out_ref[c] = placed.astype(jnp.int32).astype(jnp.int16)
        copy = pltpu.make_async_copy(
            out_ref.at[c], out_hbm.at[:, pl.ds(c * LANES, LANES)], out_sems.at[c]
        )
        copy.start()
        out_copies.append(copy)
    for copy in out_copies:
        copy.wait()


def source_kernel(received_ref, source_ref):
    slots = received_ref.shape[0]
    wide = 2 * LANES
    highs, lows = [], []
    for c in range(3):
        values = received_ref[:, pl.ds(c * LANES, LANES)].astype(jnp.int32).astype(jnp.float32)
        if c == 0:
            element = values[:, NODES + 1 : NODES + 2].astype(jnp.int32)
        values = jnp.transpose(values)
        if c == 0:
            scale = jnp.exp2(values[NODES : NODES + 1, :] - 14.0)
        values = values * scale
        high = values.astype(jnp.bfloat16)
        highs.append(high)
        lows.append((values - high.astype(jnp.float32)).astype(jnp.bfloat16))
    parts = jnp.concatenate(highs + lows, axis=0)
    column = lax.broadcasted_iota(jnp.int32, (slots, wide), 1)
    for group in range(ROWS // 2):
        member = (element == column + group * wide).astype(jnp.bfloat16)
        total = jnp.dot(parts, member, preferred_element_type=jnp.float32)
        total = total[0 : 3 * LANES] + total[3 * LANES :]
        for c in range(3):
            for k in range(2):
                start = c * NODES * ROWS + group * 2 + k
                source_ref[pl.ds(start, LANES, stride=ROWS), :] = total[
                    c * LANES : (c + 1) * LANES, k * LANES : (k + 1) * LANES
                ]

STATE = (FIELDS * NODES, ROWS, LANES)
AX_FACE = (FIELDS * 25, 4, LANES)
AZ_FACE = (FIELDS * 25, 2, LANES)


LONG = pl.CostEstimate(flops=10**11, bytes_accessed=10**9, transcendentals=0)
IN_VMEM = pl.BlockSpec(memory_space=pltpu.VMEM)
IN_HBM = pl.BlockSpec(memory_space=pltpu.HBM)


def in_hbm(x):
    return pltpu.with_memory_space_constraint(x, pltpu.HBM)


def call(kernel, out_shape, in_specs, out_specs=IN_VMEM, aliases=None, scratch=(), cost=None):
    if not isinstance(out_specs, list):
        out_specs = jax.tree.map(lambda _: out_specs, out_shape)
    return pl.pallas_call(
        kernel,
        out_shape=out_shape,
        in_specs=in_specs if isinstance(in_specs, list) else [IN_VMEM] * in_specs,
        out_specs=out_specs,
        scratch_shapes=scratch,
        input_output_aliases=aliases or {},
        cost_estimate=cost,
        compiler_params=pltpu.CompilerParams(vmem_limit_bytes=VMEM_BYTES),
    )


def swap(far, near):
    count = lax.axis_size("ax")
    pairs = ([], [])
    for i in range(count - 1):
        pairs[i % 2].extend([(i, i + 1), (i + 1, i)])
    return (
        None if far is None else lax.ppermute(far, "ax", pairs[1]),
        None if near is None else lax.ppermute(near, "ax", pairs[0]),
    )


def turn(far, near):
    count = lax.axis_size("az")
    pairs = ([], [])
    for i in range(count):
        pairs[i % 2].extend([(i, (i + 1) % count), ((i + 1) % count, i)])
    return lax.ppermute(far, "az", pairs[1]), lax.ppermute(near, "az", pairs[0])


def body(lamb_vector, owner, element, shape_class, interp_tables, acoustic_state):
    devices = lax.axis_size("ax") * lax.axis_size("az")
    flow, _, points = lamb_vector.shape
    capacity = max(2, 3 * flow // devices)
    slots = devices * capacity
    f32, bf16 = jnp.float32, jnp.bfloat16

    state = acoustic_state.reshape(STATE)
    face_shapes = [jax.ShapeDtypeStruct(s, bf16) for s in (AX_FACE, AX_FACE, AZ_FACE, AZ_FACE)]
    vmem_state = pltpu.VMEM(STATE, f32)
    source_shape = (3 * NODES * ROWS, LANES)

    buffer = call(
        functools.partial(contribution_kernel, capacity, devices),
        pltpu.HBM((slots, 3 * LANES), jnp.int16),
        [IN_HBM] * 5,
        IN_HBM,
        scratch=[
            pltpu.VMEM((3, flow, points), bf16),
            pltpu.VMEM((1, flow), jnp.int32),
            pltpu.VMEM((2, 1, flow), jnp.int32),
            pltpu.VMEM((LANES, 2, points), bf16),
            pltpu.VMEM((3, slots, LANES), jnp.int16),
            pltpu.SemaphoreType.DMA((3,)),
            pltpu.SemaphoreType.DMA((1,)),
            pltpu.SemaphoreType.DMA((1,)),
            pltpu.SemaphoreType.DMA((3,)),
        ],
    )(
        in_hbm(jnp.transpose(lamb_vector, (1, 0, 2))),
        in_hbm(owner.reshape(1, flow)),
        in_hbm(element.reshape(1, flow)),
        in_hbm(shape_class.reshape(1, flow)),
        in_hbm(jnp.transpose(interp_tables, (2, 0, 1))),
    )
    routed = lax.all_to_all(buffer, ("ax", "az"), split_axis=0, concat_axis=0, tiled=True)

    state, far, near, az_far, az_near = call(
        load_kernel,
        [vmem_state] + face_shapes,
        [IN_HBM],
        scratch=[pltpu.SemaphoreType.DMA((FIELDS,))],
    )(in_hbm(state))
    far, near = swap(far, near)
    az_far, az_near = turn(az_far, az_near)
    moved = call(functools.partial(volume_first_kernel, STEP_SCALES[0]), vmem_state, 1)(state)
    moved = call(
        functools.partial(first_az_kernel, STEP_SCALES[0]), vmem_state, 3, aliases={0: 0}
    )(moved, az_far, az_near)
    source_rows = 3 * NODES * ROWS + 3 * ROWS
    source = call(source_kernel, pltpu.VMEM((source_rows, LANES), f32), 1)(routed)
    rate, far = call(
        functools.partial(first_far_kernel, STEP_SCALES[0]),
        [vmem_state, face_shapes[0]],
        3,
        aliases={0: 0},
    )(moved, source, far)
    far, _ = swap(far, None)
    rate, near, az_far, az_near = call(
        functools.partial(first_near_kernel, STEP_SCALES[0]),
        [vmem_state] + face_shapes[1:],
        3,
        aliases={0: 0},
    )(rate, source, near)
    _, near = swap(None, near)
    az_far, az_near = turn(az_far, az_near)
    moved, total, source = call(
        functools.partial(volume_and_source_kernel, STEP_SCALES[1]),
        [vmem_state, vmem_state, pltpu.HBM(source_shape, f32)],
        3,
        [IN_VMEM, IN_VMEM, IN_HBM],
        scratch=[pltpu.SemaphoreType.DMA((1,))],
    )(rate, state, source)

    for scale in STEP_SCALES[1:3]:
        rate, far = call(
            functools.partial(finish_far_kernel, scale),
            [vmem_state, face_shapes[0]],
            4,
            aliases={0: 0},
            cost=LONG,
        )(moved, far, az_far, az_near)
        far, _ = swap(far, None)
        rate, near, az_far, az_near = call(
            functools.partial(finish_near_kernel, scale),
            [vmem_state] + face_shapes[1:],
            2,
            aliases={0: 0},
        )(rate, near)
        _, near = swap(None, near)
        az_far, az_near = turn(az_far, az_near)
        if scale == STEP_SCALES[1]:
            moved, total = call(
                functools.partial(volume_kernel, STEP_SCALES[2]), [vmem_state, vmem_state], 2
            )(rate, total)

    total = call(
        functools.partial(volume_last_kernel, STEP_SCALES[3]),
        vmem_state,
        2,
        scratch=[pltpu.VMEM(STATE, f32)],
    )(rate, total)
    planes = (FIELDS, 5, 25, ROWS, LANES)
    vmem_planes, hbm_planes = pltpu.VMEM(planes, f32), pltpu.HBM(planes, f32)
    total, partial = call(
        functools.partial(last_far_kernel, STEP_SCALES[3]),
        [vmem_planes, hbm_planes],
        4,
        [IN_VMEM, IN_HBM],
        aliases={0: 0},
        cost=LONG,
        scratch=[pltpu.SemaphoreType.DMA((10,))],
    )(total.reshape(planes), far, az_far, az_near)
    _, new_state = call(
        functools.partial(last_near_kernel, STEP_SCALES[3]),
        [vmem_planes, hbm_planes],
        [IN_VMEM, IN_HBM, IN_VMEM],
        [IN_VMEM, IN_HBM],
        aliases={0: 0, 1: 1},
        scratch=[pltpu.SemaphoreType.DMA((1,))],
    )(total, partial, near)
    shape = acoustic_state.shape
    return new_state.reshape(shape), source.reshape((3,) + shape[1:])


def solution(mesh):
    in_specs = (
        P(("ax", "az"), None, None),
        P(("ax", "az"), None),
        P(("ax", "az")),
        P(("ax", "az")),
        P(),
        P(None, None, "ax", "az", None),
    )
    out_specs = (P(None, None, "ax", "az", None), P(None, None, "ax", "az", None))
    return jax.shard_map(body, mesh=mesh, in_specs=in_specs, out_specs=out_specs, check_vma=False)
```

```python
import functools
import math

import jax
import jax.numpy as jnp
import numpy as np
from jax import lax
from jax.experimental import pallas as pl
from jax.experimental.pallas import tpu as pltpu
from jax.sharding import PartitionSpec as P

MACH = 0.3
RUSANOV = 1.3
DT = 0.03
LIFT = 10.0
VOLUME = 2.0
STEP_SCALES = (DT, DT / 2.0, DT / 3.0, DT / 4.0)

FIELDS = 5
NODES = 125
ROWS = 8
LANES = 128
VMEM_BYTES = 24 * 1024 * 1024


def derivative_matrix():
    points = np.array([-1.0, -math.sqrt(3.0 / 7.0), 0.0, math.sqrt(3.0 / 7.0), 1.0])
    weights = [1.0 / np.prod([points[j] - points[k] for k in range(5) if k != j]) for j in range(5)]
    matrix = np.zeros((5, 5))
    for i in range(5):
        for j in range(5):
            if i != j:
                matrix[i, j] = weights[j] / weights[i] / (points[i] - points[j])
        matrix[i, i] = -np.sum(matrix[i])
    return matrix


DERIVATIVE = -VOLUME * derivative_matrix()


def differentiate(g, scale):
    d = [[float(scale * v) for v in row] for row in DERIVATIVE]
    even_out, odd_out = g[0] - g[4], g[1] - g[3]
    s_out, s_in = g[0] + g[4], g[1] + g[3]
    results = [None] * 5
    for i in (0, 1):
        same = (d[i][0] - d[i][4]) / 2 * even_out + (d[i][1] - d[i][3]) / 2 * odd_out
        flip = (d[i][0] + d[i][4]) / 2 * s_out + (d[i][1] + d[i][3]) / 2 * s_in + d[i][2] * g[2]
        results[i] = same + flip
        results[4 - i] = same - flip
    results[2] = d[2][0] * even_out + d[2][1] * odd_out
    return results


def original(q):
    g, u, v, w, e = q
    p = g - MACH * u
    return [p, u, v, w, e + p]


def coupled(jump, direction, normal, scale):
    g, u, v, w, e = jump
    rusanov, lift = scale * LIFT * RUSANOV, scale * LIFT * normal
    if direction == 0:
        return [
            (2.0 * MACH * lift - rusanov) * g + ((1.0 - MACH**2) * lift) * u,
            lift * g - rusanov * u,
            -rusanov * v,
            -rusanov * w,
            (MACH * lift - rusanov) * e,
        ]
    normal_velocity = (v, w)[direction - 1]
    along = lift * g - rusanov * normal_velocity
    return [
        lift * normal_velocity - rusanov * g,
        -rusanov * u,
        along if direction == 1 else -rusanov * v,
        along if direction == 2 else -rusanov * w,
        -rusanov * e,
    ]


def shifted(q, amount, axis, keep):
    return [jnp.where(keep, pltpu.roll(value, amount, axis), 0.0) for value in q]


def volume_into(state_ref, scale, store):
    row = lax.broadcasted_iota(jnp.int32, (ROWS, LANES), 0)
    lane = lax.broadcasted_iota(jnp.int32, (ROWS, LANES), 1)
    cell = row % 4
    keep = {
        0: (row >= 4, row < 4),
        1: (cell != 0, cell != 3),
        2: (lane != 0, lane != LANES - 1),
    }
    rolls = {0: (4, 4, 0), 1: (1, ROWS - 1, 0), 2: (1, LANES - 1, 1)}

    def load(field, node):
        return state_ref[field * NODES + node]

    def face_terms(direction, low, high):
        up, down, axis = rolls[direction]
        keep_low, keep_high = keep[direction]
        if direction == 0:
            turned = [pltpu.roll(jnp.where(keep_high, b, a), up, axis) for a, b in zip(low, high)]
            below = [jnp.where(keep_low, value, 0.0) for value in turned]
            above = [jnp.where(keep_high, value, 0.0) for value in turned]
        else:
            below = shifted(high, up, axis, keep_low)
            above = shifted(low, down, axis, keep_high)
        jump_low = [a - b for a, b in zip(low, below)]
        jump_high = [a - b for a, b in zip(high, above)]
        return coupled(jump_low, direction, -1.0, scale), coupled(jump_high, direction, 1.0, scale)

    def line(direction, nodes):
        q = [[load(f, n) for n in nodes] for f in range(FIELDS)]
        ends = face_terms(direction, [x[0] for x in q], [x[4] for x in q])
        g, u, e = q[0], q[1], q[4]
        if direction == 0:
            mixed = [(2.0 * MACH) * g[k] + (1.0 - MACH**2) * u[k] for k in range(5)]
            parts = {
                0: differentiate(mixed, scale),
                1: differentiate(g, scale),
                4: differentiate(e, scale * MACH),
            }
        else:
            parts = {
                0: differentiate(q[direction + 1], scale),
                direction + 1: differentiate(g, scale),
            }
        values = []
        for f in range(FIELDS):
            row = list(parts[f]) if f in parts else [None] * 5
            for k, end in ((0, ends[0][f]), (4, ends[1][f])):
                row[k] = end if row[k] is None else row[k] + end
            values.append(row)
        store(direction, nodes, values, q)

    @pl.loop(0, 5)
    def _(outer):
        for inner in range(5):
            line(0, [k * 25 + outer * 5 + inner for k in range(5)])

    @pl.loop(0, 5)
    def _(outer):
        for inner in range(5):
            line(1, [outer * 25 + k * 5 + inner for k in range(5)])

    @pl.loop(0, 5)
    def _(outer):
        for inner in range(5):
            line(2, [outer * 25 + inner * 5 + k for k in range(5)])


def volume_first_kernel(scale, state_ref, out_ref):
    volume_into(state_ref, scale, add_to(out_ref))


def add_to(out_ref):
    def store(direction, nodes, values, q):
        for f in range(FIELDS):
            for node, value in zip(nodes, values[f]):
                at = f * NODES + node
                if direction == 0:
                    out_ref[at] = jnp.zeros_like(q[0][0]) if value is None else value
                elif value is not None:
                    out_ref[at] += value

    return store


def volume_kernel(scale, state_ref, sum_in, out_ref, sum_ref):
    add = add_to(out_ref)

    def store(direction, nodes, values, q):
        add(direction, nodes, values, q)
        if direction == 2:
            for f in range(FIELDS):
                for node, value in zip(nodes, q[f]):
                    at = f * NODES + node
                    sum_ref[at] = sum_in[at] + value

    volume_into(state_ref, scale, store)


def volume_and_source_kernel(
    scale, state_in, sum_in, source_ref, state_ref, out_ref, sum_ref, out_hbm, sem
):
    rows = pl.ds(0, out_hbm.shape[0])
    copy = pltpu.make_async_copy(source_ref.at[rows], out_hbm, sem.at[0])
    copy.start()
    add_source(state_ref, source_ref, STEP_SCALES[0], INNER)
    volume_kernel(scale, state_ref, sum_in, out_ref, sum_ref)
    copy.wait()


def volume_last_kernel(scale, state_ref, sum_in, sum_ref, out_ref):
    add = add_to(out_ref)

    def store(direction, nodes, values, q):
        if direction < 2:
            add(direction, nodes, values, q)
            return
        for k, node in enumerate(nodes):
            totals = []
            for f in range(FIELDS):
                at = f * NODES + node
                total = sum_in[at] + q[f][k] + out_ref[at]
                totals.append(total if values[f][k] is None else total + values[f][k])
            for f, total in enumerate(original(totals)):
                sum_ref[f * NODES + node] = total

    volume_into(state_ref, scale, store)


def on_parity(axis, even, odd):
    parity = lax.axis_index(axis) % 2
    pl.when(parity == 0)(even)
    pl.when(parity == 1)(odd)


def five(ref, f, at):
    return (pl.ds(f * NODES + at, 5),) if len(ref.shape) == 3 else (f, at // 25, pl.ds(at % 25, 5))


def received(ref, start):
    return [ref[pl.ds(f * 25 + start, 5)].astype(jnp.float32) for f in range(FIELDS)]


def add_ax(out_ref, face, high, weight, final):
    first, rows = (100, slice(4, 8)) if high else (0, slice(0, 4))
    for chunk in range(5):
        terms = coupled(received(face, chunk * 5), 0, 1.0 if high else -1.0, -weight)
        terms = original(terms) if final else terms
        for f, term in enumerate(terms):
            out_ref[*five(out_ref, f, first + chunk * 5), rows, :] += term


def add_far(out_ref, face, weight, final=False):
    on_parity(
        "ax",
        lambda: add_ax(out_ref, face, False, weight, final),
        lambda: add_ax(out_ref, face, True, weight, final),
    )


def add_near(out_ref, face, weight, final=False):
    on_parity(
        "ax",
        lambda: add_ax(out_ref, face, True, weight, final),
        lambda: add_ax(out_ref, face, False, weight, final),
    )


def add_az(out_ref, far, near, weight, final=False):
    row = lax.broadcasted_iota(jnp.int32, (5, ROWS, LANES), 1)

    def add_side(face, at, rows, chunk, normal):
        terms = coupled(received(face, chunk), 1, normal, -weight)
        for f, term in enumerate(original(terms) if final else terms):
            spread = jnp.where(row == rows[1], term[:, 1:2], 0.0)
            out_ref[*five(out_ref, f, at)] += jnp.where(row == rows[0], term[:, 0:1], spread)

    def add(low, high):
        for a in range(5):
            add_side(low, a * 25, (0, 4), a * 5, -1.0)
            add_side(high, a * 25 + 20, (3, 7), a * 5, 1.0)

    on_parity("az", lambda: add(far, near), lambda: add(near, far))


def pack_ax(state_ref, face, high):
    first, rows = (100, slice(4, 8)) if high else (0, slice(0, 4))
    for f in range(FIELDS):
        face[pl.ds(f * 25, 25)] = state_ref[pl.ds(f * NODES + first, 25), rows, :].astype(
            jnp.bfloat16
        )


def pack_far(state_ref, face):
    on_parity("ax", lambda: pack_ax(state_ref, face, False), lambda: pack_ax(state_ref, face, True))


def pack_near(state_ref, face):
    on_parity("ax", lambda: pack_ax(state_ref, face, True), lambda: pack_ax(state_ref, face, False))


def pack_az(state_ref, far, near):
    def pack(az_low, az_high):
        for f in range(FIELDS):
            for a in range(5):
                at, to = f * NODES + a * 25, pl.ds((f * 5 + a) * 5, 5)
                low = [state_ref[pl.ds(at, 5), k : k + 1, :] for k in (0, 4)]
                high = [state_ref[pl.ds(at + 20, 5), k : k + 1, :] for k in (3, 7)]
                az_low[to] = jnp.concatenate(low, axis=1).astype(jnp.bfloat16)
                az_high[to] = jnp.concatenate(high, axis=1).astype(jnp.bfloat16)

    on_parity("az", lambda: pack(far, near), lambda: pack(near, far))


def load_kernel(state_hbm, state_ref, far, near, az_far, az_near, sems):
    copies = []
    for f in range(FIELDS):
        nodes = pl.ds(f * NODES, NODES)
        copy = pltpu.make_async_copy(state_hbm.at[nodes], state_ref.at[nodes], sems.at[f])
        copy.start()
        copies.append(copy)
    for copy in copies:
        copy.wait()

    @pl.loop(0, NODES // 5)
    def _(chunk):
        for k in range(5):
            node = chunk * 5 + k
            p = state_ref[node]
            state_ref[node] = p + MACH * state_ref[NODES + node]
            state_ref[4 * NODES + node] -= p

    pack_faces(state_ref, far, near, az_far, az_near)


def pack_faces(state_ref, far, near, az_far, az_near):
    pack_far(state_ref, far)
    pack_near(state_ref, near)
    pack_az(state_ref, az_far, az_near)


INNER = [a * 25 + n for a in (1, 2, 3) for n in range(5, 20)]


def add_source(state_ref, source_ref, scale, nodes):
    for node in nodes:
        for c in range(3):
            value = scale * source_ref[pl.ds((c * NODES + node) * ROWS, ROWS), :]
            state_ref[(c + 1) * NODES + node] += value
            if c == 0:
                state_ref[node] += MACH * value


def first_az_kernel(scale, state_in, az_far, az_near, state_ref):
    add_az(state_ref, az_far, az_near, scale)


def first_far_kernel(scale, state_in, source_ref, far, state_ref, far_out):
    add_far(state_ref, far, scale)
    add_source(state_ref, source_ref, scale, [*range(25), *range(100, NODES)])
    pack_far(state_ref, far_out)


def first_near_kernel(scale, state_in, source_ref, near, state_ref, near_out, *az_out):
    add_near(state_ref, near, scale)
    add_source(state_ref, source_ref, scale, [n for n in range(25, 100) if n not in INNER])
    pack_near(state_ref, near_out)
    pack_az(state_ref, *az_out)


def finish_far_kernel(scale, state_in, far, az_far, az_near, state_ref, far_out):
    add_az(state_ref, az_far, az_near, scale)
    add_far(state_ref, far, scale)
    pack_far(state_ref, far_out)


def finish_near_kernel(scale, state_in, near, state_ref, near_out, az_far_out, az_near_out):
    add_near(state_ref, near, scale)
    pack_near(state_ref, near_out)
    pack_az(state_ref, az_far_out, az_near_out)


def last_far_kernel(weight, state_in, far, az_far, az_near, state_ref, out_hbm, sems):
    far_plane = 4 * (lax.axis_index("ax") % 2)

    def copy(k, plane, nodes):
        part = (slice(None), plane, nodes)
        return pltpu.make_async_copy(state_ref.at[*part], out_hbm.at[*part], sems.at[k])

    inside = [copy(k, plane, pl.ds(5, 15)) for k, plane in enumerate((1, 2, 3))]
    for part in inside:
        part.start()
    add_az(state_ref, az_far, az_near, weight, final=True)
    outside = [copy(3 + k, k + 1, pl.ds(0, 5)) for k in range(3)]
    outside += [copy(6 + k, k + 1, pl.ds(20, 5)) for k in range(3)]
    for part in outside:
        part.start()
    add_far(state_ref, far, weight, final=True)
    face = copy(9, far_plane, pl.ds(0, 25))
    face.start()
    for part in inside + outside + [face]:
        part.wait()


def last_near_kernel(weight, state_in, out_in, near, state_ref, out_hbm, sem):
    add_near(state_ref, near, weight, final=True)
    part = (slice(None), 4 - 4 * (lax.axis_index("ax") % 2))
    copy = pltpu.make_async_copy(state_ref.at[*part], out_hbm.at[*part], sem.at[0])
    copy.start()
    copy.wait()


def contribution_kernel(
    capacity,
    devices,
    lamb_hbm,
    owner_hbm,
    element_hbm,
    class_hbm,
    tables_hbm,
    out_hbm,
    lamb_ref,
    owner_ref,
    rows_ref,
    tables_ref,
    out_ref,
    row_sems,
    tables_sem,
    lamb_sem,
    out_sems,
):
    flow = lamb_ref.shape[1]
    slots = devices * capacity
    row_copies = [
        pltpu.make_async_copy(owner_hbm, owner_ref, row_sems.at[0]),
        pltpu.make_async_copy(element_hbm, rows_ref.at[0], row_sems.at[1]),
        pltpu.make_async_copy(class_hbm, rows_ref.at[1], row_sems.at[2]),
    ]
    lamb_copy = pltpu.make_async_copy(lamb_hbm, lamb_ref, lamb_sem.at[0])
    tables_copy = pltpu.make_async_copy(
        tables_hbm, tables_ref.at[pl.ds(0, NODES)], tables_sem.at[0]
    )
    for copy in row_copies + [tables_copy, lamb_copy]:
        copy.start()
    for copy in row_copies:
        copy.wait()

    tables_ref[pl.ds(NODES, LANES - NODES)] = jnp.zeros(
        (LANES - NODES,) + tables_ref.shape[1:], jnp.bfloat16
    )
    owner_row = owner_ref[...]
    rows = jnp.concatenate(
        [rows_ref[0], rows_ref[1], jnp.zeros((ROWS - 2, flow), jnp.int32)], axis=0
    )
    columns = jnp.transpose(rows.astype(jnp.float32))
    element = columns[:, 0:1]
    second = columns[:, 1:2]

    owned = (lax.broadcasted_iota(jnp.int32, (devices, flow), 0) == owner_row).astype(jnp.float32)
    earlier = lax.broadcasted_iota(jnp.int32, (flow, flow), 0) < lax.broadcasted_iota(
        jnp.int32, (flow, flow), 1
    )
    running = jnp.dot(
        owned.astype(jnp.bfloat16),
        earlier.astype(jnp.bfloat16),
        preferred_element_type=jnp.float32,
    )
    position = jnp.sum(running * owned, axis=0, keepdims=True).astype(jnp.int32)
    slot_row = owner_row * capacity + position
    placing = (lax.broadcasted_iota(jnp.int32, (slots, flow), 0) == slot_row).astype(jnp.bfloat16)

    tables_copy.wait()
    tables = jnp.concatenate([tables_ref[:, 0, :], tables_ref[:, 1, :]], axis=0)
    lamb_copy.wait()
    both = lax.dot_general(
        lamb_ref[...].reshape(3 * flow, lamb_ref.shape[2]),
        tables,
        (((1,), (1,)), ((), ())),
        preferred_element_type=jnp.float32,
    )
    use_second = jnp.broadcast_to(second, (flow, LANES)) > 0.5
    values = [
        jnp.where(
            use_second, both[c * flow : (c + 1) * flow, LANES:], both[c * flow : (c + 1) * flow, :LANES]
        )
        for c in range(3)
    ]
    largest = jnp.maximum(jnp.maximum(jnp.abs(values[0]), jnp.abs(values[1])), jnp.abs(values[2]))
    largest = jnp.max(largest, axis=1, keepdims=True)
    exponent = jnp.clip(jnp.ceil(jnp.log2(jnp.maximum(largest, 1e-36))), -100.0, 30.0)
    scale = jnp.broadcast_to(jnp.exp2(14.0 - exponent), (flow, LANES))
    column = lax.broadcasted_iota(jnp.int32, (flow, LANES), 1)
    out_copies = []
    for c in range(3):
        whole = jnp.round(values[c] * scale)
        if c == 0:
            whole = jnp.where(column == NODES, exponent, whole)
            whole = jnp.where(column == NODES + 1, element, whole)
        high = jnp.floor(whole * (1.0 / 256.0))
        low = whole - 256.0 * high
        pieces = jnp.concatenate([high, low], axis=1).astype(jnp.bfloat16)
        placed = jnp.dot(placing, pieces, preferred_element_type=jnp.float32)
        placed = placed[:, :LANES] * 256.0 + placed[:, LANES:]
        out_ref[c] = placed.astype(jnp.int32).astype(jnp.int16)
        copy = pltpu.make_async_copy(
            out_ref.at[c], out_hbm.at[:, pl.ds(c * LANES, LANES)], out_sems.at[c]
        )
        copy.start()
        out_copies.append(copy)
    for copy in out_copies:
        copy.wait()


def source_kernel(received_ref, source_ref):
    slots = received_ref.shape[0]
    wide = 2 * LANES
    highs, lows = [], []
    for c in range(3):
        values = received_ref[:, pl.ds(c * LANES, LANES)].astype(jnp.int32).astype(jnp.float32)
        if c == 0:
            element = values[:, NODES + 1 : NODES + 2].astype(jnp.int32)
        values = jnp.transpose(values)
        if c == 0:
            scale = jnp.exp2(values[NODES : NODES + 1, :] - 14.0)
        values = values * scale
        high = values.astype(jnp.bfloat16)
        highs.append(high)
        lows.append((values - high.astype(jnp.float32)).astype(jnp.bfloat16))
    parts = jnp.concatenate(highs + lows, axis=0)
    column = lax.broadcasted_iota(jnp.int32, (slots, wide), 1)
    for group in range(ROWS // 2):
        member = (element == column + group * wide).astype(jnp.bfloat16)
        total = jnp.dot(parts, member, preferred_element_type=jnp.float32)
        total = total[0 : 3 * LANES] + total[3 * LANES :]
        for c in range(3):
            for k in range(2):
                start = c * NODES * ROWS + group * 2 + k
                source_ref[pl.ds(start, LANES, stride=ROWS), :] = total[
                    c * LANES : (c + 1) * LANES, k * LANES : (k + 1) * LANES
                ]

STATE = (FIELDS * NODES, ROWS, LANES)
AX_FACE = (FIELDS * 25, 4, LANES)
AZ_FACE = (FIELDS * 25, 2, LANES)


LONG = pl.CostEstimate(flops=10**11, bytes_accessed=10**9, transcendentals=0)
IN_VMEM = pl.BlockSpec(memory_space=pltpu.VMEM)
IN_HBM = pl.BlockSpec(memory_space=pltpu.HBM)


def in_hbm(x):
    return pltpu.with_memory_space_constraint(x, pltpu.HBM)


def call(kernel, out_shape, in_specs, out_specs=IN_VMEM, aliases=None, scratch=(), cost=None):
    if not isinstance(out_specs, list):
        out_specs = jax.tree.map(lambda _: out_specs, out_shape)
    return pl.pallas_call(
        kernel,
        out_shape=out_shape,
        in_specs=in_specs if isinstance(in_specs, list) else [IN_VMEM] * in_specs,
        out_specs=out_specs,
        scratch_shapes=scratch,
        input_output_aliases=aliases or {},
        cost_estimate=cost,
        compiler_params=pltpu.CompilerParams(vmem_limit_bytes=VMEM_BYTES),
    )


def swap(far, near):
    count = lax.axis_size("ax")
    pairs = ([], [])
    for i in range(count - 1):
        pairs[i % 2].extend([(i, i + 1), (i + 1, i)])
    return (
        None if far is None else lax.ppermute(far, "ax", pairs[1]),
        None if near is None else lax.ppermute(near, "ax", pairs[0]),
    )


def turn(far, near):
    count = lax.axis_size("az")
    pairs = ([], [])
    for i in range(count):
        pairs[i % 2].extend([(i, (i + 1) % count), ((i + 1) % count, i)])
    return lax.ppermute(far, "az", pairs[1]), lax.ppermute(near, "az", pairs[0])


def body(lamb_vector, owner, element, shape_class, interp_tables, acoustic_state):
    devices = lax.axis_size("ax") * lax.axis_size("az")
    flow, _, points = lamb_vector.shape
    capacity = max(2, 3 * flow // devices)
    slots = devices * capacity
    f32, bf16 = jnp.float32, jnp.bfloat16

    state = acoustic_state.reshape(STATE)
    face_shapes = [jax.ShapeDtypeStruct(s, bf16) for s in (AX_FACE, AX_FACE, AZ_FACE, AZ_FACE)]
    vmem_state = pltpu.VMEM(STATE, f32)
    source_shape = (3 * NODES * ROWS, LANES)

    buffer = call(
        functools.partial(contribution_kernel, capacity, devices),
        pltpu.HBM((slots, 3 * LANES), jnp.int16),
        [IN_HBM] * 5,
        IN_HBM,
        scratch=[
            pltpu.VMEM((3, flow, points), bf16),
            pltpu.VMEM((1, flow), jnp.int32),
            pltpu.VMEM((2, 1, flow), jnp.int32),
            pltpu.VMEM((LANES, 2, points), bf16),
            pltpu.VMEM((3, slots, LANES), jnp.int16),
            pltpu.SemaphoreType.DMA((3,)),
            pltpu.SemaphoreType.DMA((1,)),
            pltpu.SemaphoreType.DMA((1,)),
            pltpu.SemaphoreType.DMA((3,)),
        ],
    )(
        in_hbm(jnp.transpose(lamb_vector, (1, 0, 2))),
        in_hbm(owner.reshape(1, flow)),
        in_hbm(element.reshape(1, flow)),
        in_hbm(shape_class.reshape(1, flow)),
        in_hbm(jnp.transpose(interp_tables, (2, 0, 1))),
    )
    routed = lax.all_to_all(buffer, ("ax", "az"), split_axis=0, concat_axis=0, tiled=True)

    state, far, near, az_far, az_near = call(
        load_kernel,
        [vmem_state] + face_shapes,
        [IN_HBM],
        scratch=[pltpu.SemaphoreType.DMA((FIELDS,))],
    )(in_hbm(state))
    far, near = swap(far, near)
    az_far, az_near = turn(az_far, az_near)
    moved = call(functools.partial(volume_first_kernel, STEP_SCALES[0]), vmem_state, 1)(state)
    moved = call(
        functools.partial(first_az_kernel, STEP_SCALES[0]), vmem_state, 3, aliases={0: 0}
    )(moved, az_far, az_near)
    source_rows = 3 * NODES * ROWS + 3 * ROWS
    source = call(source_kernel, pltpu.VMEM((source_rows, LANES), f32), 1)(routed)
    rate, far = call(
        functools.partial(first_far_kernel, STEP_SCALES[0]),
        [vmem_state, face_shapes[0]],
        3,
        aliases={0: 0},
    )(moved, source, far)
    far, _ = swap(far, None)
    rate, near, az_far, az_near = call(
        functools.partial(first_near_kernel, STEP_SCALES[0]),
        [vmem_state] + face_shapes[1:],
        3,
        aliases={0: 0},
    )(rate, source, near)
    _, near = swap(None, near)
    az_far, az_near = turn(az_far, az_near)
    _, moved, total, source = call(
        functools.partial(volume_and_source_kernel, STEP_SCALES[1]),
        [vmem_state, vmem_state, vmem_state, pltpu.HBM(source_shape, f32)],
        3,
        [IN_VMEM, IN_VMEM, IN_VMEM, IN_HBM],
        aliases={0: 0},
        scratch=[pltpu.SemaphoreType.DMA((1,))],
    )(rate, state, source)

    for scale in STEP_SCALES[1:3]:
        rate, far = call(
            functools.partial(finish_far_kernel, scale),
            [vmem_state, face_shapes[0]],
            4,
            aliases={0: 0},
            cost=LONG,
        )(moved, far, az_far, az_near)
        far, _ = swap(far, None)
        rate, near, az_far, az_near = call(
            functools.partial(finish_near_kernel, scale),
            [vmem_state] + face_shapes[1:],
            2,
            aliases={0: 0},
        )(rate, near)
        _, near = swap(None, near)
        az_far, az_near = turn(az_far, az_near)
        if scale == STEP_SCALES[1]:
            moved, total = call(
                functools.partial(volume_kernel, STEP_SCALES[2]), [vmem_state, vmem_state], 2
            )(rate, total)

    total = call(
        functools.partial(volume_last_kernel, STEP_SCALES[3]),
        vmem_state,
        2,
        scratch=[pltpu.VMEM(STATE, f32)],
    )(rate, total)
    planes = (FIELDS, 5, 25, ROWS, LANES)
    vmem_planes, hbm_planes = pltpu.VMEM(planes, f32), pltpu.HBM(planes, f32)
    total, partial = call(
        functools.partial(last_far_kernel, STEP_SCALES[3]),
        [vmem_planes, hbm_planes],
        4,
        [IN_VMEM, IN_HBM],
        aliases={0: 0},
        cost=LONG,
        scratch=[pltpu.SemaphoreType.DMA((10,))],
    )(total.reshape(planes), far, az_far, az_near)
    _, new_state = call(
        functools.partial(last_near_kernel, STEP_SCALES[3]),
        [vmem_planes, hbm_planes],
        [IN_VMEM, IN_HBM, IN_VMEM],
        [IN_VMEM, IN_HBM],
        aliases={0: 0, 1: 1},
        scratch=[pltpu.SemaphoreType.DMA((1,))],
    )(total, partial, near)
    shape = acoustic_state.shape
    return new_state.reshape(shape), source.reshape((3,) + shape[1:])


def solution(mesh):
    in_specs = (
        P(("ax", "az"), None, None),
        P(("ax", "az"), None),
        P(("ax", "az")),
        P(("ax", "az")),
        P(),
        P(None, None, "ax", "az", None),
    )
    out_specs = (P(None, None, "ax", "az", None), P(None, None, "ax", "az", None))
    return jax.shard_map(body, mesh=mesh, in_specs=in_specs, out_specs=out_specs, check_vma=False)
```
